32 devices in a mesh: fsdp: 32 (over z, y, x, core).
Axes of the slice: x: 2, y: 2, z: 4, core: 2. Of those that a mesh axis runs over, the one named last changes fastest.
Arguments:
- tokens: bfloat16 [16384, 1024], P('fsdp'), may hold values from -6 to 6
- positions: int32 [16384], P('fsdp'), may hold values from 0 to 1021, as said below
- routes: int32 [16384, 8], P('fsdp'), may hold values from 0 to 15, all different within a row; in each aligned block of 512 rows (0 to 511, 512 to 1023, ...) at most 384 rows name the same one
- attn_gain: bfloat16 [1024], P('fsdp'), may hold values from 0.5 to 1.5
- w_query: bfloat16 [1024, 1024], P('fsdp'), may hold values from -0.1875 to 0.1875
- w_key: bfloat16 [1024, 512], P('fsdp'), may hold values from -0.1875 to 0.1875
- w_value: bfloat16 [1024, 512], P('fsdp'), may hold values from -0.1875 to 0.1875
- w_out: bfloat16 [1024, 1024], P('fsdp'), may hold values from -3 to 3
- mlp_gain: bfloat16 [1024], P('fsdp'), may hold values from 0.5 to 1.5
- w_router: bfloat16 [1024, 16], P('fsdp'), may hold values from -0.09375 to 0.09375
- w_gate: bfloat16 [16, 1024, 512], P(None, 'fsdp'), may hold values from -0.1875 to 0.1875
- w_up: bfloat16 [16, 1024, 512], P(None, 'fsdp'), may hold values from -0.1875 to 0.1875
- w_down: bfloat16 [16, 1024, 512], P(None, 'fsdp'), may hold values from -0.75 to 0.75
- cotangent: bfloat16 [16384, 1024], P('fsdp'), may hold values from -6 to 6
Outputs:
- activations: bfloat16 [16384, 1024], P('fsdp')
- token_grad: float32 [16384, 1024], P('fsdp')
- grad_attn_gain: float32 [1024], P('fsdp')
- grad_query: float32 [1024, 1024], P('fsdp')
- grad_key: float32 [1024, 512], P('fsdp')
- grad_value: float32 [1024, 512], P('fsdp')
- grad_out: float32 [1024, 1024], P('fsdp')
- grad_mlp_gain: float32 [1024], P('fsdp')
- grad_router: float32 [1024, 16], P('fsdp')
- grad_gate: float32 [16, 1024, 512], P(None, 'fsdp')
- grad_up: float32 [16, 1024, 512], P(None, 'fsdp')
- grad_down: float32 [16, 1024, 512], P(None, 'fsdp')
The draws below stay inside these ranges and needn't reach their ends.
Inputs may be any that keep to these rules, and one draw needn't show every extreme that they name: `positions`: positions count up by one from 0 inside a document; documents lie end to end, and each device's 512 tokens hold at least one document start at a local index of 1 or more (besides token 0), so a document covers at most two neighbouring devices' tokens. `routes`: 8 different experts a token; among the 512 rows of one device no expert is named more than 384 times.
All inputs are finite; a program needn't handle non-finite values.
Results may differ from the reference program's by a relative error of at most 0.013.
The reference program's roundings to bfloat16 on the way count: a program that leaves them out, or rounds other values in their place, can miss the bound.
Values may be sent and summed in bfloat16 or wider, within the bound.
No kernel may reach another device: no remote copies, remote signals or barrier semaphores. Data moves between devices by JAX's collectives and lax.ppermute only.
A program may use at most 296 MiB of HBM per device.

```python
import math
from functools import partial
import jax
import jax.numpy as jnp
import numpy as np
from jax import lax

D = 1024
HEADS = 16
KV_HEADS = 8
HEAD_DIM = 64
FF = 512
TOP = 8
EXPERTS = 16
TOK_DEV = 512
TOKENS = 16384
CAP = 384


def draw_positions(key, part):
    key = jax.random.fold_in(key, 11)
    blocks = TOKENS // TOK_DEV
    first_key, second_key, use_key, pick_key = jax.random.split(key, 4)
    first_cut = jax.random.randint(first_key, (blocks, 1), 1, TOK_DEV)
    second_cut = jax.random.randint(second_key, (blocks, 1), 1, TOK_DEV)
    use_second = jax.random.randint(use_key, (blocks, 1), 0, 2)
    chosen_block = jax.random.randint(pick_key, (), 0, blocks - 1)
    block_index = jnp.arange(blocks, dtype=jnp.int32)[:, None]
    first_cut = jnp.where(block_index == chosen_block, 1, first_cut)
    first_cut = jnp.where(block_index == chosen_block + 1, TOK_DEV - 1, first_cut)
    use_second = jnp.where((block_index == chosen_block) | (block_index == chosen_block + 1), 0, use_second)
    local_index = jnp.arange(TOK_DEV, dtype=jnp.int32)[None, :]
    cut_here = (local_index == first_cut) | (use_second == 1) & (local_index == second_cut)
    token_index = jnp.arange(TOKENS, dtype=jnp.int32)
    doc_starts = cut_here.reshape(-1) | (token_index == 0)
    start_index = lax.cummax(jnp.where(doc_starts, token_index, 0), axis=0)
    return (token_index - start_index).astype(jnp.int32)


def level_of(own_key, extent, shards, least, high):
    def one(position, parts):
        steps = jax.random.uniform(jax.random.fold_in(jax.random.fold_in(own_key, 6), position), (parts,), jnp.float32, least / len(shards), high / len(shards))
        return jnp.repeat(jnp.exp(steps), extent[position] // parts).reshape((-1,) + (1,) * (len(extent) - position - 1))

    factor_of = one(*shards[0])
    for cut in shards[1:]:
        factor_of = factor_of * one(*cut)
    return factor_of


def assign_block(rng, own, number, rows, amount, top, reach, slope):
    sequence = jax.random.permutation(rng, amount)
    heavy_load, common = shares(amount, rows * top, reach, slope, True), shares(amount, rows * top, reach, slope, False)
    places = jnp.arange(amount)

    def named(lengths, turn):
        used = int((lengths > 0).sum())
        fixed = max(1, used // 4)
        passed = fixed + (places - fixed + turn * (used - fixed)) % max(1, amount - fixed)
        return jnp.zeros((amount,), jnp.int32).at[sequence[jnp.where(places < fixed, places, passed)]].set(jnp.asarray(lengths, jnp.int32))

    lengths = jnp.where(number % 4 == 0, named(heavy_load, number // 4), named(common, number - number // 4 - 1))
    mixed = jax.random.permutation(jax.random.fold_in(own, 3), amount)
    donor, receiver = mixed[0:amount // 2 * 2:2], mixed[1:amount // 2 * 2:2]
    room = jnp.minimum(lengths[donor] - 1, reach - lengths[receiver]) // 2
    room = jnp.where((donor == sequence[0]) | (receiver == sequence[0]) | (lengths[receiver] == 0), 0, jnp.maximum(room, 0))
    passed = jax.random.randint(jax.random.fold_in(own, 4), (amount // 2,), 0, 1 << 20) % (room + 1)
    lengths = lengths.at[donor].add(-passed).at[receiver].add(passed)
    labels = jnp.searchsorted(jnp.cumsum(lengths), jnp.arange(rows * top), side="right").astype(jnp.int32)
    listing = labels.reshape(top, rows).T
    listing = listing[jax.random.permutation(jax.random.fold_in(own, 1), rows)]
    turn = jax.random.randint(jax.random.fold_in(own, 2), (rows, 1), 0, top)
    return jnp.take_along_axis(listing, (jnp.arange(top)[None, :] + turn) % top, axis=1)


def shares(count, total, limit, slope, full):
    weights = [(1 << 20) // math.isqrt(grade ** slope) + 1 for grade in range(1, count + 1)]
    largest = limit if full else min(limit, max(-(-total // count), total * weights[0] // sum(weights)))
    least = 1 if total - largest >= count - 1 else 0
    given, surplus = [largest] + [least] * (count - 1), total - largest - least * (count - 1)
    while surplus > 0:
        movable = [i for i in range(1, count) if given[i] < largest] or [i for i in range(1, count) if given[i] < limit]
        mass, remaining = sum([weights[i] for i in movable]), surplus
        for i in movable:
            addition = min(limit - given[i], max(1, remaining * weights[i] // mass), surplus)
            given[i] = given[i] + addition
            surplus = surplus - addition
    return np.array(given)


def gaussian(key, dims, width, reach, cuts=(), kind=jnp.bfloat16):
    level = level_of(key, dims, cuts, -0.22, 0.18) if cuts else 1.0
    result = jax.random.normal(key, dims, jnp.float32) * width * level
    return jnp.minimum(jnp.maximum(result, -reach), reach).astype(kind)


def setup_inputs(seed: int = 0) -> dict:
    streams_of = jax.random.split(jax.random.key(seed), 15)
    tokens = gaussian(streams_of[0], (TOKENS, D), 1.0, 6.0, ((0, 32),))
    positions = draw_positions(jax.random.fold_in(streams_of[14], 71), 0)
    routes_keys = jax.random.split(jax.random.fold_in(streams_of[2], 1), TOKENS // TOK_DEV)
    routes_turns = jax.random.permutation(jax.random.fold_in(streams_of[2], 3), TOKENS // TOK_DEV)
    routes = jax.vmap(lambda own, number: assign_block(jax.random.fold_in(streams_of[2], 2), own, number, TOK_DEV, EXPERTS, TOP, CAP, 1))(routes_keys, routes_turns).reshape((TOKENS, TOP))
    attn_gain = jnp.clip(1.0 + 0.1 * jax.random.normal(streams_of[3], (D,), jnp.float32), 0.5, 1.5).astype(jnp.bfloat16)
    w_query = gaussian(streams_of[4], (D, D), D ** -0.5, 0.1875, ((0, 32),))
    w_key = gaussian(streams_of[5], (D, KV_HEADS * HEAD_DIM), D ** -0.5, 0.1875, ((0, 32),))
    w_value = gaussian(streams_of[6], (D, KV_HEADS * HEAD_DIM), D ** -0.5, 0.1875, ((0, 32),))
    w_out = gaussian(streams_of[7], (D, D), (max(1, 2 * D // TOK_DEV)) ** -0.5, 3.0, ((0, 32),))
    mlp_gain = jnp.clip(1.0 + 0.1 * jax.random.normal(streams_of[8], (D,), jnp.float32), 0.5, 1.5).astype(jnp.bfloat16)
    w_router = gaussian(streams_of[9], (D, EXPERTS), (4 * D) ** -0.5, 0.09375, ((0, 32),))
    w_gate = gaussian(streams_of[10], (EXPERTS, D, FF), D ** -0.5, 0.1875, ((1, 32),))
    w_up = gaussian(streams_of[11], (EXPERTS, D, FF), D ** -0.5, 0.1875, ((1, 32),))
    w_down = gaussian(streams_of[12], (EXPERTS, D, FF), (FF // TOP) ** -0.5, 0.75, ((1, 32),))
    cotangent = gaussian(streams_of[13], (TOKENS, D), 1.0, 6.0, ((0, 32),))
    return dict(tokens=tokens, positions=positions, routes=routes, attn_gain=attn_gain, w_query=w_query, w_key=w_key, w_value=w_value, w_out=w_out, mlp_gain=mlp_gain, w_router=w_router, w_gate=w_gate, w_up=w_up, w_down=w_down, cotangent=cotangent)


@jax.custom_vjp
def low(v):
    return lax.optimization_barrier(v.astype(jnp.bfloat16)).astype(jnp.float32)

@jax.custom_vjp
def low_back(v):
    return v

def low_keep(v):
    return (low(v), None)

def low_pass(kept, grad):
    return (grad,)

def back_keep(v):
    return (v, None)

def back_low(kept, grad):
    return (low(grad),)
low.defvjp(low_keep, low_pass)
low_back.defvjp(back_keep, back_low)
NORM_EPS = 1e-06
ROPE_THETA = 10000.0
HIGH_PRECISION = lax.Precision.HIGHEST

def rms_norm(source, gain):
    inverse = lax.rsqrt(lax.optimization_barrier(jnp.mean(source * source, axis=-1, keepdims=True)) + NORM_EPS)
    return source * inverse * gain

def rope_tables(positions, head_size):
    half_width = head_size // 2
    frequency = ROPE_THETA ** (-(jnp.arange(half_width, dtype=jnp.float32) * 2.0) / head_size)
    angle_rows = positions.astype(jnp.float32)[:, None] * frequency[None, :]
    angle_rows = jnp.concatenate([angle_rows, angle_rows], axis=1)
    return (jnp.cos(angle_rows), jnp.sin(angle_rows))

def rotate(source, cosine_table, sine_table):
    half_width = source.shape[-1] // 2
    turned = jnp.concatenate([-source[..., half_width:], source[..., :half_width]], axis=-1)
    return source * cosine_table[:, None, :] + turned * sine_table[:, None, :]

def dispatch_tables(route_rows):
    flat_routes = route_rows.reshape(-1)
    assign_count = flat_routes.shape[0]
    one_hot = (flat_routes[:, None] == jnp.arange(EXPERTS, dtype=jnp.int32)[None, :]).astype(jnp.int32)
    slot_rank = lax.optimization_barrier(jnp.sum((jnp.cumsum(one_hot, axis=0) - 1) * one_hot, axis=1))
    slot_place = (flat_routes * CAP + slot_rank).astype(jnp.int32)
    slot_table = jnp.full((EXPERTS * CAP,), assign_count, jnp.int32)
    slot_table = slot_table.at[slot_place].set(jnp.arange(assign_count, dtype=jnp.int32))
    return (slot_place, slot_table.reshape(EXPERTS, CAP))

def layer_forward(inputs_f, gain_one, query_w, key_w, value_w, out_w, gain_two, router_w, gate_w, up_w, down_w, positions=None, routes=None):
    group_size = HEADS // KV_HEADS
    score_scale = HEAD_DIM ** (-0.5)
    blocks = TOKENS // TOK_DEV
    normed_one = low(rms_norm(inputs_f, gain_one))
    query_lin = low_back(jnp.dot(normed_one, query_w, precision=HIGH_PRECISION))
    key_lin = low_back(jnp.dot(normed_one, key_w, precision=HIGH_PRECISION))
    values = low(low_back(jnp.dot(normed_one, value_w, precision=HIGH_PRECISION))).reshape(TOKENS, KV_HEADS, HEAD_DIM)
    cosine_table, sine_table = rope_tables(positions, HEAD_DIM)
    queries = low(rotate(query_lin.reshape(TOKENS, HEADS, HEAD_DIM), cosine_table, sine_table))
    queries = queries.reshape(TOKENS, KV_HEADS, group_size, HEAD_DIM)
    keys = low(rotate(key_lin.reshape(TOKENS, KV_HEADS, HEAD_DIM), cosine_table, sine_table))
    zero_rows = jnp.zeros((TOK_DEV, KV_HEADS, HEAD_DIM), jnp.float32)
    keys_pad = jnp.concatenate([zero_rows, keys], axis=0)
    values_pad = jnp.concatenate([zero_rows, values], axis=0)
    start_index = jnp.arange(TOKENS, dtype=jnp.int32) - positions

    def attend(block_index):
        first_row = block_index * TOK_DEV
        query_block = lax.dynamic_slice_in_dim(queries, first_row, TOK_DEV, 0)
        key_block = lax.dynamic_slice_in_dim(keys_pad, first_row, 2 * TOK_DEV, 0)
        value_block = lax.dynamic_slice_in_dim(values_pad, first_row, 2 * TOK_DEV, 0)
        row_index = first_row + jnp.arange(TOK_DEV, dtype=jnp.int32)
        col_index = first_row - TOK_DEV + jnp.arange(2 * TOK_DEV, dtype=jnp.int32)
        begin_rows = lax.dynamic_slice_in_dim(start_index, first_row, TOK_DEV, 0)
        key_mask = (col_index[None, :] >= begin_rows[:, None]) & (col_index[None, :] <= row_index[:, None])
        scores = low_back(jnp.einsum('qkgd,ckd->kgqc', query_block, key_block, precision=HIGH_PRECISION) * score_scale)
        scores = jnp.where(key_mask[None, None], scores, -1e+30)
        row_max = lax.optimization_barrier(jnp.max(scores, axis=-1, keepdims=True))
        weights = jnp.exp(scores - row_max)
        probabilities = weights / lax.optimization_barrier(jnp.sum(weights, axis=-1, keepdims=True))
        context = jnp.einsum('kgqc,ckd->qkgd', low(probabilities), value_block, precision=HIGH_PRECISION)
        return context.reshape(TOK_DEV, D)
    context = lax.map(jax.checkpoint(attend), jnp.arange(blocks, dtype=jnp.int32)).reshape(TOKENS, D)
    context = low(low_back(context))
    middle = inputs_f + low_back(jnp.dot(context, out_w, precision=HIGH_PRECISION))
    normed_two = low(rms_norm(middle, gain_two))
    logits = low_back(jnp.dot(normed_two, router_w, precision=HIGH_PRECISION))
    chosen = jnp.take_along_axis(logits, routes, axis=1)
    chosen_exp = jnp.exp(chosen - lax.optimization_barrier(jnp.max(chosen, axis=-1, keepdims=True)))
    gate_weights = chosen_exp / lax.optimization_barrier(jnp.sum(chosen_exp, axis=-1, keepdims=True))

    def mix_block(block_index):
        first_row = block_index * TOK_DEV
        rows_in = lax.dynamic_slice_in_dim(normed_two, first_row, TOK_DEV, 0)
        route_rows = lax.dynamic_slice_in_dim(routes, first_row, TOK_DEV, 0)
        gate_rows = lax.dynamic_slice_in_dim(gate_weights, first_row, TOK_DEV, 0)
        slot_place, slot_table = dispatch_tables(route_rows)
        padded_rows = jnp.concatenate([rows_in, jnp.zeros((1, D), jnp.float32)], axis=0)
        dispatched = padded_rows[slot_table // TOP]
        gate_val = low_back(jnp.einsum('ecd,edf->ecf', dispatched, gate_w, precision=HIGH_PRECISION))
        up_val = low_back(jnp.einsum('ecd,edf->ecf', dispatched, up_w, precision=HIGH_PRECISION))
        hidden = low(jax.nn.silu(gate_val) * up_val)
        expert_out = low_back(jnp.einsum('ecf,edf->ecd', hidden, down_w, precision=HIGH_PRECISION))
        per_assign = expert_out.reshape(EXPERTS * CAP, D)[slot_place].reshape(TOK_DEV, TOP, D)
        return jnp.einsum('tj,tjd->td', gate_rows, per_assign, precision=HIGH_PRECISION)
    mixed_out = lax.map(jax.checkpoint(mix_block), jnp.arange(blocks, dtype=jnp.int32)).reshape(TOKENS, D)
    return middle + mixed_out

def reference(tokens, positions, routes, attn_gain, w_query, w_key, w_value, w_out, mlp_gain, w_router, w_gate, w_up, w_down, cotangent):
    floats = tuple((source_array.astype(jnp.float32) for source_array in (tokens, attn_gain, w_query, w_key, w_value, w_out, mlp_gain, w_router, w_gate, w_up, w_down)))
    forward = partial(layer_forward, positions=positions, routes=routes)
    final_sum, pull_back = jax.vjp(forward, *floats)
    grad_rows = pull_back(cotangent.astype(jnp.float32))
    return (final_sum.astype(jnp.bfloat16), grad_rows[0], grad_rows[1], grad_rows[2], grad_rows[3], grad_rows[4], grad_rows[5], grad_rows[6], grad_rows[7], grad_rows[8], grad_rows[9], grad_rows[10])
```

```python
import jax
import jax.numpy as jnp
from jax import lax
from jax.experimental import pallas as pl
from jax.experimental.pallas import tpu as pltpu
from jax.sharding import PartitionSpec as P

HEADS = 16
KV_HEADS = 8
HEAD_DIM = 64
TOP = 8
EXPERTS = 16
GROUP = 4
LANES = 128
NORM_EPS = 1e-06
ROPE_THETA = 10000.0
MASKED = -1e30
MIB = 1024 * 1024

bf = jnp.bfloat16
fl = jnp.float32
SLOT = (0, 2, 1, 3)

NN = (((1,), (0,)), ((), ()))
NT = (((1,), (1,)), ((), ()))
TN = (((0,), (0,)), ((), ()))


def mm(a, b, dims=NN):
    return lax.dot_general(a, b, dims, preferred_element_type=fl)


def params(mib):
    return pltpu.CompilerParams(vmem_limit_bytes=mib * MIB)


def shifted(block, axis, distance):
    devices = range(lax.axis_size(axis))
    route = [(i - distance, i) for i in devices if i - distance in devices]
    return lax.ppermute(block, axis, route)


def swapped(block, bits):
    return lax.ppermute(block, "fsdp", [(i, i ^ bits) for i in range(lax.axis_size("fsdp"))])


def lane_index(shape):
    return lax.broadcasted_iota(jnp.int32, shape, len(shape) - 1)


def swap_halves(v):
    first = (lane_index(v.shape) & 32) == 0
    return jnp.where(first, pltpu.roll(v, LANES - 32, 1), pltpu.roll(v, 32, 1))


def rope_tables(positions):
    half_width = HEAD_DIM // 2
    frequency = ROPE_THETA ** (-(jnp.arange(half_width, dtype=fl) * 2.0) / HEAD_DIM)
    angle_rows = positions.astype(fl)[:, None] * frequency[None, :]
    cosine, sine = jnp.cos(angle_rows), jnp.sin(angle_rows)
    return (
        jnp.concatenate([cosine] * 4, axis=1),
        jnp.concatenate([-sine, sine, -sine, sine], axis=1),
    )


def query_kernel(x_ref, w_ref, cos_ref, sin_ref, out_ref):
    lin = mm(x_ref[...], w_ref[...])
    for part in range(2):
        piece = lin[:, part * LANES : (part + 1) * LANES]
        turned = piece * cos_ref[...] + swap_halves(piece) * sin_ref[...]
        out_ref[:, part * LANES : (part + 1) * LANES] = (turned.astype(bf) * HEAD_DIM**-0.5).astype(bf)


def key_value_kernel(x_ref, w_ref, cos_ref, sin_ref, out_ref):
    lin = mm(x_ref[...], w_ref[...])
    piece = lin[:, :LANES]
    out_ref[:, :LANES] = (piece * cos_ref[...] + swap_halves(piece) * sin_ref[...]).astype(bf)
    out_ref[:, LANES:] = lin[:, LANES:].astype(bf)


def project(kernel, normed, weights, first_block, cosine, sine):
    rows, width = normed.shape
    return pl.pallas_call(
        kernel,
        grid=(4,),
        in_specs=[
            pl.BlockSpec((rows, width), lambda j: (0, 0)),
            pl.BlockSpec((width, 256), lambda j: (0, first_block + j)),
            pl.BlockSpec((rows, LANES), lambda j: (0, 0)),
            pl.BlockSpec((rows, LANES), lambda j: (0, 0)),
        ],
        out_specs=pl.BlockSpec((rows, 256), lambda j: (0, j)),
        out_shape=jax.ShapeDtypeStruct((rows, 1024), bf),
        compiler_params=params(32),
    )(normed, weights, cosine, sine)


def fill_bias(start_ref, bias_ref):
    rows = bias_ref.shape[0]
    column = lax.broadcasted_iota(jnp.int32, bias_ref.shape, 1) - rows
    row = lax.broadcasted_iota(jnp.int32, bias_ref.shape, 0)
    seen = (column >= start_ref[...]) & (column <= row)
    bias_ref[...] = jnp.where(seen, 0.0, MASKED)


def attend_kernel(start_ref, q_ref, prev_ref, own_ref, ctx_ref, low_ref, lse_ref, bias_ref, kv_ref):
    rows = q_ref.shape[0]
    half = rows // 2

    @pl.when(pl.program_id(0) == 0)
    def _():
        fill_bias(start_ref, bias_ref)

    kv_ref[:rows, :] = prev_ref[...]
    kv_ref[rows:, :] = own_ref[...]
    for tile in range(2):
        queries = pl.ds(tile * half, half)
        keys = rows + (tile + 1) * half
        bias = bias_ref[queries, :keys]
        for head in range(4):
            lane = 64 * (head // 2)
            scores = mm(
                q_ref[queries, head * 64 : head * 64 + 64], kv_ref[:keys, lane : lane + 64], NT
            )
            scores = scores + bias
            row_max = jnp.max(scores, axis=1, keepdims=True)
            weights = jnp.exp(scores - row_max)
            total = jnp.sum(weights, axis=1, keepdims=True)
            probs = (weights * (1.0 / total)).astype(bf)
            context = mm(probs, kv_ref[:keys, LANES + lane : LANES + lane + 64])
            ctx_ref[queries, head * 64 : head * 64 + 64] = context
            low_ref[queries, head * 64 : head * 64 + 64] = context.astype(bf)
            lse_ref[0, queries, head : head + 1] = row_max + jnp.log(total)


def attend(start, queries, before, own):
    rows = queries.shape[0]
    wide = pl.BlockSpec((rows, 256), lambda j: (0, j))
    return pl.pallas_call(
        attend_kernel,
        grid=(4,),
        in_specs=[pl.BlockSpec((rows, 1), lambda j: (0, 0)), wide, wide, wide],
        out_specs=[wide, wide, pl.BlockSpec((1, rows, LANES), lambda j: (j, 0, 0))],
        out_shape=[
            jax.ShapeDtypeStruct((rows, 1024), fl),
            jax.ShapeDtypeStruct((rows, 1024), bf),
            jax.ShapeDtypeStruct((4, rows, LANES), fl),
        ],
        scratch_shapes=[pltpu.VMEM((rows, 2 * rows), fl), pltpu.VMEM((2 * rows, 256), bf)],
        compiler_params=params(40),
    )(start, queries, before, own)


def attend_back_kernel(
    start_ref, q_ref, prev_ref, own_ref, gctx_ref, ctx_ref, lse_ref, cos_ref, sin_ref,
    gq_ref, sent_ref, kept_ref, bias_ref, kv_ref, gkv_ref, gq_acc_ref,
):
    rows = q_ref.shape[0]
    half = rows // 2

    @pl.when(pl.program_id(0) == 0)
    def _():
        fill_bias(start_ref, bias_ref)

    kv_ref[:rows, :] = prev_ref[...]
    kv_ref[rows:, :] = own_ref[...]
    gkv_ref[...] = jnp.zeros_like(gkv_ref)
    for tile in range(2):
        queries = pl.ds(tile * half, half)
        keys = rows + (tile + 1) * half
        bias = bias_ref[queries, :keys]
        for head in range(4):
            lane = 64 * (head // 2)
            here = slice(head * 64, head * 64 + 64)
            query = q_ref[queries, here]
            grad = gctx_ref[queries, here]
            key = kv_ref[:keys, lane : lane + 64]
            value = kv_ref[:keys, LANES + lane : LANES + lane + 64]
            inner = jnp.sum(grad.astype(fl) * ctx_ref[queries, here], axis=1, keepdims=True)
            scores = mm(query, key, NT) + bias
            probs = jnp.exp(scores - lse_ref[0, queries, head : head + 1])
            grad_probs = mm(grad, value, NT)
            grad_scores = (probs * (grad_probs - inner)).astype(bf)
            gq_acc_ref[queries, here] = mm(grad_scores, key) * HEAD_DIM**-0.5
            gkv_ref[:keys, lane : lane + 64] += mm(grad_scores, query, TN)
            gkv_ref[:keys, LANES + lane : LANES + lane + 64] += mm(probs.astype(bf), grad, TN)
    for part in range(2):
        here = slice(part * LANES, part * LANES + LANES)
        piece = gq_acc_ref[:, here]
        gq_ref[:, here] = (piece * cos_ref[...] - swap_halves(piece) * sin_ref[...]).astype(bf)
    sent_ref[...] = gkv_ref[:rows, :].astype(bf)
    kept_ref[...] = gkv_ref[rows:, :]


def attend_back(start, queries, before, own, grad_context, context, log_total, cosine, sine):
    rows = queries.shape[0]
    wide = pl.BlockSpec((rows, 256), lambda j: (0, j))
    table = pl.BlockSpec((rows, LANES), lambda j: (0, 0))
    return pl.pallas_call(
        attend_back_kernel,
        grid=(4,),
        in_specs=[
            pl.BlockSpec((rows, 1), lambda j: (0, 0)), wide, wide, wide, wide, wide,
            pl.BlockSpec((1, rows, LANES), lambda j: (j, 0, 0)), table, table,
        ],
        out_specs=[wide, wide, wide],
        out_shape=[
            jax.ShapeDtypeStruct((rows, 1024), bf),
            jax.ShapeDtypeStruct((rows, 1024), bf),
            jax.ShapeDtypeStruct((rows, 1024), fl),
        ],
        scratch_shapes=[
            pltpu.VMEM((rows, 2 * rows), fl),
            pltpu.VMEM((2 * rows, 256), bf),
            pltpu.VMEM((2 * rows, 256), fl),
            pltpu.VMEM((rows, 256), fl),
        ],
        compiler_params=params(48),
    )(start, queries, before, own, grad_context, context, log_total, cosine, sine)


def middle_kernel(ctx_ref, out_w_ref, router_ref, x_ref, gain_ref, chosen_ref, middle_ref, block_ref, gates_ref):
    width = x_ref.shape[1]
    middle = x_ref[...].astype(fl) + mm(ctx_ref[...], out_w_ref[...])
    inverse = lax.rsqrt(jnp.mean(middle * middle, axis=1, keepdims=True) + NORM_EPS)
    normed = (middle * inverse * gain_ref[...]).astype(bf)
    logits = mm(normed, router_ref[...])
    chosen = chosen_ref[...] > 0.0
    logits = jnp.where(chosen, logits, MASKED)
    weights = jnp.exp(logits - jnp.max(logits, axis=1, keepdims=True))
    weights = jnp.where(chosen, weights, 0.0)
    gates = weights / jnp.sum(weights, axis=1, keepdims=True)
    high = gates.astype(bf).astype(fl)
    middle_ref[...] = middle
    gates_ref[...] = gates
    block_ref[:, :width] = normed
    block_ref[:, width:] = (high + pltpu.roll(gates - high, EXPERTS, 1)).astype(bf)


def middle_part(ctx, full, tokens, gain, chosen):
    rows, width = tokens.shape
    return pl.pallas_call(
        middle_kernel,
        grid=(1,),
        in_specs=[
            pl.BlockSpec((rows, width), lambda j: (0, 0)),
            pl.BlockSpec((width, width), lambda j: (0, 2)),
            pl.BlockSpec((width, LANES), lambda j: (0, 24)),
            pl.BlockSpec((rows, width), lambda j: (0, 0)),
            pl.BlockSpec((1, width), lambda j: (0, 0)),
            pl.BlockSpec((rows, LANES), lambda j: (0, 0)),
        ],
        out_specs=[
            pl.BlockSpec((rows, width), lambda j: (0, 0)),
            pl.BlockSpec((rows, width + LANES), lambda j: (0, 0)),
            pl.BlockSpec((rows, LANES), lambda j: (0, 0)),
        ],
        out_shape=[
            jax.ShapeDtypeStruct((rows, width), fl),
            jax.ShapeDtypeStruct((rows, width + LANES), bf),
            jax.ShapeDtypeStruct((rows, LANES), fl),
        ],
        compiler_params=params(48),
    )(ctx, full, full, tokens, gain, chosen)


def experts_kernel(
    first_ref, x0, x1, x2, x3, c0, c1, c2, c3, w_ref, out_hbm, gn_hbm, grad_ref,
    xs, cs, xt, ct, out_acc, gn_acc, hid_s, gate_s, up_s, sems,
):
    step = pl.program_id(0)
    rows = c0.shape[0]
    width = c0.shape[1]
    hidden_width = w_ref.shape[1] // 3
    expert = first_ref[0] + step

    @pl.when(step == 0)
    def _():
        copies = []
        for slot, (x, c) in enumerate(((x0, c0), (x1, c1), (x2, c2), (x3, c3))):
            here = pl.ds(slot * rows, rows)
            copies.append(pltpu.make_async_copy(x, xs.at[here], sems.at[2 * slot]))
            copies.append(pltpu.make_async_copy(c, cs.at[here], sems.at[2 * slot + 1]))
        for copy in copies:
            copy.start()
        for copy in copies:
            copy.wait()
        out_acc[...] = jnp.zeros_like(out_acc)
        gn_acc[...] = jnp.zeros_like(gn_acc)
        for slot in range(GROUP):
            here = slice(slot * rows, (slot + 1) * rows)
            xt[:, here] = xs[here, :width].T
            ct[:, here] = cs[here, :].T

    def tile_step(tile, carry):
        here = pl.ds(pl.multiple_of(tile * rows, rows), rows)
        x_tile = xs[here, :width]
        gate_w = w_ref[:, :hidden_width]
        up_w = w_ref[:, hidden_width : 2 * hidden_width]
        down_w = w_ref[:, 2 * hidden_width :]
        gate = mm(x_tile, gate_w)
        up = mm(x_tile, up_w)
        raw = mm(cs[here, :], down_w)
        packed = xs[here, width:].astype(fl)
        lane = lane_index(packed.shape)
        mine = (lane == expert) | (lane == expert + EXPERTS)
        gates = jnp.sum(jnp.where(mine, packed, 0.0), axis=1, keepdims=True)
        sigmoid = 1.0 / (1.0 + jnp.exp(-gate))
        silu = gate * sigmoid
        hidden = (silu * up).astype(bf).astype(fl)
        grad_gates = jnp.sum(hidden * raw, axis=1, keepdims=True)
        grad_hidden = raw * gates
        hid = (hidden * gates).astype(bf)
        grad_gate = (grad_hidden * up * sigmoid * (1.0 + gate * (1.0 - sigmoid))).astype(bf)
        grad_up = (grad_hidden * silu).astype(bf)
        hid_s[here, :] = hid
        gate_s[here, :] = grad_gate
        up_s[here, :] = grad_up
        out_acc[here, :] += mm(hid, down_w, NT)
        gn_acc[here, :width] += mm(grad_gate, gate_w, NT) + mm(grad_up, up_w, NT)
        gn_acc[here, width:] += jnp.where(lane == expert, grad_gates, 0.0)
        return carry

    lax.fori_loop(0, GROUP, tile_step, 0)
    grad_ref[:, :hidden_width] = mm(xt[...], gate_s[...]).astype(bf)
    grad_ref[:, hidden_width : 2 * hidden_width] = mm(xt[...], up_s[...]).astype(bf)
    grad_ref[:, 2 * hidden_width :] = mm(ct[...], hid_s[...]).astype(bf)

    @pl.when(step == pl.num_programs(0) - 1)
    def _():
        gates_part = gn_acc[:, width:]
        high = gates_part.astype(bf).astype(fl)
        low = (gates_part - high).astype(bf).astype(fl)
        gn_acc[:, width:] = high + pltpu.roll(low, EXPERTS, 1)
        one = pltpu.make_async_copy(out_acc, out_hbm, sems.at[0])
        two = pltpu.make_async_copy(gn_acc, gn_hbm, sems.at[1])
        one.start()
        two.start()
        one.wait()
        two.wait()


def experts_part(first, blocks, cots, weights):
    rows, width = cots[0].shape
    local = EXPERTS // GROUP
    cols = weights.shape[1] // local
    hidden_width = cols // 3
    total = GROUP * rows
    anywhere = pl.BlockSpec(memory_space=pl.ANY)
    return pl.pallas_call(
        experts_kernel,
        grid_spec=pltpu.PrefetchScalarGridSpec(
            num_scalar_prefetch=1,
            grid=(local,),
            in_specs=[anywhere] * 8 + [pl.BlockSpec((width, cols), lambda e, s: (0, e))],
            out_specs=[anywhere, anywhere, pl.BlockSpec((width, cols), lambda e, s: (0, e))],
            scratch_shapes=[
                pltpu.VMEM((total, width + LANES), bf),
                pltpu.VMEM((total, width), bf),
                pltpu.VMEM((width, total), bf),
                pltpu.VMEM((width, total), bf),
                pltpu.VMEM((total, width), fl),
                pltpu.VMEM((total, width + LANES), fl),
                pltpu.VMEM((total, hidden_width), bf),
                pltpu.VMEM((total, hidden_width), bf),
                pltpu.VMEM((total, hidden_width), bf),
                pltpu.SemaphoreType.DMA((8,)),
            ],
        ),
        out_shape=[
            jax.ShapeDtypeStruct((total, width), fl),
            jax.ShapeDtypeStruct((total, width + LANES), fl),
            jax.ShapeDtypeStruct((width, local * cols), bf),
        ],
        compiler_params=params(62),
    )(first, *blocks, *cots, weights)


def middle_back_kernel(
    gn_ref, gates_ref, middle_ref, cot_ref, ctx_ref, out_w_ref, router_ref, gain_ref,
    gm_ref, gctx_ref, gw_ref, gain_grad_ref,
):
    width = cot_ref.shape[1]
    packed = gn_ref[:, width:]
    gates = gates_ref[...]
    grad_gates = packed + pltpu.roll(packed, LANES - EXPERTS, 1)
    inner = jnp.sum(gates * grad_gates, axis=1, keepdims=True)
    grad_logits = (gates * (grad_gates - inner)).astype(bf)
    middle = middle_ref[...]
    inverse = lax.rsqrt(jnp.mean(middle * middle, axis=1, keepdims=True) + NORM_EPS)
    gain = gain_ref[...]
    unit = middle * inverse
    normed = (unit * gain).astype(bf)
    grad_normed = gn_ref[:, :width] + mm(grad_logits, router_ref[...], NT)
    gw_ref[:, width:] = mm(normed, grad_logits, TN).astype(bf)
    gain_grad_ref[...] = jnp.sum(grad_normed * unit, axis=0, keepdims=True)
    scaled = grad_normed * gain
    mean = jnp.mean(scaled * middle, axis=1, keepdims=True)
    grad_middle = cot_ref[...].astype(fl) + inverse * scaled - unit * (inverse * inverse * mean)
    gm_ref[...] = grad_middle
    branch = grad_middle.astype(bf)
    gctx_ref[...] = mm(branch, out_w_ref[...], NT).astype(bf)
    gw_ref[:, :width] = mm(ctx_ref[...], branch, TN).astype(bf)


def middle_back(gn, gates, middle, cot, ctx, full, gain):
    rows, width = cot.shape
    here = lambda *shape: pl.BlockSpec(shape, lambda j: (0, 0))
    return pl.pallas_call(
        middle_back_kernel,
        grid=(1,),
        in_specs=[
            here(rows, width + LANES), here(rows, LANES), here(rows, width), here(rows, width), here(rows, width),
            pl.BlockSpec((width, width), lambda j: (0, 2)),
            pl.BlockSpec((width, LANES), lambda j: (0, 24)),
            here(1, width),
        ],
        out_specs=[here(rows, width), here(rows, width), here(width, width + LANES), here(1, width)],
        out_shape=[
            jax.ShapeDtypeStruct((rows, width), fl),
            jax.ShapeDtypeStruct((rows, width), bf),
            jax.ShapeDtypeStruct((width, width + LANES), bf),
            jax.ShapeDtypeStruct((1, width), fl),
        ],
        compiler_params=params(56),
    )(gn, gates, middle, cot, ctx, full, full, gain)


def finish_kernel(
    gq_ref, kept_ref, back_ref, normed_ref, x_ref, gm_ref, w_ref, gain_ref, cos_ref, sin_ref,
    token_ref, gw_ref, gain_grad_ref, gkv_ref,
):
    width = x_ref.shape[1]
    for part in range(4):
        first = part * 256
        both = kept_ref[:, first : first + 256] + back_ref[:, first : first + 256].astype(fl)
        piece = both[:, :LANES]
        gkv_ref[:, first : first + LANES] = (
            piece * cos_ref[...] - swap_halves(piece) * sin_ref[...]
        ).astype(bf)
        gkv_ref[:, first + LANES : first + 256] = both[:, LANES:].astype(bf)
    normed = normed_ref[...]
    gw_ref[:, :width] = mm(normed, gq_ref[...], TN).astype(bf)
    gw_ref[:, width:] = mm(normed, gkv_ref[...], TN).astype(bf)
    grad_normed = mm(gq_ref[...], w_ref[:, :width], NT) + mm(gkv_ref[...], w_ref[:, width:], NT)
    x = x_ref[...].astype(fl)
    inverse = lax.rsqrt(jnp.mean(x * x, axis=1, keepdims=True) + NORM_EPS)
    unit = x * inverse
    gain_grad_ref[...] = jnp.sum(grad_normed * unit, axis=0, keepdims=True)
    scaled = grad_normed * gain_ref[...]
    mean = jnp.mean(scaled * x, axis=1, keepdims=True)
    token_ref[...] = gm_ref[...] + inverse * scaled - unit * (inverse * inverse * mean)


def finish(grad_query, kept, back, normed, tokens, grad_middle, full, gain, cosine, sine):
    rows, width = tokens.shape
    here = lambda *shape: pl.BlockSpec(shape, lambda j: (0, 0))
    return pl.pallas_call(
        finish_kernel,
        grid=(1,),
        in_specs=[
            here(rows, width), here(rows, width), here(rows, width), here(rows, width), here(rows, width),
            here(rows, width), here(width, 2 * width), here(1, width), here(rows, LANES), here(rows, LANES),
        ],
        out_specs=[here(rows, width), here(width, 2 * width), here(1, width)],
        out_shape=[
            jax.ShapeDtypeStruct((rows, width), fl),
            jax.ShapeDtypeStruct((width, 2 * width), bf),
            jax.ShapeDtypeStruct((1, width), fl),
        ],
        scratch_shapes=[pltpu.VMEM((rows, width), bf)],
        compiler_params=params(60),
    )(grad_query, kept, back, normed, tokens, grad_middle, full, gain, cosine, sine)


def halving_sum(part, index):
    n = lax.axis_size("fsdp")
    cur = part.reshape(n, part.shape[0] // n, part.shape[1])
    bits = 1
    while bits < n:
        mine = (index // bits) % 2
        pairs = cur.reshape(cur.shape[0] // 2, 2, cur.shape[1], cur.shape[2])
        keep = lax.dynamic_index_in_dim(pairs, mine, 1, keepdims=False)
        send = lax.dynamic_index_in_dim(pairs, 1 - mine, 1, keepdims=False)
        cur = keep.astype(fl) + swapped(send.astype(bf), bits).astype(fl)
        bits *= 2
    return cur[0]


def group_order(pieces, member):
    one, two = member % 2 == 1, member // 2 == 1
    a, b, c, d = pieces
    a, b, c, d = jnp.where(one, b, a), jnp.where(one, a, b), jnp.where(one, d, c), jnp.where(one, c, d)
    return jnp.where(two, c, a), jnp.where(two, d, b), jnp.where(two, a, c), jnp.where(two, b, d)


def per_device(
    tokens, positions, routes, attn_gain, w_query, w_key, w_value, w_out, mlp_gain, w_router,
    w_gate, w_up, w_down, cotangent,
):
    n = lax.axis_size("fsdp")
    index = lax.axis_index("fsdp")
    member = index % GROUP
    rows_dev, model_width = tokens.shape
    own_rows = w_query.shape[0]
    hidden_width = w_gate.shape[2]
    local = EXPERTS // GROUP
    across = [[r * GROUP + g for r in range(n // GROUP)] for g in range(GROUP)]

    key_value = jnp.concatenate(
        [w_key.reshape(own_rows, 4, LANES), w_value.reshape(own_rows, 4, LANES)], axis=2
    ).reshape(own_rows, model_width)
    small = jnp.concatenate(
        [w_router, attn_gain[:, None], mlp_gain[:, None], jnp.zeros((own_rows, LANES - EXPERTS - 2), bf)],
        axis=1,
    )
    packed = jnp.concatenate([w_query, key_value, w_out, small], axis=1)
    full = lax.all_gather(packed, "fsdp", axis=0, tiled=True)

    shard = jnp.concatenate([w_gate, w_up, w_down], axis=2).reshape(
        GROUP, local, own_rows, 3 * hidden_width
    )
    pieces = []
    for bits in range(GROUP):
        piece = lax.dynamic_index_in_dim(shard, member ^ bits, 0, keepdims=False)
        pieces.append(swapped(piece, bits) if bits else piece)
    mine = jnp.stack(group_order(pieces, member))
    mine = mine.transpose(0, 2, 1, 3).reshape(GROUP * own_rows, local * 3 * hidden_width)
    mine, full = lax.optimization_barrier((mine, full))
    expert_w = lax.all_gather(mine, "fsdp", axis=0, tiled=True, axis_index_groups=across)

    cot_x = swapped(cotangent, 2)
    cots = (cotangent, cot_x, swapped(cotangent, 1), swapped(cot_x, 1))

    gain_one = full[:, 3088].astype(fl)[None, :]
    gain_two = full[:, 3089].astype(fl)[None, :]
    cosine, sine = rope_tables(positions)
    residual = tokens.astype(fl)
    inverse_one = lax.rsqrt(jnp.mean(residual * residual, axis=-1, keepdims=True) + NORM_EPS)
    normed_one = (residual * inverse_one * gain_one).astype(bf)
    own = project(key_value_kernel, normed_one, full, 4, cosine, sine)
    before = shifted(own, "fsdp", 1)
    queries = project(query_kernel, normed_one, full, 0, cosine, sine)
    start = (jnp.arange(rows_dev, dtype=jnp.int32) - positions)[:, None]
    context, context_low, log_total = attend(start, queries, before, own)

    lanes = jnp.arange(LANES, dtype=jnp.int32)
    chosen = jnp.any(routes[:, :, None] == lanes[None, None, :], axis=1).astype(fl)
    middle, block, gates = middle_part(context_low, full, tokens, gain_two, chosen)

    block_x = swapped(block, 2)
    blocks = (block, block_x, swapped(block, 1), swapped(block_x, 1))
    first = (member * local).astype(jnp.int32).reshape(1)
    out_parts, gn_parts, expert_grads = experts_part(first, blocks, cots, expert_w)

    def returned(parts):
        parts = parts.reshape(GROUP, rows_dev, parts.shape[1])
        other = swapped(parts[2:].astype(bf), 1).astype(fl)
        away = swapped((parts[1] + other[1]).astype(bf), 2).astype(fl)
        return parts[0] + other[0] + away

    gn = returned(gn_parts)
    owned_experts = lax.psum_scatter(
        expert_grads, "fsdp", scatter_dimension=0, tiled=True, axis_index_groups=across
    )
    grad_middle, grad_context, out_grad, gain_two_grad = middle_back(
        gn, gates, middle, cotangent, context_low, full, gain_two
    )
    activations = (middle + returned(out_parts)).astype(bf)
    grad_query, sent, kept = attend_back(
        start, queries, before, own, grad_context, context, log_total, cosine, sine
    )
    back = shifted(sent, "fsdp", -1)
    token_grad, proj_grad, gain_one_grad = finish(
        grad_query, kept, back, normed_one, tokens, grad_middle, full, gain_one, cosine, sine
    )
    gains = jnp.concatenate(
        [gain_one_grad, gain_two_grad, jnp.zeros((LANES - 2, model_width), fl)], axis=0
    ).T.astype(bf)
    owned = halving_sum(jnp.concatenate([proj_grad, out_grad, gains], axis=1), index)
    owned_kv = owned[:, 1024:2048].reshape(own_rows, 4, 2, LANES)

    pieces = []
    for bits in range(GROUP):
        piece = lax.dynamic_slice_in_dim(owned_experts, (member ^ bits) * own_rows, own_rows, 0)
        pieces.append(swapped(piece, bits) if bits else piece)
    experts = jnp.stack(group_order(pieces, member)).reshape(GROUP, own_rows, local, 3, hidden_width)
    experts = experts.transpose(3, 0, 2, 1, 4).reshape(3, EXPERTS, own_rows, hidden_width).astype(fl)
    return (
        activations,
        token_grad,
        owned[:, 3200],
        owned[:, :1024],
        owned_kv[:, :, 0].reshape(own_rows, 512),
        owned_kv[:, :, 1].reshape(own_rows, 512),
        owned[:, 2048:3072],
        owned[:, 3201],
        owned[:, 3072 : 3072 + EXPERTS],
        experts[0],
        experts[1],
        experts[2],
    )


def solution(mesh):
    rows = P("fsdp", None)
    line = P("fsdp")
    stack = P(None, "fsdp", None)
    return jax.shard_map(
        per_device,
        mesh=mesh,
        in_specs=(rows, line, rows, line, rows, rows, rows, rows, line, rows, stack, stack, stack, rows),
        out_specs=(rows, rows, line, rows, rows, rows, rows, line, rows, stack, stack, stack),
        check_vma=False,
    )
```

```python
import functools

import jax
import jax.numpy as jnp
from jax import lax
from jax.experimental import pallas as pl
from jax.experimental.pallas import tpu as pltpu
from jax.sharding import PartitionSpec as P

HEADS = 16
KV_HEADS = 8
HEAD_DIM = 64
TOP = 8
EXPERTS = 16
GROUP = 4
LANES = 128
NORM_EPS = 1e-06
ROPE_THETA = 10000.0
MASKED = -1e30
MIB = 1024 * 1024

bf = jnp.bfloat16
fl = jnp.float32
SLOT = (0, 2, 1, 3)

NN = (((1,), (0,)), ((), ()))
NT = (((1,), (1,)), ((), ()))
TN = (((0,), (0,)), ((), ()))


def mm(a, b, dims=NN):
    return lax.dot_general(a, b, dims, preferred_element_type=fl)


def params(mib):
    return pltpu.CompilerParams(vmem_limit_bytes=mib * MIB)


def shifted(block, axis, distance):
    devices = range(lax.axis_size(axis))
    route = [(i - distance, i) for i in devices if i - distance in devices]
    return lax.ppermute(block, axis, route)


def swapped(block, bits):
    return lax.ppermute(block, "fsdp", [(i, i ^ bits) for i in range(lax.axis_size("fsdp"))])


def lane_index(shape):
    return lax.broadcasted_iota(jnp.int32, shape, len(shape) - 1)


def swap_halves(v):
    first = (lane_index(v.shape) & 32) == 0
    return jnp.where(first, pltpu.roll(v, LANES - 32, 1), pltpu.roll(v, 32, 1))


def rope_tables(positions):
    half_width = HEAD_DIM // 2
    frequency = ROPE_THETA ** (-(jnp.arange(half_width, dtype=fl) * 2.0) / HEAD_DIM)
    angle_rows = positions.astype(fl)[:, None] * frequency[None, :]
    cosine, sine = jnp.cos(angle_rows), jnp.sin(angle_rows)
    return (
        jnp.concatenate([cosine] * 4, axis=1),
        jnp.concatenate([-sine, sine, -sine, sine], axis=1),
    )


def query_kernel(x_ref, w_ref, cos_ref, sin_ref, out_ref):
    lin = mm(x_ref[...], w_ref[...])
    for part in range(2):
        piece = lin[:, part * LANES : (part + 1) * LANES]
        turned = piece * cos_ref[...] + swap_halves(piece) * sin_ref[...]
        out_ref[:, part * LANES : (part + 1) * LANES] = (turned.astype(bf) * HEAD_DIM**-0.5).astype(bf)


def key_value_kernel(x_ref, w_ref, cos_ref, sin_ref, out_ref):
    lin = mm(x_ref[...], w_ref[...])
    piece = lin[:, :LANES]
    out_ref[:, :LANES] = (piece * cos_ref[...] + swap_halves(piece) * sin_ref[...]).astype(bf)
    out_ref[:, LANES:] = lin[:, LANES:].astype(bf)


def project(kernel, normed, weights, first_block, cosine, sine):
    rows, width = normed.shape
    return pl.pallas_call(
        kernel,
        grid=(4,),
        in_specs=[
            pl.BlockSpec((rows, width), lambda j: (0, 0)),
            pl.BlockSpec((width, 256), lambda j: (0, first_block + j)),
            pl.BlockSpec((rows, LANES), lambda j: (0, 0)),
            pl.BlockSpec((rows, LANES), lambda j: (0, 0)),
        ],
        out_specs=pl.BlockSpec((rows, 256), lambda j: (0, j)),
        out_shape=jax.ShapeDtypeStruct((rows, 1024), bf),
        compiler_params=params(32),
    )(normed, weights, cosine, sine)


def fill_bias(start_ref, bias_ref):
    rows = bias_ref.shape[0]
    column = lax.broadcasted_iota(jnp.int32, bias_ref.shape, 1) - rows
    row = lax.broadcasted_iota(jnp.int32, bias_ref.shape, 0)
    seen = (column >= start_ref[...]) & (column <= row)
    bias_ref[...] = jnp.where(seen, 0.0, MASKED)


def attend_kernel(start_ref, q_ref, prev_ref, own_ref, ctx_ref, low_ref, lse_ref, bias_ref, kv_ref):
    rows = q_ref.shape[0]
    half = rows // 2

    @pl.when(pl.program_id(0) == 0)
    def _():
        fill_bias(start_ref, bias_ref)

    kv_ref[:rows, :] = prev_ref[...]
    kv_ref[rows:, :] = own_ref[...]
    for tile in range(2):
        queries = pl.ds(tile * half, half)
        keys = rows + (tile + 1) * half
        bias = bias_ref[queries, :keys]
        for head in range(4):
            lane = 64 * (head // 2)
            scores = mm(
                q_ref[queries, head * 64 : head * 64 + 64], kv_ref[:keys, lane : lane + 64], NT
            )
            scores = scores + bias
            row_max = jnp.max(scores, axis=1, keepdims=True)
            weights = jnp.exp(scores - row_max)
            total = jnp.sum(weights, axis=1, keepdims=True)
            probs = (weights * (1.0 / total)).astype(bf)
            context = mm(probs, kv_ref[:keys, LANES + lane : LANES + lane + 64])
            ctx_ref[queries, head * 64 : head * 64 + 64] = context
            low_ref[queries, head * 64 : head * 64 + 64] = context.astype(bf)
            lse_ref[0, queries, head : head + 1] = row_max + jnp.log(total)


def attend(start, queries, before, own):
    rows = queries.shape[0]
    wide = pl.BlockSpec((rows, 256), lambda j: (0, j))
    return pl.pallas_call(
        attend_kernel,
        grid=(4,),
        in_specs=[pl.BlockSpec((rows, 1), lambda j: (0, 0)), wide, wide, wide],
        out_specs=[wide, wide, pl.BlockSpec((1, rows, LANES), lambda j: (j, 0, 0))],
        out_shape=[
            jax.ShapeDtypeStruct((rows, 1024), fl),
            jax.ShapeDtypeStruct((rows, 1024), bf),
            jax.ShapeDtypeStruct((4, rows, LANES), fl),
        ],
        scratch_shapes=[pltpu.VMEM((rows, 2 * rows), fl), pltpu.VMEM((2 * rows, 256), bf)],
        compiler_params=params(40),
    )(start, queries, before, own)


def attend_back_kernel(
    start_ref, q_ref, prev_ref, own_ref, gctx_ref, ctx_ref, lse_ref, cos_ref, sin_ref,
    gq_ref, sent_ref, kept_ref, bias_ref, kv_ref, gkv_ref, gq_acc_ref,
):
    rows = q_ref.shape[0]
    half = rows // 2

    @pl.when(pl.program_id(0) == 0)
    def _():
        fill_bias(start_ref, bias_ref)

    kv_ref[:rows, :] = prev_ref[...]
    kv_ref[rows:, :] = own_ref[...]
    gkv_ref[...] = jnp.zeros_like(gkv_ref)
    for tile in range(2):
        queries = pl.ds(tile * half, half)
        keys = rows + (tile + 1) * half
        bias = bias_ref[queries, :keys]
        for head in range(4):
            lane = 64 * (head // 2)
            here = slice(head * 64, head * 64 + 64)
            query = q_ref[queries, here]
            grad = gctx_ref[queries, here]
            key = kv_ref[:keys, lane : lane + 64]
            value = kv_ref[:keys, LANES + lane : LANES + lane + 64]
            inner = jnp.sum(grad.astype(fl) * ctx_ref[queries, here], axis=1, keepdims=True)
            scores = mm(query, key, NT) + bias
            probs = jnp.exp(scores - lse_ref[0, queries, head : head + 1])
            grad_probs = mm(grad, value, NT)
            grad_scores = (probs * (grad_probs - inner)).astype(bf)
            gq_acc_ref[queries, here] = mm(grad_scores, key) * HEAD_DIM**-0.5
            gkv_ref[:keys, lane : lane + 64] += mm(grad_scores, query, TN)
            gkv_ref[:keys, LANES + lane : LANES + lane + 64] += mm(probs.astype(bf), grad, TN)
    for part in range(2):
        here = slice(part * LANES, part * LANES + LANES)
        piece = gq_acc_ref[:, here]
        gq_ref[:, here] = (piece * cos_ref[...] - swap_halves(piece) * sin_ref[...]).astype(bf)
    sent_ref[...] = gkv_ref[:rows, :].astype(bf)
    kept_ref[...] = gkv_ref[rows:, :]


def attend_back(start, queries, before, own, grad_context, context, log_total, cosine, sine):
    rows = queries.shape[0]
    wide = pl.BlockSpec((rows, 256), lambda j: (0, j))
    table = pl.BlockSpec((rows, LANES), lambda j: (0, 0))
    return pl.pallas_call(
        attend_back_kernel,
        grid=(4,),
        in_specs=[
            pl.BlockSpec((rows, 1), lambda j: (0, 0)), wide, wide, wide, wide, wide,
            pl.BlockSpec((1, rows, LANES), lambda j: (j, 0, 0)), table, table,
        ],
        out_specs=[wide, wide, wide],
        out_shape=[
            jax.ShapeDtypeStruct((rows, 1024), bf),
            jax.ShapeDtypeStruct((rows, 1024), bf),
            jax.ShapeDtypeStruct((rows, 1024), fl),
        ],
        scratch_shapes=[
            pltpu.VMEM((rows, 2 * rows), fl),
            pltpu.VMEM((2 * rows, 256), bf),
            pltpu.VMEM((2 * rows, 256), fl),
            pltpu.VMEM((rows, 256), fl),
        ],
        compiler_params=params(48),
    )(start, queries, before, own, grad_context, context, log_total, cosine, sine)


def middle_kernel(ctx_ref, out_w_ref, router_ref, x_ref, gain_ref, chosen_ref, middle_ref, block_ref, gates_ref):
    width = x_ref.shape[1]
    middle = x_ref[...].astype(fl) + mm(ctx_ref[...], out_w_ref[...])
    inverse = lax.rsqrt(jnp.mean(middle * middle, axis=1, keepdims=True) + NORM_EPS)
    normed = (middle * inverse * gain_ref[...]).astype(bf)
    logits = mm(normed, router_ref[...])
    chosen = chosen_ref[...] > 0.0
    logits = jnp.where(chosen, logits, MASKED)
    weights = jnp.exp(logits - jnp.max(logits, axis=1, keepdims=True))
    weights = jnp.where(chosen, weights, 0.0)
    gates = weights / jnp.sum(weights, axis=1, keepdims=True)
    high = gates.astype(bf).astype(fl)
    middle_ref[...] = middle
    gates_ref[...] = gates
    block_ref[:, :width] = normed
    block_ref[:, width:] = (high + pltpu.roll(gates - high, EXPERTS, 1)).astype(bf)


def middle_part(ctx, full, tokens, gain, chosen):
    rows, width = tokens.shape
    return pl.pallas_call(
        middle_kernel,
        grid=(1,),
        in_specs=[
            pl.BlockSpec((rows, width), lambda j: (0, 0)),
            pl.BlockSpec((width, width), lambda j: (0, 2)),
            pl.BlockSpec((width, LANES), lambda j: (0, 24)),
            pl.BlockSpec((rows, width), lambda j: (0, 0)),
            pl.BlockSpec((1, width), lambda j: (0, 0)),
            pl.BlockSpec((rows, LANES), lambda j: (0, 0)),
        ],
        out_specs=[
            pl.BlockSpec((rows, width), lambda j: (0, 0)),
            pl.BlockSpec((rows, width + LANES), lambda j: (0, 0)),
            pl.BlockSpec((rows, LANES), lambda j: (0, 0)),
        ],
        out_shape=[
            jax.ShapeDtypeStruct((rows, width), fl),
            jax.ShapeDtypeStruct((rows, width + LANES), bf),
            jax.ShapeDtypeStruct((rows, LANES), fl),
        ],
        compiler_params=params(48),
    )(ctx, full, full, tokens, gain, chosen)


def reversed_bits(value, size):
    out = 0
    while size > 1:
        out, value, size = out * 2 + value % 2, value // 2, size // 2
    return out


def tokens_kernel(pieces, relative, where_ref, x0, x1, x2, x3, c0, c1, c2, c3, *refs):
    w_refs = refs[:pieces]
    (out_hbm, gn_hbm, hid_ref, gate_ref, up_ref, xs, cs, ws, out_acc, gn_acc, sems, w_sems) = refs[pieces:]
    step = pl.program_id(0)
    rows, width = c0.shape
    hidden_width = ws.shape[2] // 3
    cols = ws.shape[2]
    expert = where_ref[0] + step
    replica = where_ref[1]
    blocks = sum(w.shape[0] for w in w_refs)
    block_rows = width // blocks

    def weight_copies(which):
        copies, place = [], 0
        for w in w_refs:
            for inner in range(w.shape[0]):
                target = jnp.bitwise_xor(replica, reversed_bits(place, blocks)) if relative else place
                target = target * block_rows
                if relative:
                    target = pl.multiple_of(target, block_rows)
                copies.append(
                    pltpu.make_async_copy(
                        w.at[inner, :, which * cols : (which + 1) * cols],
                        ws.at[which, pl.ds(target, block_rows), :],
                        w_sems.at[which, place],
                    )
                )
                place += 1
        return copies

    @pl.when(step == 0)
    def _():
        copies = []
        for slot, (x, c) in enumerate(((x0, c0), (x1, c1), (x2, c2), (x3, c3))):
            here = pl.ds(slot * rows, rows)
            copies.append(pltpu.make_async_copy(x, xs.at[here], sems.at[2 * slot]))
            copies.append(pltpu.make_async_copy(c, cs.at[here], sems.at[2 * slot + 1]))
        for which in range(ws.shape[0]):
            copies += weight_copies(which)
        for copy in copies:
            copy.start()
        out_acc[...] = jnp.zeros_like(out_acc)
        gn_acc[...] = jnp.zeros_like(gn_acc)
        for copy in copies:
            copy.wait()

    def tile_step(tile, carry):
        here = pl.ds(pl.multiple_of(tile * rows, rows), rows)
        x_tile = xs[here, :width]
        gate_w = ws[step, :, :hidden_width]
        up_w = ws[step, :, hidden_width : 2 * hidden_width]
        down_w = ws[step, :, 2 * hidden_width :]
        gate = mm(x_tile, gate_w)
        up = mm(x_tile, up_w)
        raw = mm(cs[here, :], down_w)
        packed = xs[here, width:].astype(fl)
        lane = lane_index(packed.shape)
        mine = (lane == expert) | (lane == expert + EXPERTS)
        gates = jnp.sum(jnp.where(mine, packed, 0.0), axis=1, keepdims=True)
        sigmoid = 1.0 / (1.0 + jnp.exp(-gate))
        silu = gate * sigmoid
        hidden = (silu * up).astype(bf).astype(fl)
        grad_gates = jnp.sum(hidden * raw, axis=1, keepdims=True)
        grad_hidden = raw * gates
        hid = (hidden * gates).astype(bf)
        grad_gate = (grad_hidden * up * sigmoid * (1.0 + gate * (1.0 - sigmoid))).astype(bf)
        grad_up = (grad_hidden * silu).astype(bf)
        hid_ref[0, here, :] = hid
        gate_ref[0, here, :] = grad_gate
        up_ref[0, here, :] = grad_up
        out_acc[here, :] += mm(hid, down_w, NT)
        gn_acc[here, :width] += mm(grad_gate, gate_w, NT) + mm(grad_up, up_w, NT)
        gn_acc[here, width:] += jnp.where(lane == expert, grad_gates, 0.0)
        return carry

    lax.fori_loop(0, GROUP, tile_step, 0)

    @pl.when(step == pl.num_programs(0) - 1)
    def _():
        gates_part = gn_acc[:, width:]
        high = gates_part.astype(bf).astype(fl)
        low = (gates_part - high).astype(bf).astype(fl)
        gn_acc[:, width:] = high + pltpu.roll(low, EXPERTS, 1)
        one = pltpu.make_async_copy(out_acc, out_hbm, sems.at[0])
        two = pltpu.make_async_copy(gn_acc, gn_hbm, sems.at[1])
        one.start()
        two.start()
        one.wait()
        two.wait()


def experts_tokens(first, replica, blocks, cots, weights):
    rows, width = cots[0].shape
    local = EXPERTS // GROUP // 2
    cols = weights[0].shape[2] // local
    hidden_width = cols // 3
    total = GROUP * rows
    row_blocks = sum(w.shape[0] for w in weights)
    anywhere = pl.BlockSpec(memory_space=pl.ANY)
    kept = pl.BlockSpec((1, total, hidden_width), lambda e, s: (e, 0, 0))
    kept_shape = jax.ShapeDtypeStruct((local, total, hidden_width), bf)
    return pl.pallas_call(
        functools.partial(tokens_kernel, len(weights), len(weights) > 1),
        grid_spec=pltpu.PrefetchScalarGridSpec(
            num_scalar_prefetch=1,
            grid=(local,),
            in_specs=[anywhere] * (8 + len(weights)),
            out_specs=[anywhere, anywhere, kept, kept, kept],
            scratch_shapes=[
                pltpu.VMEM((total, width + LANES), bf),
                pltpu.VMEM((total, width), bf),
                pltpu.VMEM((local, width, cols), bf),
                pltpu.VMEM((total, width), fl),
                pltpu.VMEM((total, width + LANES), fl),
                pltpu.SemaphoreType.DMA((8,)),
                pltpu.SemaphoreType.DMA((local, row_blocks)),
            ],
        ),
        out_shape=[
            jax.ShapeDtypeStruct((total, width), fl),
            jax.ShapeDtypeStruct((total, width + LANES), fl),
            kept_shape, kept_shape, kept_shape,
        ],
        compiler_params=params(60),
    )(jnp.stack([first, replica]), *blocks, *cots, *weights)


def weights_kernel(relative, where_ref, x0, x1, x2, x3, c0, c1, c2, c3, hid_ref, gate_ref, up_ref, *refs):
    outs = refs[: 2 if relative else 1]
    xs, cs, xt, ct, sems = refs[len(outs) :]
    rows, width = c0.shape
    hidden_width = hid_ref.shape[2]

    @pl.when(pl.program_id(0) == 0)
    def _():
        copies = []
        for slot, (x, c) in enumerate(((x0, c0), (x1, c1), (x2, c2), (x3, c3))):
            here = pl.ds(slot * rows, rows)
            copies.append(pltpu.make_async_copy(x, xs.at[here], sems.at[2 * slot]))
            copies.append(pltpu.make_async_copy(c, cs.at[here], sems.at[2 * slot + 1]))
        for copy in copies:
            copy.start()
        for copy in copies:
            copy.wait()
        for slot in range(GROUP):
            here = slice(slot * rows, (slot + 1) * rows)
            for source, target in ((xs, xt), (cs, ct)):
                turned = source[here, :width].T
                if not relative:
                    target[:, here] = turned
                    continue
                blocks = 2 * outs[0].shape[0]
                size = width // blocks
                for block in range(blocks):
                    place = jnp.bitwise_xor(where_ref[0], reversed_bits(block, blocks))
                    place = pl.multiple_of(place * size, size)
                    target[pl.ds(place, size), here] = turned[block * size : (block + 1) * size]

    for part, (left, right) in enumerate(((xt, gate_ref), (xt, up_ref), (ct, hid_ref))):
        grad = mm(left[...], right[0]).astype(bf)
        here = slice(part * hidden_width, (part + 1) * hidden_width)
        if relative:
            half, size = outs[0].shape[:2]
            outs[0][:, :, here] = grad[: width // 2].reshape(half, size, hidden_width)
            outs[1][:, :, here] = grad[width // 2 :].reshape(half, size, hidden_width)
        else:
            outs[0][:, here] = grad


def experts_weights(replica, replicas, relative, blocks, cots, hid, gate, up):
    rows, width = cots[0].shape
    local, total, hidden_width = hid.shape
    cols = 3 * hidden_width
    anywhere = pl.BlockSpec(memory_space=pl.ANY)
    kept = pl.BlockSpec((1, total, hidden_width), lambda e, s: (e, 0, 0))
    if relative:
        half = (replicas // 2, width // replicas)
        out_specs = [pl.BlockSpec((*half, cols), lambda e, s: (0, 0, e))] * 2
        out_shape = [jax.ShapeDtypeStruct((*half, local * cols), bf)] * 2
    else:
        out_specs = [pl.BlockSpec((width, cols), lambda e, s: (0, e))]
        out_shape = [jax.ShapeDtypeStruct((width, local * cols), bf)]
    back = 0 * replica
    for bit in range(replicas.bit_length() - 1):
        back = back * 2 + (replica // 2**bit) % 2
    return pl.pallas_call(
        functools.partial(weights_kernel, relative),
        grid_spec=pltpu.PrefetchScalarGridSpec(
            num_scalar_prefetch=1,
            grid=(local,),
            in_specs=[anywhere] * 8 + [kept] * 3,
            out_specs=out_specs,
            scratch_shapes=[
                pltpu.VMEM((total, width + LANES), bf),
                pltpu.VMEM((total, width), bf),
                pltpu.VMEM((width, total), bf),
                pltpu.VMEM((width, total), bf),
                pltpu.SemaphoreType.DMA((8,)),
            ],
        ),
        out_shape=out_shape,
        compiler_params=params(56),
    )(back.reshape(1), *blocks, *cots, hid, gate, up)


def middle_back_kernel(
    gn_ref, gates_ref, middle_ref, cot_ref, ctx_ref, out_w_ref, router_ref, gain_ref,
    gm_ref, gctx_ref, gw_ref, gain_grad_ref,
):
    width = cot_ref.shape[1]
    packed = gn_ref[:, width:]
    gates = gates_ref[...]
    grad_gates = packed + pltpu.roll(packed, LANES - EXPERTS, 1)
    inner = jnp.sum(gates * grad_gates, axis=1, keepdims=True)
    grad_logits = (gates * (grad_gates - inner)).astype(bf)
    middle = middle_ref[...]
    inverse = lax.rsqrt(jnp.mean(middle * middle, axis=1, keepdims=True) + NORM_EPS)
    gain = gain_ref[...]
    unit = middle * inverse
    normed = (unit * gain).astype(bf)
    grad_normed = gn_ref[:, :width] + mm(grad_logits, router_ref[...], NT)
    gw_ref[:, width:] = mm(normed, grad_logits, TN).astype(bf)
    gain_grad_ref[...] = jnp.sum(grad_normed * unit, axis=0, keepdims=True)
    scaled = grad_normed * gain
    mean = jnp.mean(scaled * middle, axis=1, keepdims=True)
    grad_middle = cot_ref[...].astype(fl) + inverse * scaled - unit * (inverse * inverse * mean)
    gm_ref[...] = grad_middle
    branch = grad_middle.astype(bf)
    gctx_ref[...] = mm(branch, out_w_ref[...], NT).astype(bf)
    gw_ref[:, :width] = mm(ctx_ref[...], branch, TN).astype(bf)


def middle_back(gn, gates, middle, cot, ctx, full, gain):
    rows, width = cot.shape
    here = lambda *shape: pl.BlockSpec(shape, lambda j: (0, 0))
    return pl.pallas_call(
        middle_back_kernel,
        grid=(1,),
        in_specs=[
            here(rows, width + LANES), here(rows, LANES), here(rows, width), here(rows, width), here(rows, width),
            pl.BlockSpec((width, width), lambda j: (0, 2)),
            pl.BlockSpec((width, LANES), lambda j: (0, 24)),
            here(1, width),
        ],
        out_specs=[here(rows, width), here(rows, width), here(width, width + LANES), here(1, width)],
        out_shape=[
            jax.ShapeDtypeStruct((rows, width), fl),
            jax.ShapeDtypeStruct((rows, width), bf),
            jax.ShapeDtypeStruct((width, width + LANES), bf),
            jax.ShapeDtypeStruct((1, width), fl),
        ],
        compiler_params=params(56),
    )(gn, gates, middle, cot, ctx, full, full, gain)


def finish_kernel(
    gq_ref, kept_ref, back_ref, normed_ref, x_ref, gm_ref, w_ref, gain_ref, cos_ref, sin_ref,
    token_ref, gw_ref, gain_grad_ref, gkv_ref,
):
    width = x_ref.shape[1]
    for part in range(4):
        first = part * 256
        both = kept_ref[:, first : first + 256] + back_ref[:, first : first + 256].astype(fl)
        piece = both[:, :LANES]
        gkv_ref[:, first : first + LANES] = (
            piece * cos_ref[...] - swap_halves(piece) * sin_ref[...]
        ).astype(bf)
        gkv_ref[:, first + LANES : first + 256] = both[:, LANES:].astype(bf)
    normed = normed_ref[...]
    gw_ref[:, :width] = mm(normed, gq_ref[...], TN).astype(bf)
    gw_ref[:, width:] = mm(normed, gkv_ref[...], TN).astype(bf)
    grad_normed = mm(gq_ref[...], w_ref[:, :width], NT) + mm(gkv_ref[...], w_ref[:, width:], NT)
    x = x_ref[...].astype(fl)
    inverse = lax.rsqrt(jnp.mean(x * x, axis=1, keepdims=True) + NORM_EPS)
    unit = x * inverse
    gain_grad_ref[...] = jnp.sum(grad_normed * unit, axis=0, keepdims=True)
    scaled = grad_normed * gain_ref[...]
    mean = jnp.mean(scaled * x, axis=1, keepdims=True)
    token_ref[...] = gm_ref[...] + inverse * scaled - unit * (inverse * inverse * mean)


def finish(grad_query, kept, back, normed, tokens, grad_middle, full, gain, cosine, sine):
    rows, width = tokens.shape
    here = lambda *shape: pl.BlockSpec(shape, lambda j: (0, 0))
    return pl.pallas_call(
        finish_kernel,
        grid=(1,),
        in_specs=[
            here(rows, width), here(rows, width), here(rows, width), here(rows, width), here(rows, width),
            here(rows, width), here(width, 2 * width), here(1, width), here(rows, LANES), here(rows, LANES),
        ],
        out_specs=[here(rows, width), here(width, 2 * width), here(1, width)],
        out_shape=[
            jax.ShapeDtypeStruct((rows, width), fl),
            jax.ShapeDtypeStruct((width, 2 * width), bf),
            jax.ShapeDtypeStruct((1, width), fl),
        ],
        scratch_shapes=[pltpu.VMEM((rows, width), bf)],
        compiler_params=params(60),
    )(grad_query, kept, back, normed, tokens, grad_middle, full, gain, cosine, sine)


def halving_sum(part, index):
    n = lax.axis_size("fsdp")
    cur = part.reshape(n, part.shape[0] // n, part.shape[1])
    bits = 1
    while bits < n:
        mine = (index // bits) % 2
        pairs = cur.reshape(cur.shape[0] // 2, 2, cur.shape[1], cur.shape[2])
        keep = lax.dynamic_index_in_dim(pairs, mine, 1, keepdims=False)
        send = lax.dynamic_index_in_dim(pairs, 1 - mine, 1, keepdims=False)
        cur = keep.astype(fl) + swapped(send.astype(bf), bits).astype(fl)
        bits *= 2
    return cur[0]


def group_order(pieces, member):
    one, two = member % 2 == 1, member // 2 == 1
    a, b, c, d = pieces
    a, b, c, d = jnp.where(one, b, a), jnp.where(one, a, b), jnp.where(one, d, c), jnp.where(one, c, d)
    return jnp.where(two, c, a), jnp.where(two, d, b), jnp.where(two, a, c), jnp.where(two, b, d)


def per_device(
    tokens, positions, routes, attn_gain, w_query, w_key, w_value, w_out, mlp_gain, w_router,
    w_gate, w_up, w_down, cotangent,
):
    n = lax.axis_size("fsdp")
    index = lax.axis_index("fsdp")
    member = index % GROUP
    rows_dev, model_width = tokens.shape
    own_rows = w_query.shape[0]
    hidden_width = w_gate.shape[2]
    local = EXPERTS // GROUP
    across = [[r * GROUP + g for r in range(n // GROUP)] for g in range(GROUP)]

    key_value = jnp.concatenate(
        [w_key.reshape(own_rows, 4, LANES), w_value.reshape(own_rows, 4, LANES)], axis=2
    ).reshape(own_rows, model_width)
    small = jnp.concatenate(
        [w_router, attn_gain[:, None], mlp_gain[:, None], jnp.zeros((own_rows, LANES - EXPERTS - 2), bf)],
        axis=1,
    )
    packed = jnp.concatenate([w_query, key_value, w_out, small], axis=1)
    full = lax.all_gather(packed, "fsdp", axis=0, tiled=True)

    shard = jnp.concatenate([w_gate, w_up, w_down], axis=2).reshape(
        GROUP, local, own_rows, 3 * hidden_width
    )
    pieces = []
    for bits in range(GROUP):
        piece = lax.dynamic_index_in_dim(shard, member ^ bits, 0, keepdims=False)
        pieces.append(swapped(piece, bits) if bits else piece)
    mine = jnp.stack(group_order(pieces, member)).transpose(0, 2, 1, 3)
    mine = mine.reshape(GROUP * own_rows, 2, local // 2 * 3 * hidden_width)
    mine_b, full = lax.optimization_barrier((mine[:, 1], full))
    weights_b = lax.all_gather(mine_b, "fsdp", axis=0, tiled=False, axis_index_groups=across)
    gathered, bits = mine[None, :, 0], n // 2
    while bits > GROUP:
        gathered = jnp.concatenate([gathered, swapped(gathered, bits)], axis=0)
        bits //= 2
    weights_a = (gathered, swapped(gathered, GROUP))

    cot_x = swapped(cotangent, 2)
    cots = (cotangent, cot_x, swapped(cotangent, 1), swapped(cot_x, 1))
    tokens, *cots = lax.optimization_barrier((tokens, *cots))

    gain_one = full[:, 3088].astype(fl)[None, :]
    gain_two = full[:, 3089].astype(fl)[None, :]
    cosine, sine = rope_tables(positions)
    residual = tokens.astype(fl)
    inverse_one = lax.rsqrt(jnp.mean(residual * residual, axis=-1, keepdims=True) + NORM_EPS)
    normed_one = (residual * inverse_one * gain_one).astype(bf)
    own = project(key_value_kernel, normed_one, full, 4, cosine, sine)
    before = shifted(own, "fsdp", 1)
    queries = project(query_kernel, normed_one, full, 0, cosine, sine)
    start = (jnp.arange(rows_dev, dtype=jnp.int32) - positions)[:, None]
    context, context_low, log_total = attend(start, queries, before, own)

    lanes = jnp.arange(LANES, dtype=jnp.int32)
    chosen = jnp.any(routes[:, :, None] == lanes[None, None, :], axis=1).astype(fl)
    middle, block, gates = middle_part(context_low, full, tokens, gain_two, chosen)

    block_x = swapped(block, 2)
    blocks = (block, block_x, swapped(block, 1), swapped(block_x, 1))
    first = (member * local).astype(jnp.int32)
    replica = (index // GROUP).astype(jnp.int32)
    out_a, gn_a, *kept_a = experts_tokens(first, replica, blocks, cots, weights_a)
    out_b, gn_b, *kept_b = experts_tokens(first + local // 2, 0 * replica, blocks, cots, (weights_b,))

    def returned(one, two):
        parts = (one + two).reshape(GROUP, rows_dev, one.shape[1])
        other = swapped(parts[2:].astype(bf), 1).astype(fl)
        away = swapped((parts[1] + other[1]).astype(bf), 2).astype(fl)
        return parts[0] + other[0] + away

    gn = returned(gn_a, gn_b)
    (grads_a,) = experts_weights(replica, n // GROUP, False, blocks, cots, *kept_a)
    grads_a, *kept_b = lax.optimization_barrier((grads_a, *kept_b))
    owned_a = lax.psum_scatter(
        grads_a, "fsdp", scatter_dimension=0, tiled=True, axis_index_groups=across
    )
    keep, send = experts_weights(replica, n // GROUP, True, blocks, cots, *kept_b)
    gn, keep, send = lax.optimization_barrier((gn, keep, send))
    other = swapped(send, GROUP)
    grad_middle, grad_context, out_grad, gain_two_grad = middle_back(
        gn, gates, middle, cotangent, context_low, full, gain_two
    )
    activations = (middle + returned(out_a, out_b)).astype(bf)
    grad_query, sent, kept = attend_back(
        start, queries, before, own, grad_context, context, log_total, cosine, sine
    )
    back, other = lax.optimization_barrier((shifted(sent, "fsdp", -1), other))
    summed, bits = keep.astype(fl) + other.astype(fl), 2 * GROUP
    while bits < n:
        half = summed.shape[0] // 2
        summed = summed[:half] + swapped(summed[half:].astype(bf), bits).astype(fl)
        bits *= 2
    owned_b = summed[0].astype(bf)
    token_grad, proj_grad, gain_one_grad = finish(
        grad_query, kept, back, normed_one, tokens, grad_middle, full, gain_one, cosine, sine
    )
    gains = jnp.concatenate(
        [gain_one_grad, gain_two_grad, jnp.zeros((LANES - 2, model_width), fl)], axis=0
    ).T.astype(bf)
    owned = halving_sum(jnp.concatenate([proj_grad, out_grad, gains], axis=1), index)
    owned_kv = owned[:, 1024:2048].reshape(own_rows, 4, 2, LANES)

    chunks = []
    for owned_part in (owned_a, owned_b):
        pieces = []
        for bits in range(GROUP):
            piece = lax.dynamic_slice_in_dim(owned_part, (member ^ bits) * own_rows, own_rows, 0)
            pieces.append(swapped(piece, bits) if bits else piece)
        chunks.append(jnp.stack(group_order(pieces, member)))
    experts = jnp.stack(chunks, axis=1)
    experts = experts.reshape(GROUP, 2, own_rows, local // 2, 3, hidden_width).transpose(4, 0, 1, 3, 2, 5)
    experts = experts.reshape(3, EXPERTS, own_rows, hidden_width).astype(fl)
    return (
        activations,
        token_grad,
        owned[:, 3200],
        owned[:, :1024],
        owned_kv[:, :, 0].reshape(own_rows, 512),
        owned_kv[:, :, 1].reshape(own_rows, 512),
        owned[:, 2048:3072],
        owned[:, 3201],
        owned[:, 3072 : 3072 + EXPERTS],
        experts[0],
        experts[1],
        experts[2],
    )


def solution(mesh):
    rows = P("fsdp", None)
    line = P("fsdp")
    stack = P(None, "fsdp", None)
    return jax.shard_map(
        per_device,
        mesh=mesh,
        in_specs=(rows, line, rows, line, rows, rows, rows, rows, line, rows, stack, stack, stack, rows),
        out_specs=(rows, rows, line, rows, rows, rows, rows, line, rows, stack, stack, stack),
        check_vma=False,
    )
```

```python
import functools

import jax
import jax.numpy as jnp
from jax import lax
from jax.experimental import pallas as pl
from jax.experimental.pallas import tpu as pltpu
from jax.sharding import PartitionSpec as P

HEADS = 16
KV_HEADS = 8
HEAD_DIM = 64
TOP = 8
EXPERTS = 16
GROUP = 4
LANES = 128
NORM_EPS = 1e-06
ROPE_THETA = 10000.0
MASKED = -1e30
MIB = 1024 * 1024

bf = jnp.bfloat16
fl = jnp.float32
SLOT = (0, 2, 1, 3)

NN = (((1,), (0,)), ((), ()))
NT = (((1,), (1,)), ((), ()))
TN = (((0,), (0,)), ((), ()))


def mm(a, b, dims=NN):
    return lax.dot_general(a, b, dims, preferred_element_type=fl)


def params(mib):
    return pltpu.CompilerParams(vmem_limit_bytes=mib * MIB)


def shifted(block, axis, distance):
    devices = range(lax.axis_size(axis))
    route = [(i - distance, i) for i in devices if i - distance in devices]
    return lax.ppermute(block, axis, route)


def swapped(block, bits):
    return lax.ppermute(block, "fsdp", [(i, i ^ bits) for i in range(lax.axis_size("fsdp"))])


def lane_index(shape):
    return lax.broadcasted_iota(jnp.int32, shape, len(shape) - 1)


def swap_halves(v):
    first = (lane_index(v.shape) & 32) == 0
    return jnp.where(first, pltpu.roll(v, LANES - 32, 1), pltpu.roll(v, 32, 1))


def rope_tables(positions):
    half_width = HEAD_DIM // 2
    frequency = ROPE_THETA ** (-(jnp.arange(half_width, dtype=fl) * 2.0) / HEAD_DIM)
    angle_rows = positions.astype(fl)[:, None] * frequency[None, :]
    cosine, sine = jnp.cos(angle_rows), jnp.sin(angle_rows)
    return (
        jnp.concatenate([cosine] * 4, axis=1),
        jnp.concatenate([-sine, sine, -sine, sine], axis=1),
    )


def query_kernel(x_ref, w_ref, cos_ref, sin_ref, out_ref):
    lin = mm(x_ref[...], w_ref[...])
    for part in range(2):
        piece = lin[:, part * LANES : (part + 1) * LANES]
        turned = piece * cos_ref[...] + swap_halves(piece) * sin_ref[...]
        out_ref[:, part * LANES : (part + 1) * LANES] = (turned.astype(bf) * HEAD_DIM**-0.5).astype(bf)


def key_value_kernel(x_ref, w_ref, cos_ref, sin_ref, out_ref):
    lin = mm(x_ref[...], w_ref[...])
    piece = lin[:, :LANES]
    out_ref[:, :LANES] = (piece * cos_ref[...] + swap_halves(piece) * sin_ref[...]).astype(bf)
    out_ref[:, LANES:] = lin[:, LANES:].astype(bf)


def project(kernel, normed, weights, first_block, cosine, sine):
    rows, width = normed.shape
    return pl.pallas_call(
        kernel,
        grid=(4,),
        in_specs=[
            pl.BlockSpec((rows, width), lambda j: (0, 0)),
            pl.BlockSpec((width, 256), lambda j: (0, first_block + j)),
            pl.BlockSpec((rows, LANES), lambda j: (0, 0)),
            pl.BlockSpec((rows, LANES), lambda j: (0, 0)),
        ],
        out_specs=pl.BlockSpec((rows, 256), lambda j: (0, j)),
        out_shape=jax.ShapeDtypeStruct((rows, 1024), bf),
        compiler_params=params(32),
    )(normed, weights, cosine, sine)


def fill_bias(start_ref, bias_ref):
    rows = bias_ref.shape[0]
    column = lax.broadcasted_iota(jnp.int32, bias_ref.shape, 1) - rows
    row = lax.broadcasted_iota(jnp.int32, bias_ref.shape, 0)
    seen = (column >= start_ref[...]) & (column <= row)
    bias_ref[...] = jnp.where(seen, 0.0, MASKED)


def attend_kernel(start_ref, q_ref, prev_ref, own_ref, ctx_ref, low_ref, lse_ref, bias_ref, kv_ref):
    rows = q_ref.shape[0]
    half = rows // 2

    @pl.when(pl.program_id(0) == 0)
    def _():
        fill_bias(start_ref, bias_ref)

    kv_ref[:rows, :] = prev_ref[...]
    kv_ref[rows:, :] = own_ref[...]
    for tile in range(2):
        queries = pl.ds(tile * half, half)
        keys = rows + (tile + 1) * half
        bias = bias_ref[queries, :keys]
        for head in range(4):
            lane = 64 * (head // 2)
            scores = mm(
                q_ref[queries, head * 64 : head * 64 + 64], kv_ref[:keys, lane : lane + 64], NT
            )
            scores = scores + bias
            row_max = jnp.max(scores, axis=1, keepdims=True)
            weights = jnp.exp(scores - row_max)
            total = jnp.sum(weights, axis=1, keepdims=True)
            probs = (weights * (1.0 / total)).astype(bf)
            context = mm(probs, kv_ref[:keys, LANES + lane : LANES + lane + 64])
            ctx_ref[queries, head * 64 : head * 64 + 64] = context
            low_ref[queries, head * 64 : head * 64 + 64] = context.astype(bf)
            lse_ref[0, queries, head : head + 1] = row_max + jnp.log(total)


def attend(start, queries, before, own):
    rows = queries.shape[0]
    wide = pl.BlockSpec((rows, 256), lambda j: (0, j))
    return pl.pallas_call(
        attend_kernel,
        grid=(4,),
        in_specs=[pl.BlockSpec((rows, 1), lambda j: (0, 0)), wide, wide, wide],
        out_specs=[wide, wide, pl.BlockSpec((1, rows, LANES), lambda j: (j, 0, 0))],
        out_shape=[
            jax.ShapeDtypeStruct((rows, 1024), fl),
            jax.ShapeDtypeStruct((rows, 1024), bf),
            jax.ShapeDtypeStruct((4, rows, LANES), fl),
        ],
        scratch_shapes=[pltpu.VMEM((rows, 2 * rows), fl), pltpu.VMEM((2 * rows, 256), bf)],
        compiler_params=params(40),
    )(start, queries, before, own)


def attend_back_kernel(
    start_ref, q_ref, prev_ref, own_ref, gctx_ref, ctx_ref, lse_ref, cos_ref, sin_ref,
    gq_ref, sent_ref, kept_ref, bias_ref, kv_ref, gkv_ref, gq_acc_ref,
):
    rows = q_ref.shape[0]
    half = rows // 2

    @pl.when(pl.program_id(0) == 0)
    def _():
        fill_bias(start_ref, bias_ref)

    kv_ref[:rows, :] = prev_ref[...]
    kv_ref[rows:, :] = own_ref[...]
    gkv_ref[...] = jnp.zeros_like(gkv_ref)
    for tile in range(2):
        queries = pl.ds(tile * half, half)
        keys = rows + (tile + 1) * half
        bias = bias_ref[queries, :keys]
        for head in range(4):
            lane = 64 * (head // 2)
            here = slice(head * 64, head * 64 + 64)
            query = q_ref[queries, here]
            grad = gctx_ref[queries, here]
            key = kv_ref[:keys, lane : lane + 64]
            value = kv_ref[:keys, LANES + lane : LANES + lane + 64]
            inner = jnp.sum(grad.astype(fl) * ctx_ref[queries, here], axis=1, keepdims=True)
            scores = mm(query, key, NT) + bias
            probs = jnp.exp(scores - lse_ref[0, queries, head : head + 1])
            grad_probs = mm(grad, value, NT)
            grad_scores = (probs * (grad_probs - inner)).astype(bf)
            gq_acc_ref[queries, here] = mm(grad_scores, key) * HEAD_DIM**-0.5
            gkv_ref[:keys, lane : lane + 64] += mm(grad_scores, query, TN)
            gkv_ref[:keys, LANES + lane : LANES + lane + 64] += mm(probs.astype(bf), grad, TN)
    for part in range(2):
        here = slice(part * LANES, part * LANES + LANES)
        piece = gq_acc_ref[:, here]
        gq_ref[:, here] = (piece * cos_ref[...] - swap_halves(piece) * sin_ref[...]).astype(bf)
    sent_ref[...] = gkv_ref[:rows, :].astype(bf)
    kept_ref[...] = gkv_ref[rows:, :]


def attend_back(start, queries, before, own, grad_context, context, log_total, cosine, sine):
    rows = queries.shape[0]
    wide = pl.BlockSpec((rows, 256), lambda j: (0, j))
    table = pl.BlockSpec((rows, LANES), lambda j: (0, 0))
    return pl.pallas_call(
        attend_back_kernel,
        grid=(4,),
        in_specs=[
            pl.BlockSpec((rows, 1), lambda j: (0, 0)), wide, wide, wide, wide, wide,
            pl.BlockSpec((1, rows, LANES), lambda j: (j, 0, 0)), table, table,
        ],
        out_specs=[wide, wide, wide],
        out_shape=[
            jax.ShapeDtypeStruct((rows, 1024), bf),
            jax.ShapeDtypeStruct((rows, 1024), bf),
            jax.ShapeDtypeStruct((rows, 1024), fl),
        ],
        scratch_shapes=[
            pltpu.VMEM((rows, 2 * rows), fl),
            pltpu.VMEM((2 * rows, 256), bf),
            pltpu.VMEM((2 * rows, 256), fl),
            pltpu.VMEM((rows, 256), fl),
        ],
        compiler_params=params(48),
    )(start, queries, before, own, grad_context, context, log_total, cosine, sine)


def middle_kernel(ctx_ref, out_w_ref, router_ref, x_ref, gain_ref, chosen_ref, middle_ref, block_ref, gates_ref):
    width = x_ref.shape[1]
    middle = x_ref[...].astype(fl) + mm(ctx_ref[...], out_w_ref[...])
    inverse = lax.rsqrt(jnp.mean(middle * middle, axis=1, keepdims=True) + NORM_EPS)
    normed = (middle * inverse * gain_ref[...]).astype(bf)
    logits = mm(normed, router_ref[...])
    chosen = chosen_ref[...] > 0.0
    logits = jnp.where(chosen, logits, MASKED)
    weights = jnp.exp(logits - jnp.max(logits, axis=1, keepdims=True))
    weights = jnp.where(chosen, weights, 0.0)
    gates = weights / jnp.sum(weights, axis=1, keepdims=True)
    high = gates.astype(bf).astype(fl)
    middle_ref[...] = middle
    gates_ref[...] = gates
    block_ref[:, :width] = normed
    block_ref[:, width:] = (high + pltpu.roll(gates - high, EXPERTS, 1)).astype(bf)


def middle_part(ctx, full, tokens, gain, chosen):
    rows, width = tokens.shape
    return pl.pallas_call(
        middle_kernel,
        grid=(1,),
        in_specs=[
            pl.BlockSpec((rows, width), lambda j: (0, 0)),
            pl.BlockSpec((width, width), lambda j: (0, 2)),
            pl.BlockSpec((width, LANES), lambda j: (0, 24)),
            pl.BlockSpec((rows, width), lambda j: (0, 0)),
            pl.BlockSpec((1, width), lambda j: (0, 0)),
            pl.BlockSpec((rows, LANES), lambda j: (0, 0)),
        ],
        out_specs=[
            pl.BlockSpec((rows, width), lambda j: (0, 0)),
            pl.BlockSpec((rows, width + LANES), lambda j: (0, 0)),
            pl.BlockSpec((rows, LANES), lambda j: (0, 0)),
        ],
        out_shape=[
            jax.ShapeDtypeStruct((rows, width), fl),
            jax.ShapeDtypeStruct((rows, width + LANES), bf),
            jax.ShapeDtypeStruct((rows, LANES), fl),
        ],
        compiler_params=params(48),
    )(ctx, full, full, tokens, gain, chosen)


def reversed_bits(value, size):
    out = 0
    while size > 1:
        out, value, size = out * 2 + value % 2, value // 2, size // 2
    return out


def experts_kernel(last, where_ref, x0, x1, x2, x3, c0, c1, c2, c3, w_ref, *refs):
    if last:
        prev_out, prev_gn, prev_xt, prev_ct, out_hbm, gn_hbm, keep_ref, send_ref = refs[:8]
    else:
        out_hbm, gn_hbm, grad_ref, xt_hbm, ct_hbm = refs[:5]
    xs, cs, xt, ct, out_acc, gn_acc, hid_s, gate_s, up_s, sems, turn_sems = refs[8 if last else 5 :]
    step = pl.program_id(0)
    rows, width = c0.shape
    hidden_width = w_ref.shape[1] // 3
    expert = where_ref[0] + step

    if not last:
        turned_out = [
            pltpu.make_async_copy(xt, xt_hbm, turn_sems.at[0, 0]),
            pltpu.make_async_copy(ct, ct_hbm, turn_sems.at[1, 0]),
        ]

    @pl.when(step == 0)
    def _():
        copies = []
        for slot, (x, c) in enumerate(((x0, c0), (x1, c1), (x2, c2), (x3, c3))):
            here = pl.ds(slot * rows, rows)
            copies.append(pltpu.make_async_copy(x, xs.at[here], sems.at[2 * slot]))
            copies.append(pltpu.make_async_copy(c, cs.at[here], sems.at[2 * slot + 1]))
        if last:
            copies.append(pltpu.make_async_copy(prev_out, out_acc, sems.at[8]))
            copies.append(pltpu.make_async_copy(prev_gn, gn_acc, sems.at[9]))
            blocks = turn_sems.shape[1]
            size = width // blocks
            for kind, (source, target) in enumerate(((prev_xt, xt), (prev_ct, ct))):
                for block in range(blocks):
                    place = jnp.bitwise_xor(where_ref[1], reversed_bits(block, blocks))
                    place = pl.multiple_of(place * size, size)
                    copies.append(
                        pltpu.make_async_copy(
                            source.at[pl.ds(block * size, size), :],
                            target.at[pl.ds(place, size), :],
                            turn_sems.at[kind, block],
                        )
                    )
        for copy in copies:
            copy.start()
        if not last:
            out_acc[...] = jnp.zeros_like(out_acc)
            gn_acc[...] = jnp.zeros_like(gn_acc)
        for copy in copies:
            copy.wait()
        if not last:
            for slot in range(GROUP):
                here = slice(slot * rows, (slot + 1) * rows)
                xt[:, here] = xs[here, :width].T
                ct[:, here] = cs[here, :].T
            for copy in turned_out:
                copy.start()

    def tile_step(tile, carry):
        here = pl.ds(pl.multiple_of(tile * rows, rows), rows)
        x_tile = xs[here, :width]
        gate_w = w_ref[:, :hidden_width]
        up_w = w_ref[:, hidden_width : 2 * hidden_width]
        down_w = w_ref[:, 2 * hidden_width :]
        gate = mm(x_tile, gate_w)
        up = mm(x_tile, up_w)
        raw = mm(cs[here, :], down_w)
        packed = xs[here, width:].astype(fl)
        lane = lane_index(packed.shape)
        mine = (lane == expert) | (lane == expert + EXPERTS)
        gates = jnp.sum(jnp.where(mine, packed, 0.0), axis=1, keepdims=True)
        sigmoid = 1.0 / (1.0 + jnp.exp(-gate))
        silu = gate * sigmoid
        hidden = (silu * up).astype(bf).astype(fl)
        grad_gates = jnp.sum(hidden * raw, axis=1, keepdims=True)
        grad_hidden = raw * gates
        hid = (hidden * gates).astype(bf)
        grad_gate = (grad_hidden * up * sigmoid * (1.0 + gate * (1.0 - sigmoid))).astype(bf)
        grad_up = (grad_hidden * silu).astype(bf)
        hid_s[here, :] = hid
        gate_s[here, :] = grad_gate
        up_s[here, :] = grad_up
        out_acc[here, :] += mm(hid, down_w, NT)
        gn_acc[here, :width] += mm(grad_gate, gate_w, NT) + mm(grad_up, up_w, NT)
        gn_acc[here, width:] += jnp.where(lane == expert, grad_gates, 0.0)
        return carry

    lax.fori_loop(0, GROUP, tile_step, 0)
    for part, (left, right) in enumerate(((xt, gate_s), (xt, up_s), (ct, hid_s))):
        here = slice(part * hidden_width, (part + 1) * hidden_width)
        grad = mm(left[...], right[...]).astype(bf)
        if last:
            half, size = keep_ref.shape[:2]
            keep_ref[:, :, here] = grad[: width // 2].reshape(half, size, hidden_width)
            send_ref[:, :, here] = grad[width // 2 :].reshape(half, size, hidden_width)
        else:
            grad_ref[:, here] = grad

    @pl.when(step == pl.num_programs(0) - 1)
    def _():
        if last:
            gates_part = gn_acc[:, width:]
            high = gates_part.astype(bf).astype(fl)
            low = (gates_part - high).astype(bf).astype(fl)
            gn_acc[:, width:] = high + pltpu.roll(low, EXPERTS, 1)
        one = pltpu.make_async_copy(out_acc, out_hbm, sems.at[0])
        two = pltpu.make_async_copy(gn_acc, gn_hbm, sems.at[1])
        one.start()
        two.start()
        one.wait()
        two.wait()
        if not last:
            for copy in turned_out:
                copy.wait()


def experts_part(first, replica, replicas, blocks, cots, weights, chunk, previous):
    rows, width = cots[0].shape
    local = EXPERTS // GROUP // 2
    cols = weights.shape[1] // (2 * local)
    hidden_width = cols // 3
    total = GROUP * rows
    last = bool(previous)
    anywhere = pl.BlockSpec(memory_space=pl.ANY)
    out_shape = [
        jax.ShapeDtypeStruct((total, width), fl),
        jax.ShapeDtypeStruct((total, width + LANES), fl),
    ]
    if last:
        half = (replicas // 2, width // replicas)
        out_specs = [anywhere] * 2 + [pl.BlockSpec((*half, cols), lambda e, s: (0, 0, e))] * 2
        out_shape += [jax.ShapeDtypeStruct((*half, local * cols), bf)] * 2
    else:
        out_specs = [anywhere] * 2 + [pl.BlockSpec((width, cols), lambda e, s: (0, e))] + [anywhere] * 2
        out_shape += [jax.ShapeDtypeStruct((width, local * cols), bf)]
        out_shape += [jax.ShapeDtypeStruct((width, total), bf)] * 2
    back = 0 * replica
    for bit in range(replicas.bit_length() - 1):
        back = back * 2 + (replica // 2**bit) % 2
    return pl.pallas_call(
        functools.partial(experts_kernel, last),
        grid_spec=pltpu.PrefetchScalarGridSpec(
            num_scalar_prefetch=1,
            grid=(local,),
            in_specs=[anywhere] * 8
            + [pl.BlockSpec((width, cols), lambda e, s: (0, chunk * local + e))]
            + [anywhere] * len(previous),
            out_specs=out_specs,
            scratch_shapes=[
                pltpu.VMEM((total, width + LANES), bf),
                pltpu.VMEM((total, width), bf),
                pltpu.VMEM((width, total), bf),
                pltpu.VMEM((width, total), bf),
                pltpu.VMEM((total, width), fl),
                pltpu.VMEM((total, width + LANES), fl),
                pltpu.VMEM((total, hidden_width), bf),
                pltpu.VMEM((total, hidden_width), bf),
                pltpu.VMEM((total, hidden_width), bf),
                pltpu.SemaphoreType.DMA((10,)),
                pltpu.SemaphoreType.DMA((2, replicas)),
            ],
        ),
        out_shape=out_shape,
        compiler_params=params(62),
    )(jnp.stack([first + chunk * local, back]), *blocks, *cots, weights, *previous)


def middle_back_kernel(
    gn_ref, gates_ref, middle_ref, cot_ref, ctx_ref, out_w_ref, router_ref, gain_ref,
    gm_ref, gctx_ref, gw_ref, gain_grad_ref,
):
    width = cot_ref.shape[1]
    packed = gn_ref[:, width:]
    gates = gates_ref[...]
    grad_gates = packed + pltpu.roll(packed, LANES - EXPERTS, 1)
    inner = jnp.sum(gates * grad_gates, axis=1, keepdims=True)
    grad_logits = (gates * (grad_gates - inner)).astype(bf)
    middle = middle_ref[...]
    inverse = lax.rsqrt(jnp.mean(middle * middle, axis=1, keepdims=True) + NORM_EPS)
    gain = gain_ref[...]
    unit = middle * inverse
    normed = (unit * gain).astype(bf)
    grad_normed = gn_ref[:, :width] + mm(grad_logits, router_ref[...], NT)
    gw_ref[:, width:] = mm(normed, grad_logits, TN).astype(bf)
    gain_grad_ref[...] = jnp.sum(grad_normed * unit, axis=0, keepdims=True)
    scaled = grad_normed * gain
    mean = jnp.mean(scaled * middle, axis=1, keepdims=True)
    grad_middle = cot_ref[...].astype(fl) + inverse * scaled - unit * (inverse * inverse * mean)
    gm_ref[...] = grad_middle
    branch = grad_middle.astype(bf)
    gctx_ref[...] = mm(branch, out_w_ref[...], NT).astype(bf)
    gw_ref[:, :width] = mm(ctx_ref[...], branch, TN).astype(bf)


def middle_back(gn, gates, middle, cot, ctx, full, gain):
    rows, width = cot.shape
    here = lambda *shape: pl.BlockSpec(shape, lambda j: (0, 0))
    return pl.pallas_call(
        middle_back_kernel,
        grid=(1,),
        in_specs=[
            here(rows, width + LANES), here(rows, LANES), here(rows, width), here(rows, width), here(rows, width),
            pl.BlockSpec((width, width), lambda j: (0, 2)),
            pl.BlockSpec((width, LANES), lambda j: (0, 24)),
            here(1, width),
        ],
        out_specs=[here(rows, width), here(rows, width), here(width, width + LANES), here(1, width)],
        out_shape=[
            jax.ShapeDtypeStruct((rows, width), fl),
            jax.ShapeDtypeStruct((rows, width), bf),
            jax.ShapeDtypeStruct((width, width + LANES), bf),
            jax.ShapeDtypeStruct((1, width), fl),
        ],
        compiler_params=params(56),
    )(gn, gates, middle, cot, ctx, full, full, gain)


def finish_kernel(
    gq_ref, kept_ref, back_ref, normed_ref, x_ref, gm_ref, w_ref, gain_ref, cos_ref, sin_ref,
    token_ref, gw_ref, gain_grad_ref, gkv_ref,
):
    width = x_ref.shape[1]
    for part in range(4):
        first = part * 256
        both = kept_ref[:, first : first + 256] + back_ref[:, first : first + 256].astype(fl)
        piece = both[:, :LANES]
        gkv_ref[:, first : first + LANES] = (
            piece * cos_ref[...] - swap_halves(piece) * sin_ref[...]
        ).astype(bf)
        gkv_ref[:, first + LANES : first + 256] = both[:, LANES:].astype(bf)
    normed = normed_ref[...]
    gw_ref[:, :width] = mm(normed, gq_ref[...], TN).astype(bf)
    gw_ref[:, width:] = mm(normed, gkv_ref[...], TN).astype(bf)
    grad_normed = mm(gq_ref[...], w_ref[:, :width], NT) + mm(gkv_ref[...], w_ref[:, width:], NT)
    x = x_ref[...].astype(fl)
    inverse = lax.rsqrt(jnp.mean(x * x, axis=1, keepdims=True) + NORM_EPS)
    unit = x * inverse
    gain_grad_ref[...] = jnp.sum(grad_normed * unit, axis=0, keepdims=True)
    scaled = grad_normed * gain_ref[...]
    mean = jnp.mean(scaled * x, axis=1, keepdims=True)
    token_ref[...] = gm_ref[...] + inverse * scaled - unit * (inverse * inverse * mean)


def finish(grad_query, kept, back, normed, tokens, grad_middle, full, gain, cosine, sine):
    rows, width = tokens.shape
    here = lambda *shape: pl.BlockSpec(shape, lambda j: (0, 0))
    return pl.pallas_call(
        finish_kernel,
        grid=(1,),
        in_specs=[
            here(rows, width), here(rows, width), here(rows, width), here(rows, width), here(rows, width),
            here(rows, width), here(width, 2 * width), here(1, width), here(rows, LANES), here(rows, LANES),
        ],
        out_specs=[here(rows, width), here(width, 2 * width), here(1, width)],
        out_shape=[
            jax.ShapeDtypeStruct((rows, width), fl),
            jax.ShapeDtypeStruct((width, 2 * width), bf),
            jax.ShapeDtypeStruct((1, width), fl),
        ],
        scratch_shapes=[pltpu.VMEM((rows, width), bf)],
        compiler_params=params(60),
    )(grad_query, kept, back, normed, tokens, grad_middle, full, gain, cosine, sine)


def doubling_gather(part, index):
    cur = part[None]
    bits = lax.axis_size("fsdp") // 2
    while bits:
        other = swapped(cur, bits)
        pair = jnp.where(
            (index // bits) % 2 == 0, jnp.stack([cur, other], axis=1), jnp.stack([other, cur], axis=1)
        )
        cur = pair.reshape(2 * cur.shape[0], *cur.shape[1:])
        bits //= 2
    return cur.reshape(-1, part.shape[1])


def halving_sum(part, index, meanwhile):
    n = lax.axis_size("fsdp")
    cur = part.reshape(n, part.shape[0] // n, part.shape[1])
    bits = 1
    while bits < n:
        mine = (index // bits) % 2
        pairs = cur.reshape(cur.shape[0] // 2, 2, cur.shape[1], cur.shape[2])
        keep = lax.dynamic_index_in_dim(pairs, mine, 1, keepdims=False)
        send = lax.dynamic_index_in_dim(pairs, 1 - mine, 1, keepdims=False)
        cur = keep.astype(fl) + swapped(send.astype(bf), bits).astype(fl)
        bits *= 2
        if bits == 2 * GROUP:
            cur, meanwhile = lax.optimization_barrier((cur, meanwhile))
    return cur[0], meanwhile


def group_order(pieces, member):
    one, two = member % 2 == 1, member // 2 == 1
    a, b, c, d = pieces
    a, b, c, d = jnp.where(one, b, a), jnp.where(one, a, b), jnp.where(one, d, c), jnp.where(one, c, d)
    return jnp.where(two, c, a), jnp.where(two, d, b), jnp.where(two, a, c), jnp.where(two, b, d)


def per_device(
    tokens, positions, routes, attn_gain, w_query, w_key, w_value, w_out, mlp_gain, w_router,
    w_gate, w_up, w_down, cotangent,
):
    n = lax.axis_size("fsdp")
    index = lax.axis_index("fsdp")
    member = index % GROUP
    rows_dev, model_width = tokens.shape
    own_rows = w_query.shape[0]
    hidden_width = w_gate.shape[2]
    local = EXPERTS // GROUP
    across = [[r * GROUP + g for r in range(n // GROUP)] for g in range(GROUP)]

    key_value = jnp.concatenate(
        [w_key.reshape(own_rows, 4, LANES), w_value.reshape(own_rows, 4, LANES)], axis=2
    ).reshape(own_rows, model_width)
    small = jnp.concatenate(
        [w_router, attn_gain[:, None], mlp_gain[:, None], jnp.zeros((own_rows, LANES - EXPERTS - 2), bf)],
        axis=1,
    )
    packed = jnp.concatenate([w_query, key_value, w_out, small], axis=1)
    full = doubling_gather(packed, index)

    shard = jnp.concatenate([w_gate, w_up, w_down], axis=2).reshape(
        GROUP, local, own_rows, 3 * hidden_width
    )
    pieces = []
    for bits in range(GROUP):
        piece = lax.dynamic_index_in_dim(shard, member ^ bits, 0, keepdims=False)
        pieces.append(swapped(piece, bits) if bits else piece)
    mine = jnp.stack(group_order(pieces, member))
    mine = mine.transpose(0, 2, 1, 3).reshape(GROUP * own_rows, local * 3 * hidden_width)
    expert_w = lax.all_gather(mine, "fsdp", axis=0, tiled=True, axis_index_groups=across)

    cot_x = swapped(cotangent, 2)
    cots = (cotangent, cot_x, swapped(cotangent, 1), swapped(cot_x, 1))

    gain_one = full[:, 3088].astype(fl)[None, :]
    gain_two = full[:, 3089].astype(fl)[None, :]
    cosine, sine = rope_tables(positions)
    residual = tokens.astype(fl)
    inverse_one = lax.rsqrt(jnp.mean(residual * residual, axis=-1, keepdims=True) + NORM_EPS)
    normed_one = (residual * inverse_one * gain_one).astype(bf)
    own = project(key_value_kernel, normed_one, full, 4, cosine, sine)
    before = shifted(own, "fsdp", 1)
    queries = project(query_kernel, normed_one, full, 0, cosine, sine)
    start = (jnp.arange(rows_dev, dtype=jnp.int32) - positions)[:, None]
    context, context_low, log_total = attend(start, queries, before, own)

    context_low, *cots = lax.optimization_barrier((context_low, *cots))
    lanes = jnp.arange(LANES, dtype=jnp.int32)
    chosen = jnp.any(routes[:, :, None] == lanes[None, None, :], axis=1).astype(fl)
    middle, block, gates = middle_part(context_low, full, tokens, gain_two, chosen)

    block_x = swapped(block, 2)
    blocks = (block, block_x, swapped(block, 1), swapped(block_x, 1))
    first = (member * local).astype(jnp.int32)
    replica = (index // GROUP).astype(jnp.int32)
    one = (first, replica, n // GROUP, blocks, cots, expert_w)
    out_a, gn_a, grads_a, *turned = experts_part(*one, 0, ())
    owned_a = lax.psum_scatter(
        grads_a, "fsdp", scatter_dimension=0, tiled=True, axis_index_groups=across
    )
    out_parts, gn_parts, keep, send = experts_part(*one, 1, (out_a, gn_a, *turned))
    other = swapped(send, GROUP)

    def returned(parts):
        parts = parts.reshape(GROUP, rows_dev, parts.shape[1])
        other = swapped(parts[2:].astype(bf), 1).astype(fl)
        away = swapped((parts[1] + other[1]).astype(bf), 2).astype(fl)
        return parts[0] + other[0] + away

    gn = returned(gn_parts)
    grad_middle, grad_context, out_grad, gain_two_grad = middle_back(
        gn, gates, middle, cotangent, context_low, full, gain_two
    )
    activations = (middle + returned(out_parts)).astype(bf)
    grad_query, sent, kept = attend_back(
        start, queries, before, own, grad_context, context, log_total, cosine, sine
    )
    back = shifted(sent, "fsdp", -1)
    token_grad, proj_grad, gain_one_grad = finish(
        grad_query, kept, back, normed_one, tokens, grad_middle, full, gain_one, cosine, sine
    )
    proj_grad, other = lax.optimization_barrier((proj_grad, other))
    gains = jnp.concatenate(
        [gain_one_grad, gain_two_grad, jnp.zeros((LANES - 2, model_width), fl)], axis=0
    ).T.astype(bf)
    owned, owned_a = halving_sum(
        jnp.concatenate([proj_grad, out_grad, gains], axis=1), index, owned_a
    )
    owned_kv = owned[:, 1024:2048].reshape(own_rows, 4, 2, LANES)

    summed, bits = keep.astype(fl) + other.astype(fl), 2 * GROUP
    while bits < n:
        half = summed.shape[0] // 2
        summed = summed[:half] + swapped(summed[half:].astype(bf), bits).astype(fl)
        bits *= 2
    owned_b = summed[0].astype(bf)

    chunks = []
    for owned_part in (owned_a, owned_b):
        pieces = []
        for bits in range(GROUP):
            piece = lax.dynamic_slice_in_dim(owned_part, (member ^ bits) * own_rows, own_rows, 0)
            pieces.append(swapped(piece, bits) if bits else piece)
        chunks.append(jnp.stack(group_order(pieces, member)))
    experts = jnp.stack(chunks, axis=1)
    experts = experts.reshape(GROUP, 2, own_rows, local // 2, 3, hidden_width).transpose(4, 0, 1, 3, 2, 5)
    experts = experts.reshape(3, EXPERTS, own_rows, hidden_width).astype(fl)
    return (
        activations,
        token_grad,
        owned[:, 3200],
        owned[:, :1024],
        owned_kv[:, :, 0].reshape(own_rows, 512),
        owned_kv[:, :, 1].reshape(own_rows, 512),
        owned[:, 2048:3072],
        owned[:, 3201],
        owned[:, 3072 : 3072 + EXPERTS],
        experts[0],
        experts[1],
        experts[2],
    )


def solution(mesh):
    rows = P("fsdp", None)
    line = P("fsdp")
    stack = P(None, "fsdp", None)
    return jax.shard_map(
        per_device,
        mesh=mesh,
        in_specs=(rows, line, rows, line, rows, rows, rows, rows, line, rows, stack, stack, stack, rows),
        out_specs=(rows, rows, line, rows, rows, rows, rows, line, rows, stack, stack, stack),
        check_vma=False,
    )
```

```python
import jax
import jax.numpy as jnp
from jax import lax
from jax.experimental import pallas as pl
from jax.experimental.pallas import tpu as pltpu
from jax.sharding import PartitionSpec as P

HEADS = 16
KV_HEADS = 8
HEAD_DIM = 64
TOP = 8
EXPERTS = 16
GROUP = 4
LANES = 128
NORM_EPS = 1e-06
ROPE_THETA = 10000.0
MASKED = -1e30
MIB = 1024 * 1024

bf = jnp.bfloat16
fl = jnp.float32
SLOT = (0, 2, 1, 3)

NN = (((1,), (0,)), ((), ()))
NT = (((1,), (1,)), ((), ()))
TN = (((0,), (0,)), ((), ()))


def mm(a, b, dims=NN):
    return lax.dot_general(a, b, dims, preferred_element_type=fl)


def params(mib):
    return pltpu.CompilerParams(vmem_limit_bytes=mib * MIB)


def shifted(block, axis, distance):
    devices = range(lax.axis_size(axis))
    route = [(i - distance, i) for i in devices if i - distance in devices]
    return lax.ppermute(block, axis, route)


def swapped(block, bits):
    return lax.ppermute(block, "fsdp", [(i, i ^ bits) for i in range(lax.axis_size("fsdp"))])


def lane_index(shape):
    return lax.broadcasted_iota(jnp.int32, shape, len(shape) - 1)


def swap_halves(v):
    first = (lane_index(v.shape) & 32) == 0
    return jnp.where(first, pltpu.roll(v, LANES - 32, 1), pltpu.roll(v, 32, 1))


def rope_tables(positions):
    half_width = HEAD_DIM // 2
    frequency = ROPE_THETA ** (-(jnp.arange(half_width, dtype=fl) * 2.0) / HEAD_DIM)
    angle_rows = positions.astype(fl)[:, None] * frequency[None, :]
    cosine, sine = jnp.cos(angle_rows), jnp.sin(angle_rows)
    return (
        jnp.concatenate([cosine] * 4, axis=1),
        jnp.concatenate([-sine, sine, -sine, sine], axis=1),
    )


def query_kernel(x_ref, w_ref, cos_ref, sin_ref, out_ref):
    lin = mm(x_ref[...], w_ref[...])
    for part in range(2):
        piece = lin[:, part * LANES : (part + 1) * LANES]
        turned = piece * cos_ref[...] + swap_halves(piece) * sin_ref[...]
        out_ref[:, part * LANES : (part + 1) * LANES] = (turned.astype(bf) * HEAD_DIM**-0.5).astype(bf)


def key_value_kernel(x_ref, w_ref, cos_ref, sin_ref, out_ref):
    lin = mm(x_ref[...], w_ref[...])
    piece = lin[:, :LANES]
    out_ref[:, :LANES] = (piece * cos_ref[...] + swap_halves(piece) * sin_ref[...]).astype(bf)
    out_ref[:, LANES:] = lin[:, LANES:].astype(bf)


def project(kernel, normed, weights, first_block, cosine, sine):
    rows, width = normed.shape
    return pl.pallas_call(
        kernel,
        grid=(4,),
        in_specs=[
            pl.BlockSpec((rows, width), lambda j: (0, 0)),
            pl.BlockSpec((width, 256), lambda j: (0, first_block + j)),
            pl.BlockSpec((rows, LANES), lambda j: (0, 0)),
            pl.BlockSpec((rows, LANES), lambda j: (0, 0)),
        ],
        out_specs=pl.BlockSpec((rows, 256), lambda j: (0, j)),
        out_shape=jax.ShapeDtypeStruct((rows, 1024), bf),
        compiler_params=params(32),
    )(normed, weights, cosine, sine)


def fill_bias(start_ref, bias_ref):
    rows = bias_ref.shape[0]
    column = lax.broadcasted_iota(jnp.int32, bias_ref.shape, 1) - rows
    row = lax.broadcasted_iota(jnp.int32, bias_ref.shape, 0)
    seen = (column >= start_ref[...]) & (column <= row)
    bias_ref[...] = jnp.where(seen, 0.0, MASKED)


def attend_kernel(start_ref, q_ref, prev_ref, own_ref, ctx_ref, low_ref, lse_ref, bias_ref, kv_ref):
    rows = q_ref.shape[0]
    half = rows // 2

    @pl.when(pl.program_id(0) == 0)
    def _():
        fill_bias(start_ref, bias_ref)

    kv_ref[:rows, :] = prev_ref[...]
    kv_ref[rows:, :] = own_ref[...]
    for tile in range(2):
        queries = pl.ds(tile * half, half)
        keys = rows + (tile + 1) * half
        bias = bias_ref[queries, :keys]
        for head in range(4):
            lane = 64 * (head // 2)
            scores = mm(
                q_ref[queries, head * 64 : head * 64 + 64], kv_ref[:keys, lane : lane + 64], NT
            )
            scores = scores + bias
            row_max = jnp.max(scores, axis=1, keepdims=True)
            weights = jnp.exp(scores - row_max)
            total = jnp.sum(weights, axis=1, keepdims=True)
            probs = (weights * (1.0 / total)).astype(bf)
            context = mm(probs, kv_ref[:keys, LANES + lane : LANES + lane + 64])
            ctx_ref[queries, head * 64 : head * 64 + 64] = context
            low_ref[queries, head * 64 : head * 64 + 64] = context.astype(bf)
            lse_ref[0, queries, head : head + 1] = row_max + jnp.log(total)


def attend(start, queries, before, own):
    rows = queries.shape[0]
    wide = pl.BlockSpec((rows, 256), lambda j: (0, j))
    return pl.pallas_call(
        attend_kernel,
        grid=(4,),
        in_specs=[pl.BlockSpec((rows, 1), lambda j: (0, 0)), wide, wide, wide],
        out_specs=[wide, wide, pl.BlockSpec((1, rows, LANES), lambda j: (j, 0, 0))],
        out_shape=[
            jax.ShapeDtypeStruct((rows, 1024), fl),
            jax.ShapeDtypeStruct((rows, 1024), bf),
            jax.ShapeDtypeStruct((4, rows, LANES), fl),
        ],
        scratch_shapes=[pltpu.VMEM((rows, 2 * rows), fl), pltpu.VMEM((2 * rows, 256), bf)],
        compiler_params=params(40),
    )(start, queries, before, own)


def attend_back_kernel(
    start_ref, q_ref, prev_ref, own_ref, gctx_ref, ctx_ref, lse_ref, cos_ref, sin_ref,
    gq_ref, sent_ref, kept_ref, bias_ref, kv_ref, gkv_ref, gq_acc_ref,
):
    rows = q_ref.shape[0]
    half = rows // 2

    @pl.when(pl.program_id(0) == 0)
    def _():
        fill_bias(start_ref, bias_ref)

    kv_ref[:rows, :] = prev_ref[...]
    kv_ref[rows:, :] = own_ref[...]
    gkv_ref[...] = jnp.zeros_like(gkv_ref)
    for tile in range(2):
        queries = pl.ds(tile * half, half)
        keys = rows + (tile + 1) * half
        bias = bias_ref[queries, :keys]
        for head in range(4):
            lane = 64 * (head // 2)
            here = slice(head * 64, head * 64 + 64)
            query = q_ref[queries, here]
            grad = gctx_ref[queries, here]
            key = kv_ref[:keys, lane : lane + 64]
            value = kv_ref[:keys, LANES + lane : LANES + lane + 64]
            inner = jnp.sum(grad.astype(fl) * ctx_ref[queries, here], axis=1, keepdims=True)
            scores = mm(query, key, NT) + bias
            probs = jnp.exp(scores - lse_ref[0, queries, head : head + 1])
            grad_probs = mm(grad, value, NT)
            grad_scores = (probs * (grad_probs - inner)).astype(bf)
            gq_acc_ref[queries, here] = mm(grad_scores, key) * HEAD_DIM**-0.5
            gkv_ref[:keys, lane : lane + 64] += mm(grad_scores, query, TN)
            gkv_ref[:keys, LANES + lane : LANES + lane + 64] += mm(probs.astype(bf), grad, TN)
    for part in range(2):
        here = slice(part * LANES, part * LANES + LANES)
        piece = gq_acc_ref[:, here]
        gq_ref[:, here] = (piece * cos_ref[...] - swap_halves(piece) * sin_ref[...]).astype(bf)
    sent_ref[...] = gkv_ref[:rows, :].astype(bf)
    kept_ref[...] = gkv_ref[rows:, :]


def attend_back(start, queries, before, own, grad_context, context, log_total, cosine, sine):
    rows = queries.shape[0]
    wide = pl.BlockSpec((rows, 256), lambda j: (0, j))
    table = pl.BlockSpec((rows, LANES), lambda j: (0, 0))
    return pl.pallas_call(
        attend_back_kernel,
        grid=(4,),
        in_specs=[
            pl.BlockSpec((rows, 1), lambda j: (0, 0)), wide, wide, wide, wide, wide,
            pl.BlockSpec((1, rows, LANES), lambda j: (j, 0, 0)), table, table,
        ],
        out_specs=[wide, wide, wide],
        out_shape=[
            jax.ShapeDtypeStruct((rows, 1024), bf),
            jax.ShapeDtypeStruct((rows, 1024), bf),
            jax.ShapeDtypeStruct((rows, 1024), fl),
        ],
        scratch_shapes=[
            pltpu.VMEM((rows, 2 * rows), fl),
            pltpu.VMEM((2 * rows, 256), bf),
            pltpu.VMEM((2 * rows, 256), fl),
            pltpu.VMEM((rows, 256), fl),
        ],
        compiler_params=params(48),
    )(start, queries, before, own, grad_context, context, log_total, cosine, sine)


def middle_kernel(ctx_ref, out_w_ref, router_ref, x_ref, gain_ref, chosen_ref, middle_ref, block_ref, gates_ref):
    width = x_ref.shape[1]
    middle = x_ref[...].astype(fl) + mm(ctx_ref[...], out_w_ref[...])
    inverse = lax.rsqrt(jnp.mean(middle * middle, axis=1, keepdims=True) + NORM_EPS)
    normed = (middle * inverse * gain_ref[...]).astype(bf)
    logits = mm(normed, router_ref[...])
    chosen = chosen_ref[...] > 0.0
    logits = jnp.where(chosen, logits, MASKED)
    weights = jnp.exp(logits - jnp.max(logits, axis=1, keepdims=True))
    weights = jnp.where(chosen, weights, 0.0)
    gates = weights / jnp.sum(weights, axis=1, keepdims=True)
    high = gates.astype(bf).astype(fl)
    middle_ref[...] = middle
    gates_ref[...] = gates
    block_ref[:, :width] = normed
    block_ref[:, width:] = (high + pltpu.roll(gates - high, EXPERTS, 1)).astype(bf)


def middle_part(ctx, full, tokens, gain, chosen):
    rows, width = tokens.shape
    return pl.pallas_call(
        middle_kernel,
        grid=(1,),
        in_specs=[
            pl.BlockSpec((rows, width), lambda j: (0, 0)),
            pl.BlockSpec((width, width), lambda j: (0, 2)),
            pl.BlockSpec((width, LANES), lambda j: (0, 24)),
            pl.BlockSpec((rows, width), lambda j: (0, 0)),
            pl.BlockSpec((1, width), lambda j: (0, 0)),
            pl.BlockSpec((rows, LANES), lambda j: (0, 0)),
        ],
        out_specs=[
            pl.BlockSpec((rows, width), lambda j: (0, 0)),
            pl.BlockSpec((rows, width + LANES), lambda j: (0, 0)),
            pl.BlockSpec((rows, LANES), lambda j: (0, 0)),
        ],
        out_shape=[
            jax.ShapeDtypeStruct((rows, width), fl),
            jax.ShapeDtypeStruct((rows, width + LANES), bf),
            jax.ShapeDtypeStruct((rows, LANES), fl),
        ],
        compiler_params=params(48),
    )(ctx, full, full, tokens, gain, chosen)


def experts_kernel(
    first_ref, x0, x1, x2, x3, c0, c1, c2, c3, w_ref, out_hbm, gn_hbm, grad_ref,
    xs, cs, xt, ct, ws, out_acc, gn_acc, hid_s, gate_s, up_s, sems, w_sems,
):
    step = pl.program_id(0)
    steps = pl.num_programs(0)
    rows = c0.shape[0]
    width = c0.shape[1]
    cols = ws.shape[2]
    hidden_width = cols // 3
    expert = first_ref[0] + step
    order = snake(w_sems.shape[1])
    size = width // len(order)
    held = lax.rem(step, 2)

    def weight_copies(which, slot):
        columns = pl.ds(pl.multiple_of(which * cols, cols), cols)
        return [
            pltpu.make_async_copy(
                w_ref.at[pl.ds(place * size, size), columns],
                ws.at[slot, pl.ds(replica * size, size), :],
                w_sems.at[slot, place],
            )
            for place, replica in enumerate(order)
        ]

    @pl.when(step == 0)
    def _():
        copies = []
        for slot, (x, c) in enumerate(((x0, c0), (x1, c1), (x2, c2), (x3, c3))):
            here = pl.ds(slot * rows, rows)
            copies.append(pltpu.make_async_copy(x, xs.at[here], sems.at[2 * slot]))
            copies.append(pltpu.make_async_copy(c, cs.at[here], sems.at[2 * slot + 1]))
        for copy in copies + weight_copies(0, 0) + weight_copies(1, 1):
            copy.start()
        for copy in copies:
            copy.wait()
        out_acc[...] = jnp.zeros_like(out_acc)
        gn_acc[...] = jnp.zeros_like(gn_acc)
        for slot in range(GROUP):
            here = slice(slot * rows, (slot + 1) * rows)
            for source, target in ((xs, xt), (cs, ct)):
                turned = source[here, :width].T
                for place, replica in enumerate(order):
                    target[place * size : (place + 1) * size, here] = turned[
                        replica * size : (replica + 1) * size
                    ]

    for copy in weight_copies(step, held):
        copy.wait()

    def tile_step(tile, carry):
        here = pl.ds(pl.multiple_of(tile * rows, rows), rows)
        x_tile = xs[here, :width]
        gate_w = ws[held, :, :hidden_width]
        up_w = ws[held, :, hidden_width : 2 * hidden_width]
        down_w = ws[held, :, 2 * hidden_width :]
        gate = mm(x_tile, gate_w)
        up = mm(x_tile, up_w)
        raw = mm(cs[here, :], down_w)
        packed = xs[here, width:].astype(fl)
        lane = lane_index(packed.shape)
        mine = (lane == expert) | (lane == expert + EXPERTS)
        gates = jnp.sum(jnp.where(mine, packed, 0.0), axis=1, keepdims=True)
        sigmoid = 1.0 / (1.0 + jnp.exp(-gate))
        silu = gate * sigmoid
        hidden = (silu * up).astype(bf).astype(fl)
        grad_gates = jnp.sum(hidden * raw, axis=1, keepdims=True)
        grad_hidden = raw * gates
        hid = (hidden * gates).astype(bf)
        grad_gate = (grad_hidden * up * sigmoid * (1.0 + gate * (1.0 - sigmoid))).astype(bf)
        grad_up = (grad_hidden * silu).astype(bf)
        hid_s[here, :] = hid
        gate_s[here, :] = grad_gate
        up_s[here, :] = grad_up
        out_acc[here, :] += mm(hid, down_w, NT)
        gn_acc[here, :width] += mm(grad_gate, gate_w, NT) + mm(grad_up, up_w, NT)
        gn_acc[here, width:] += jnp.where(lane == expert, grad_gates, 0.0)
        return carry

    lax.fori_loop(0, GROUP, tile_step, 0)

    @pl.when(step + 2 < steps)
    def _():
        for copy in weight_copies(step + 2, held):
            copy.start()

    grad_ref[:, :hidden_width] = mm(xt[...], gate_s[...]).astype(bf)
    grad_ref[:, hidden_width : 2 * hidden_width] = mm(xt[...], up_s[...]).astype(bf)
    grad_ref[:, 2 * hidden_width :] = mm(ct[...], hid_s[...]).astype(bf)

    @pl.when(step == pl.num_programs(0) - 1)
    def _():
        gates_part = gn_acc[:, width:]
        high = gates_part.astype(bf).astype(fl)
        low = (gates_part - high).astype(bf).astype(fl)
        gn_acc[:, width:] = high + pltpu.roll(low, EXPERTS, 1)
        one = pltpu.make_async_copy(out_acc, out_hbm, sems.at[0])
        two = pltpu.make_async_copy(gn_acc, gn_hbm, sems.at[1])
        one.start()
        two.start()
        one.wait()
        two.wait()


def experts_part(first, replicas, blocks, cots, weights):
    rows, width = cots[0].shape
    local = EXPERTS // GROUP
    cols = weights.shape[1] // local
    hidden_width = cols // 3
    total = GROUP * rows
    anywhere = pl.BlockSpec(memory_space=pl.ANY)
    return pl.pallas_call(
        experts_kernel,
        grid_spec=pltpu.PrefetchScalarGridSpec(
            num_scalar_prefetch=1,
            grid=(local,),
            in_specs=[anywhere] * 9,
            out_specs=[anywhere, anywhere, pl.BlockSpec((width, cols), lambda e, s: (0, e))],
            scratch_shapes=[
                pltpu.VMEM((total, width + LANES), bf),
                pltpu.VMEM((total, width), bf),
                pltpu.VMEM((width, total), bf),
                pltpu.VMEM((width, total), bf),
                pltpu.VMEM((2, width, cols), bf),
                pltpu.VMEM((total, width), fl),
                pltpu.VMEM((total, width + LANES), fl),
                pltpu.VMEM((total, hidden_width), bf),
                pltpu.VMEM((total, hidden_width), bf),
                pltpu.VMEM((total, hidden_width), bf),
                pltpu.SemaphoreType.DMA((8,)),
                pltpu.SemaphoreType.DMA((2, replicas)),
            ],
        ),
        out_shape=[
            jax.ShapeDtypeStruct((total, width), fl),
            jax.ShapeDtypeStruct((total, width + LANES), fl),
            jax.ShapeDtypeStruct((width, local * cols), bf),
        ],
        compiler_params=params(62),
    )(first, *blocks, *cots, weights)


def middle_back_kernel(
    gn_ref, gates_ref, middle_ref, cot_ref, ctx_ref, out_w_ref, router_ref, gain_ref,
    gm_ref, gctx_ref, gw_ref, gain_grad_ref,
):
    width = cot_ref.shape[1]
    packed = gn_ref[:, width:]
    gates = gates_ref[...]
    grad_gates = packed + pltpu.roll(packed, LANES - EXPERTS, 1)
    inner = jnp.sum(gates * grad_gates, axis=1, keepdims=True)
    grad_logits = (gates * (grad_gates - inner)).astype(bf)
    middle = middle_ref[...]
    inverse = lax.rsqrt(jnp.mean(middle * middle, axis=1, keepdims=True) + NORM_EPS)
    gain = gain_ref[...]
    unit = middle * inverse
    normed = (unit * gain).astype(bf)
    grad_normed = gn_ref[:, :width] + mm(grad_logits, router_ref[...], NT)
    gw_ref[:, width:] = mm(normed, grad_logits, TN).astype(bf)
    gain_grad_ref[...] = jnp.sum(grad_normed * unit, axis=0, keepdims=True)
    scaled = grad_normed * gain
    mean = jnp.mean(scaled * middle, axis=1, keepdims=True)
    grad_middle = cot_ref[...].astype(fl) + inverse * scaled - unit * (inverse * inverse * mean)
    gm_ref[...] = grad_middle
    branch = grad_middle.astype(bf)
    gctx_ref[...] = mm(branch, out_w_ref[...], NT).astype(bf)
    gw_ref[:, :width] = mm(ctx_ref[...], branch, TN).astype(bf)


def middle_back(gn, gates, middle, cot, ctx, full, gain):
    rows, width = cot.shape
    here = lambda *shape: pl.BlockSpec(shape, lambda j: (0, 0))
    return pl.pallas_call(
        middle_back_kernel,
        grid=(1,),
        in_specs=[
            here(rows, width + LANES), here(rows, LANES), here(rows, width), here(rows, width), here(rows, width),
            pl.BlockSpec((width, width), lambda j: (0, 2)),
            pl.BlockSpec((width, LANES), lambda j: (0, 24)),
            here(1, width),
        ],
        out_specs=[here(rows, width), here(rows, width), here(width, width + LANES), here(1, width)],
        out_shape=[
            jax.ShapeDtypeStruct((rows, width), fl),
            jax.ShapeDtypeStruct((rows, width), bf),
            jax.ShapeDtypeStruct((width, width + LANES), bf),
            jax.ShapeDtypeStruct((1, width), fl),
        ],
        compiler_params=params(56),
    )(gn, gates, middle, cot, ctx, full, full, gain)


def finish_kernel(
    gq_ref, kept_ref, back_ref, normed_ref, x_ref, gm_ref, w_ref, gain_ref, cos_ref, sin_ref,
    token_ref, gw_ref, gain_grad_ref, gkv_ref,
):
    width = x_ref.shape[1]
    for part in range(4):
        first = part * 256
        both = kept_ref[:, first : first + 256] + back_ref[:, first : first + 256].astype(fl)
        piece = both[:, :LANES]
        gkv_ref[:, first : first + LANES] = (
            piece * cos_ref[...] - swap_halves(piece) * sin_ref[...]
        ).astype(bf)
        gkv_ref[:, first + LANES : first + 256] = both[:, LANES:].astype(bf)
    normed = normed_ref[...]
    gw_ref[:, :width] = mm(normed, gq_ref[...], TN).astype(bf)
    gw_ref[:, width:] = mm(normed, gkv_ref[...], TN).astype(bf)
    grad_normed = mm(gq_ref[...], w_ref[:, :width], NT) + mm(gkv_ref[...], w_ref[:, width:], NT)
    x = x_ref[...].astype(fl)
    inverse = lax.rsqrt(jnp.mean(x * x, axis=1, keepdims=True) + NORM_EPS)
    unit = x * inverse
    gain_grad_ref[...] = jnp.sum(grad_normed * unit, axis=0, keepdims=True)
    scaled = grad_normed * gain_ref[...]
    mean = jnp.mean(scaled * x, axis=1, keepdims=True)
    token_ref[...] = gm_ref[...] + inverse * scaled - unit * (inverse * inverse * mean)


def finish(grad_query, kept, back, normed, tokens, grad_middle, full, gain, cosine, sine):
    rows, width = tokens.shape
    here = lambda *shape: pl.BlockSpec(shape, lambda j: (0, 0))
    return pl.pallas_call(
        finish_kernel,
        grid=(1,),
        in_specs=[
            here(rows, width), here(rows, width), here(rows, width), here(rows, width), here(rows, width),
            here(rows, width), here(width, 2 * width), here(1, width), here(rows, LANES), here(rows, LANES),
        ],
        out_specs=[here(rows, width), here(width, 2 * width), here(1, width)],
        out_shape=[
            jax.ShapeDtypeStruct((rows, width), fl),
            jax.ShapeDtypeStruct((width, 2 * width), bf),
            jax.ShapeDtypeStruct((1, width), fl),
        ],
        scratch_shapes=[pltpu.VMEM((rows, width), bf)],
        compiler_params=params(60),
    )(grad_query, kept, back, normed, tokens, grad_middle, full, gain, cosine, sine)


def doubling_gather(part, index, bits, last):
    cur = part
    while bits >= last:
        other = swapped(cur, bits)
        pair = jnp.where(
            (index // bits) % 2 == 0, jnp.stack([cur, other], axis=1), jnp.stack([other, cur], axis=1)
        )
        cur = pair.reshape(2 * cur.shape[0], *cur.shape[1:])
        bits //= 2
    return cur


def halving_sum(part, index, meanwhile):
    n = lax.axis_size("fsdp")
    cur = part.reshape(n, part.shape[0] // n, part.shape[1])
    bits = 1
    while bits < n:
        mine = (index // bits) % 2
        pairs = cur.reshape(cur.shape[0] // 2, 2, cur.shape[1], cur.shape[2])
        keep = lax.dynamic_index_in_dim(pairs, mine, 1, keepdims=False)
        send = lax.dynamic_index_in_dim(pairs, 1 - mine, 1, keepdims=False)
        cur = keep.astype(fl) + swapped(send.astype(bf), bits).astype(fl)
        bits *= 2
        if bits == GROUP:
            cur, meanwhile = lax.optimization_barrier((cur, meanwhile))
    return cur[0], meanwhile


def snake(replicas):
    return [*range(0, replicas, 2), *range(replicas - 1, 0, -2)]


def group_order(pieces, member):
    one, two = member % 2 == 1, member // 2 == 1
    a, b, c, d = pieces
    a, b, c, d = jnp.where(one, b, a), jnp.where(one, a, b), jnp.where(one, d, c), jnp.where(one, c, d)
    return jnp.where(two, c, a), jnp.where(two, d, b), jnp.where(two, a, c), jnp.where(two, b, d)


def per_device(
    tokens, positions, routes, attn_gain, w_query, w_key, w_value, w_out, mlp_gain, w_router,
    w_gate, w_up, w_down, cotangent,
):
    n = lax.axis_size("fsdp")
    index = lax.axis_index("fsdp")
    member = index % GROUP
    rows_dev, model_width = tokens.shape
    own_rows = w_query.shape[0]
    hidden_width = w_gate.shape[2]
    local = EXPERTS // GROUP
    across = [[r * GROUP + g for r in snake(n // GROUP)] for g in range(GROUP)]

    key_value = jnp.concatenate(
        [w_key.reshape(own_rows, 4, LANES), w_value.reshape(own_rows, 4, LANES)], axis=2
    ).reshape(own_rows, model_width)
    small = jnp.concatenate(
        [w_router, attn_gain[:, None], mlp_gain[:, None], jnp.zeros((own_rows, LANES - EXPERTS - 2), bf)],
        axis=1,
    )
    packed = jnp.concatenate([w_query, key_value, w_out, small], axis=1)
    far = doubling_gather(packed[None], index, n // 2, 2 * GROUP)

    shard = jnp.concatenate([w_gate, w_up, w_down], axis=2).reshape(
        GROUP, local, own_rows, 3 * hidden_width
    )
    pieces = []
    for bits in range(GROUP):
        piece = lax.dynamic_index_in_dim(shard, member ^ bits, 0, keepdims=False)
        pieces.append(swapped(piece, bits) if bits else piece)
    mine = jnp.stack(group_order(pieces, member))
    mine = mine.transpose(0, 2, 1, 3).reshape(GROUP * own_rows, local * 3 * hidden_width)
    mine, far = lax.optimization_barrier((mine, far))
    full = doubling_gather(far, index, GROUP, 1).reshape(n * own_rows, packed.shape[1])
    expert_w = lax.all_gather(mine, "fsdp", axis=0, tiled=True, axis_index_groups=across)

    cot_x = swapped(cotangent, 2)
    cots = (cotangent, cot_x, swapped(cotangent, 1), swapped(cot_x, 1))

    gain_one = full[:, 3088].astype(fl)[None, :]
    gain_two = full[:, 3089].astype(fl)[None, :]
    cosine, sine = rope_tables(positions)
    residual = tokens.astype(fl)
    inverse_one = lax.rsqrt(jnp.mean(residual * residual, axis=-1, keepdims=True) + NORM_EPS)
    normed_one = (residual * inverse_one * gain_one).astype(bf)
    own = project(key_value_kernel, normed_one, full, 4, cosine, sine)
    before = shifted(own, "fsdp", 1)
    queries = project(query_kernel, normed_one, full, 0, cosine, sine)
    start = (jnp.arange(rows_dev, dtype=jnp.int32) - positions)[:, None]
    context, context_low, log_total = attend(start, queries, before, own)

    context_low, *cots = lax.optimization_barrier((context_low, *cots))
    lanes = jnp.arange(LANES, dtype=jnp.int32)
    chosen = jnp.any(routes[:, :, None] == lanes[None, None, :], axis=1).astype(fl)
    middle, block, gates = middle_part(context_low, full, tokens, gain_two, chosen)

    block_x = swapped(block, 2)
    blocks = (block, block_x, swapped(block, 1), swapped(block_x, 1))
    first = (member * local).astype(jnp.int32).reshape(1)
    out_parts, gn_parts, expert_grads = experts_part(first, n // GROUP, blocks, cots, expert_w)

    owned_experts = lax.psum_scatter(
        expert_grads, "fsdp", scatter_dimension=0, tiled=True, axis_index_groups=across
    )

    def returned(parts):
        parts = parts.reshape(GROUP, rows_dev, parts.shape[1])
        other = swapped(parts[2:].astype(bf), 1).astype(fl)
        away = swapped((parts[1] + other[1]).astype(bf), 2).astype(fl)
        return parts[0] + other[0] + away

    gn = returned(gn_parts)
    grad_middle, grad_context, out_grad, gain_two_grad = middle_back(
        gn, gates, middle, cotangent, context_low, full, gain_two
    )
    activations = (middle + returned(out_parts)).astype(bf)
    grad_query, sent, kept = attend_back(
        start, queries, before, own, grad_context, context, log_total, cosine, sine
    )
    back = shifted(sent, "fsdp", -1)
    token_grad, proj_grad, gain_one_grad = finish(
        grad_query, kept, back, normed_one, tokens, grad_middle, full, gain_one, cosine, sine
    )
    gains = jnp.concatenate(
        [gain_one_grad, gain_two_grad, jnp.zeros((LANES - 2, model_width), fl)], axis=0
    ).T.astype(bf)
    owned, owned_experts = halving_sum(
        jnp.concatenate([proj_grad, out_grad, gains], axis=1), index, owned_experts
    )
    owned_kv = owned[:, 1024:2048].reshape(own_rows, 4, 2, LANES)

    pieces = []
    for bits in range(GROUP):
        piece = lax.dynamic_slice_in_dim(owned_experts, (member ^ bits) * own_rows, own_rows, 0)
        pieces.append(swapped(piece, bits) if bits else piece)
    experts = jnp.stack(group_order(pieces, member)).reshape(GROUP, own_rows, local, 3, hidden_width)
    experts = experts.transpose(3, 0, 2, 1, 4).reshape(3, EXPERTS, own_rows, hidden_width).astype(fl)
    return (
        activations,
        token_grad,
        owned[:, 3200],
        owned[:, :1024],
        owned_kv[:, :, 0].reshape(own_rows, 512),
        owned_kv[:, :, 1].reshape(own_rows, 512),
        owned[:, 2048:3072],
        owned[:, 3201],
        owned[:, 3072 : 3072 + EXPERTS],
        experts[0],
        experts[1],
        experts[2],
    )


def solution(mesh):
    rows = P("fsdp", None)
    line = P("fsdp")
    stack = P(None, "fsdp", None)
    return jax.shard_map(
        per_device,
        mesh=mesh,
        in_specs=(rows, line, rows, line, rows, rows, rows, rows, line, rows, stack, stack, stack, rows),
        out_specs=(rows, rows, line, rows, rows, rows, rows, line, rows, stack, stack, stack),
        check_vma=False,
    )
```

```python
import jax
import jax.numpy as jnp
from jax import lax
from jax.experimental import pallas as pl
from jax.experimental.pallas import tpu as pltpu
from jax.sharding import PartitionSpec as P

HEADS = 16
KV_HEADS = 8
HEAD_DIM = 64
TOP = 8
EXPERTS = 16
GROUP = 4
LANES = 128
NORM_EPS = 1e-06
ROPE_THETA = 10000.0
MASKED = -1e30
MIB = 1024 * 1024

bf = jnp.bfloat16
fl = jnp.float32
SLOT = (0, 2, 1, 3)

NN = (((1,), (0,)), ((), ()))
NT = (((1,), (1,)), ((), ()))
TN = (((0,), (0,)), ((), ()))


def mm(a, b, dims=NN):
    return lax.dot_general(a, b, dims, preferred_element_type=fl)


def params(mib):
    return pltpu.CompilerParams(vmem_limit_bytes=mib * MIB)


def shifted(block, axis, distance):
    devices = range(lax.axis_size(axis))
    route = [(i - distance, i) for i in devices if i - distance in devices]
    return lax.ppermute(block, axis, route)


def swapped(block, bits):
    return lax.ppermute(block, "fsdp", [(i, i ^ bits) for i in range(lax.axis_size("fsdp"))])


def lane_index(shape):
    return lax.broadcasted_iota(jnp.int32, shape, len(shape) - 1)


def swap_halves(v):
    first = (lane_index(v.shape) & 32) == 0
    return jnp.where(first, pltpu.roll(v, LANES - 32, 1), pltpu.roll(v, 32, 1))


def rope_tables(positions):
    half_width = HEAD_DIM // 2
    frequency = ROPE_THETA ** (-(jnp.arange(half_width, dtype=fl) * 2.0) / HEAD_DIM)
    angle_rows = positions.astype(fl)[:, None] * frequency[None, :]
    cosine, sine = jnp.cos(angle_rows), jnp.sin(angle_rows)
    return (
        jnp.concatenate([cosine] * 4, axis=1),
        jnp.concatenate([-sine, sine, -sine, sine], axis=1),
    )


def query_kernel(x_ref, w_ref, cos_ref, sin_ref, out_ref):
    lin = mm(x_ref[...], w_ref[...])
    for part in range(2):
        piece = lin[:, part * LANES : (part + 1) * LANES]
        turned = piece * cos_ref[...] + swap_halves(piece) * sin_ref[...]
        out_ref[:, part * LANES : (part + 1) * LANES] = (turned.astype(bf) * HEAD_DIM**-0.5).astype(bf)


def key_value_kernel(x_ref, w_ref, cos_ref, sin_ref, out_ref):
    lin = mm(x_ref[...], w_ref[...])
    piece = lin[:, :LANES]
    out_ref[:, :LANES] = (piece * cos_ref[...] + swap_halves(piece) * sin_ref[...]).astype(bf)
    out_ref[:, LANES:] = lin[:, LANES:].astype(bf)


def project(kernel, normed, weights, first_block, cosine, sine):
    rows, width = normed.shape
    return pl.pallas_call(
        kernel,
        grid=(4,),
        in_specs=[
            pl.BlockSpec((rows, width), lambda j: (0, 0)),
            pl.BlockSpec((width, 256), lambda j: (0, first_block + j)),
            pl.BlockSpec((rows, LANES), lambda j: (0, 0)),
            pl.BlockSpec((rows, LANES), lambda j: (0, 0)),
        ],
        out_specs=pl.BlockSpec((rows, 256), lambda j: (0, j)),
        out_shape=jax.ShapeDtypeStruct((rows, 1024), bf),
        compiler_params=params(32),
    )(normed, weights, cosine, sine)


def fill_bias(start_ref, bias_ref):
    rows = bias_ref.shape[0]
    column = lax.broadcasted_iota(jnp.int32, bias_ref.shape, 1) - rows
    row = lax.broadcasted_iota(jnp.int32, bias_ref.shape, 0)
    seen = (column >= start_ref[...]) & (column <= row)
    bias_ref[...] = jnp.where(seen, 0.0, MASKED)


def attend_kernel(start_ref, q_ref, prev_ref, own_ref, ctx_ref, low_ref, lse_ref, bias_ref, kv_ref):
    rows = q_ref.shape[0]
    half = rows // 2

    @pl.when(pl.program_id(0) == 0)
    def _():
        fill_bias(start_ref, bias_ref)

    kv_ref[:rows, :] = prev_ref[...]
    kv_ref[rows:, :] = own_ref[...]
    for tile in range(2):
        queries = pl.ds(tile * half, half)
        keys = rows + (tile + 1) * half
        bias = bias_ref[queries, :keys]
        for head in range(4):
            lane = 64 * (head // 2)
            scores = mm(
                q_ref[queries, head * 64 : head * 64 + 64], kv_ref[:keys, lane : lane + 64], NT
            )
            scores = scores + bias
            row_max = jnp.max(scores, axis=1, keepdims=True)
            weights = jnp.exp(scores - row_max)
            total = jnp.sum(weights, axis=1, keepdims=True)
            probs = (weights * (1.0 / total)).astype(bf)
            context = mm(probs, kv_ref[:keys, LANES + lane : LANES + lane + 64])
            ctx_ref[queries, head * 64 : head * 64 + 64] = context
            low_ref[queries, head * 64 : head * 64 + 64] = context.astype(bf)
            lse_ref[0, queries, head : head + 1] = row_max + jnp.log(total)


def attend(start, queries, before, own):
    rows = queries.shape[0]
    wide = pl.BlockSpec((rows, 256), lambda j: (0, j))
    return pl.pallas_call(
        attend_kernel,
        grid=(4,),
        in_specs=[pl.BlockSpec((rows, 1), lambda j: (0, 0)), wide, wide, wide],
        out_specs=[wide, wide, pl.BlockSpec((1, rows, LANES), lambda j: (j, 0, 0))],
        out_shape=[
            jax.ShapeDtypeStruct((rows, 1024), fl),
            jax.ShapeDtypeStruct((rows, 1024), bf),
            jax.ShapeDtypeStruct((4, rows, LANES), fl),
        ],
        scratch_shapes=[pltpu.VMEM((rows, 2 * rows), fl), pltpu.VMEM((2 * rows, 256), bf)],
        compiler_params=params(40),
    )(start, queries, before, own)


def attend_back_kernel(
    start_ref, q_ref, prev_ref, own_ref, gctx_ref, ctx_ref, lse_ref, cos_ref, sin_ref,
    gq_ref, sent_ref, kept_ref, bias_ref, kv_ref, gkv_ref, gq_acc_ref,
):
    rows = q_ref.shape[0]
    half = rows // 2

    @pl.when(pl.program_id(0) == 0)
    def _():
        fill_bias(start_ref, bias_ref)

    kv_ref[:rows, :] = prev_ref[...]
    kv_ref[rows:, :] = own_ref[...]
    gkv_ref[...] = jnp.zeros_like(gkv_ref)
    for tile in range(2):
        queries = pl.ds(tile * half, half)
        keys = rows + (tile + 1) * half
        bias = bias_ref[queries, :keys]
        for head in range(4):
            lane = 64 * (head // 2)
            here = slice(head * 64, head * 64 + 64)
            query = q_ref[queries, here]
            grad = gctx_ref[queries, here]
            key = kv_ref[:keys, lane : lane + 64]
            value = kv_ref[:keys, LANES + lane : LANES + lane + 64]
            inner = jnp.sum(grad.astype(fl) * ctx_ref[queries, here], axis=1, keepdims=True)
            scores = mm(query, key, NT) + bias
            probs = jnp.exp(scores - lse_ref[0, queries, head : head + 1])
            grad_probs = mm(grad, value, NT)
            grad_scores = (probs * (grad_probs - inner)).astype(bf)
            gq_acc_ref[queries, here] = mm(grad_scores, key) * HEAD_DIM**-0.5
            gkv_ref[:keys, lane : lane + 64] += mm(grad_scores, query, TN)
            gkv_ref[:keys, LANES + lane : LANES + lane + 64] += mm(probs.astype(bf), grad, TN)
    for part in range(2):
        here = slice(part * LANES, part * LANES + LANES)
        piece = gq_acc_ref[:, here]
        gq_ref[:, here] = (piece * cos_ref[...] - swap_halves(piece) * sin_ref[...]).astype(bf)
    sent_ref[...] = gkv_ref[:rows, :].astype(bf)
    kept_ref[...] = gkv_ref[rows:, :]


def attend_back(start, queries, before, own, grad_context, context, log_total, cosine, sine):
    rows = queries.shape[0]
    wide = pl.BlockSpec((rows, 256), lambda j: (0, j))
    table = pl.BlockSpec((rows, LANES), lambda j: (0, 0))
    return pl.pallas_call(
        attend_back_kernel,
        grid=(4,),
        in_specs=[
            pl.BlockSpec((rows, 1), lambda j: (0, 0)), wide, wide, wide, wide, wide,
            pl.BlockSpec((1, rows, LANES), lambda j: (j, 0, 0)), table, table,
        ],
        out_specs=[wide, wide, wide],
        out_shape=[
            jax.ShapeDtypeStruct((rows, 1024), bf),
            jax.ShapeDtypeStruct((rows, 1024), bf),
            jax.ShapeDtypeStruct((rows, 1024), fl),
        ],
        scratch_shapes=[
            pltpu.VMEM((rows, 2 * rows), fl),
            pltpu.VMEM((2 * rows, 256), bf),
            pltpu.VMEM((2 * rows, 256), fl),
            pltpu.VMEM((rows, 256), fl),
        ],
        compiler_params=params(48),
    )(start, queries, before, own, grad_context, context, log_total, cosine, sine)


def middle_kernel(ctx_ref, out_w_ref, router_ref, x_ref, gain_ref, chosen_ref, middle_ref, block_ref, gates_ref):
    width = x_ref.shape[1]
    middle = x_ref[...].astype(fl) + mm(ctx_ref[...], out_w_ref[...])
    inverse = lax.rsqrt(jnp.mean(middle * middle, axis=1, keepdims=True) + NORM_EPS)
    normed = (middle * inverse * gain_ref[...]).astype(bf)
    logits = mm(normed, router_ref[...])
    chosen = chosen_ref[...] > 0.0
    logits = jnp.where(chosen, logits, MASKED)
    weights = jnp.exp(logits - jnp.max(logits, axis=1, keepdims=True))
    weights = jnp.where(chosen, weights, 0.0)
    gates = weights / jnp.sum(weights, axis=1, keepdims=True)
    high = gates.astype(bf).astype(fl)
    middle_ref[...] = middle
    gates_ref[...] = gates
    block_ref[:, :width] = normed
    block_ref[:, width:] = (high + pltpu.roll(gates - high, EXPERTS, 1)).astype(bf)


def middle_part(ctx, full, tokens, gain, chosen):
    rows, width = tokens.shape
    return pl.pallas_call(
        middle_kernel,
        grid=(1,),
        in_specs=[
            pl.BlockSpec((rows, width), lambda j: (0, 0)),
            pl.BlockSpec((width, width), lambda j: (0, 0)),
            pl.BlockSpec((width, LANES), lambda j: (0, 8)),
            pl.BlockSpec((rows, width), lambda j: (0, 0)),
            pl.BlockSpec((1, width), lambda j: (0, 0)),
            pl.BlockSpec((rows, LANES), lambda j: (0, 0)),
        ],
        out_specs=[
            pl.BlockSpec((rows, width), lambda j: (0, 0)),
            pl.BlockSpec((rows, width + LANES), lambda j: (0, 0)),
            pl.BlockSpec((rows, LANES), lambda j: (0, 0)),
        ],
        out_shape=[
            jax.ShapeDtypeStruct((rows, width), fl),
            jax.ShapeDtypeStruct((rows, width + LANES), bf),
            jax.ShapeDtypeStruct((rows, LANES), fl),
        ],
        compiler_params=params(48),
    )(ctx, full, full, tokens, gain, chosen)


def experts_kernel(
    first_ref, x0, x1, x2, x3, c0, c1, c2, c3, w_ref, out_hbm, gn_hbm, out_send, gn_send, grad_ref,
    xs, cs, xt, ct, ws, out_acc, gn_acc, hid_s, gate_s, up_s, sems, w_sems,
):
    step = pl.program_id(0)
    steps = pl.num_programs(0)
    rows = c0.shape[0]
    width = c0.shape[1]
    cols = ws.shape[2]
    hidden_width = cols // 3
    expert = first_ref[0] + step
    order = snake(w_sems.shape[1])
    size = width // len(order)
    held = lax.rem(step, 2)

    def weight_copies(which, slot):
        columns = pl.ds(pl.multiple_of(which * cols, cols), cols)
        return [
            pltpu.make_async_copy(
                w_ref.at[pl.ds(place * size, size), columns],
                ws.at[slot, pl.ds(replica * size, size), :],
                w_sems.at[slot, place],
            )
            for place, replica in enumerate(order)
        ]

    @pl.when(step == 0)
    def _():
        copies = []
        for slot, (x, c) in enumerate(((x0, c0), (x1, c1), (x2, c2), (x3, c3))):
            here = pl.ds(slot * rows, rows)
            copies.append(pltpu.make_async_copy(x, xs.at[here], sems.at[2 * slot]))
            copies.append(pltpu.make_async_copy(c, cs.at[here], sems.at[2 * slot + 1]))
        for copy in copies + weight_copies(0, 0) + weight_copies(1, 1):
            copy.start()
        for copy in copies:
            copy.wait()
        out_acc[...] = jnp.zeros_like(out_acc)
        gn_acc[...] = jnp.zeros_like(gn_acc)
        for slot in range(GROUP):
            here = slice(slot * rows, (slot + 1) * rows)
            for source, target in ((xs, xt), (cs, ct)):
                turned = source[here, :width].T
                for place, replica in enumerate(order):
                    target[place * size : (place + 1) * size, here] = turned[
                        replica * size : (replica + 1) * size
                    ]

    for copy in weight_copies(step, held):
        copy.wait()

    def tile_step(tile, carry):
        here = pl.ds(pl.multiple_of(tile * rows, rows), rows)
        x_tile = xs[here, :width]
        gate_w = ws[held, :, :hidden_width]
        up_w = ws[held, :, hidden_width : 2 * hidden_width]
        down_w = ws[held, :, 2 * hidden_width :]
        gate = mm(x_tile, gate_w)
        up = mm(x_tile, up_w)
        raw = mm(cs[here, :], down_w)
        packed = xs[here, width:].astype(fl)
        lane = lane_index(packed.shape)
        mine = (lane == expert) | (lane == expert + EXPERTS)
        gates = jnp.sum(jnp.where(mine, packed, 0.0), axis=1, keepdims=True)
        sigmoid = 1.0 / (1.0 + jnp.exp(-gate))
        silu = gate * sigmoid
        hidden = (silu * up).astype(bf).astype(fl)
        grad_gates = jnp.sum(hidden * raw, axis=1, keepdims=True)
        grad_hidden = raw * gates
        hid = (hidden * gates).astype(bf)
        grad_gate = (grad_hidden * up * sigmoid * (1.0 + gate * (1.0 - sigmoid))).astype(bf)
        grad_up = (grad_hidden * silu).astype(bf)
        hid_s[here, :] = hid
        gate_s[here, :] = grad_gate
        up_s[here, :] = grad_up
        out_acc[here, :] += mm(hid, down_w, NT)
        gn_acc[here, :width] += mm(grad_gate, gate_w, NT) + mm(grad_up, up_w, NT)
        gn_acc[here, width:] += jnp.where(lane == expert, grad_gates, 0.0)
        return carry

    lax.fori_loop(0, GROUP, tile_step, 0)

    @pl.when(step + 2 < steps)
    def _():
        for copy in weight_copies(step + 2, held):
            copy.start()

    half = out_hbm.shape[0]
    results = [
        pltpu.make_async_copy(out_acc.at[:half], out_hbm, sems.at[0]),
        pltpu.make_async_copy(gn_acc.at[:half], gn_hbm, sems.at[1]),
        pltpu.make_async_copy(xs.at[half:, :width], out_send, sems.at[2]),
        pltpu.make_async_copy(xs.at[:half], gn_send, sems.at[3]),
    ]

    @pl.when(step == steps - 1)
    def _():
        gates_part = gn_acc[:, width:]
        high = gates_part.astype(bf).astype(fl)
        low = (gates_part - high).astype(bf).astype(fl)
        gn_acc[:, width:] = high + pltpu.roll(low, EXPERTS, 1)
        xs[:half, :] = gn_acc[half:, :].astype(bf)
        xs[half:, :width] = out_acc[half:, :].astype(bf)
        for copy in results:
            copy.start()

    grad_ref[:, :hidden_width] = mm(xt[...], gate_s[...]).astype(bf)
    grad_ref[:, hidden_width : 2 * hidden_width] = mm(xt[...], up_s[...]).astype(bf)
    grad_ref[:, 2 * hidden_width :] = mm(ct[...], hid_s[...]).astype(bf)

    @pl.when(step == steps - 1)
    def _():
        for copy in results:
            copy.wait()


def experts_part(first, replicas, blocks, cots, weights):
    rows, width = cots[0].shape
    local = EXPERTS // GROUP
    cols = weights.shape[1] // local
    hidden_width = cols // 3
    total = GROUP * rows
    anywhere = pl.BlockSpec(memory_space=pl.ANY)
    return pl.pallas_call(
        experts_kernel,
        grid_spec=pltpu.PrefetchScalarGridSpec(
            num_scalar_prefetch=1,
            grid=(local,),
            in_specs=[anywhere] * 9,
            out_specs=[anywhere] * 4 + [pl.BlockSpec((width, cols), lambda e, s: (0, e))],
            scratch_shapes=[
                pltpu.VMEM((total, width + LANES), bf),
                pltpu.VMEM((total, width), bf),
                pltpu.VMEM((width, total), bf),
                pltpu.VMEM((width, total), bf),
                pltpu.VMEM((2, width, cols), bf),
                pltpu.VMEM((total, width), fl),
                pltpu.VMEM((total, width + LANES), fl),
                pltpu.VMEM((total, hidden_width), bf),
                pltpu.VMEM((total, hidden_width), bf),
                pltpu.VMEM((total, hidden_width), bf),
                pltpu.SemaphoreType.DMA((8,)),
                pltpu.SemaphoreType.DMA((2, replicas)),
            ],
        ),
        out_shape=[
            jax.ShapeDtypeStruct((total // 2, width), fl),
            jax.ShapeDtypeStruct((total // 2, width + LANES), fl),
            jax.ShapeDtypeStruct((total // 2, width), bf),
            jax.ShapeDtypeStruct((total // 2, width + LANES), bf),
            jax.ShapeDtypeStruct((width, local * cols), bf),
        ],
        compiler_params=params(62),
    )(first, *blocks, *cots, weights)


def middle_back_kernel(
    gn_ref, gates_ref, middle_ref, cot_ref, ctx_ref, out_w_ref, router_ref, gain_ref,
    gm_ref, gctx_ref, gw_ref, gain_grad_ref,
):
    width = cot_ref.shape[1]
    packed = gn_ref[:, width:]
    gates = gates_ref[...]
    grad_gates = packed + pltpu.roll(packed, LANES - EXPERTS, 1)
    inner = jnp.sum(gates * grad_gates, axis=1, keepdims=True)
    grad_logits = (gates * (grad_gates - inner)).astype(bf)
    middle = middle_ref[...]
    inverse = lax.rsqrt(jnp.mean(middle * middle, axis=1, keepdims=True) + NORM_EPS)
    gain = gain_ref[...]
    unit = middle * inverse
    normed = (unit * gain).astype(bf)
    grad_normed = gn_ref[:, :width] + mm(grad_logits, router_ref[...], NT)
    gw_ref[:, width:] = mm(normed, grad_logits, TN).astype(bf)
    gain_grad_ref[...] = jnp.sum(grad_normed * unit, axis=0, keepdims=True)
    scaled = grad_normed * gain
    mean = jnp.mean(scaled * middle, axis=1, keepdims=True)
    grad_middle = cot_ref[...].astype(fl) + inverse * scaled - unit * (inverse * inverse * mean)
    gm_ref[...] = grad_middle
    branch = grad_middle.astype(bf)
    gctx_ref[...] = mm(branch, out_w_ref[...], NT).astype(bf)
    gw_ref[:, :width] = mm(ctx_ref[...], branch, TN).astype(bf)


def middle_back(gn, gates, middle, cot, ctx, full, gain):
    rows, width = cot.shape
    here = lambda *shape: pl.BlockSpec(shape, lambda j: (0, 0))
    return pl.pallas_call(
        middle_back_kernel,
        grid=(1,),
        in_specs=[
            here(rows, width + LANES), here(rows, LANES), here(rows, width), here(rows, width), here(rows, width),
            pl.BlockSpec((width, width), lambda j: (0, 0)),
            pl.BlockSpec((width, LANES), lambda j: (0, 8)),
            here(1, width),
        ],
        out_specs=[here(rows, width), here(rows, width), here(width, width + LANES), here(1, width)],
        out_shape=[
            jax.ShapeDtypeStruct((rows, width), fl),
            jax.ShapeDtypeStruct((rows, width), bf),
            jax.ShapeDtypeStruct((width, width + LANES), bf),
            jax.ShapeDtypeStruct((1, width), fl),
        ],
        compiler_params=params(56),
    )(gn, gates, middle, cot, ctx, full, full, gain)


def finish_kernel(
    gq_ref, kept_ref, back_ref, normed_ref, x_ref, gm_ref, w_ref, gain_ref, cos_ref, sin_ref,
    token_ref, gw_ref, gain_grad_ref, gkv_ref,
):
    width = x_ref.shape[1]
    for part in range(4):
        first = part * 256
        both = kept_ref[:, first : first + 256] + back_ref[:, first : first + 256].astype(fl)
        piece = both[:, :LANES]
        gkv_ref[:, first : first + LANES] = (
            piece * cos_ref[...] - swap_halves(piece) * sin_ref[...]
        ).astype(bf)
        gkv_ref[:, first + LANES : first + 256] = both[:, LANES:].astype(bf)
    normed = normed_ref[...]
    gw_ref[:, :width] = mm(normed, gq_ref[...], TN).astype(bf)
    gw_ref[:, width:] = mm(normed, gkv_ref[...], TN).astype(bf)
    grad_normed = mm(gq_ref[...], w_ref[:, :width], NT) + mm(gkv_ref[...], w_ref[:, width:], NT)
    x = x_ref[...].astype(fl)
    inverse = lax.rsqrt(jnp.mean(x * x, axis=1, keepdims=True) + NORM_EPS)
    unit = x * inverse
    gain_grad_ref[...] = jnp.sum(grad_normed * unit, axis=0, keepdims=True)
    scaled = grad_normed * gain_ref[...]
    mean = jnp.mean(scaled * x, axis=1, keepdims=True)
    token_ref[...] = gm_ref[...] + inverse * scaled - unit * (inverse * inverse * mean)


def finish(grad_query, kept, back, normed, tokens, grad_middle, full, gain, cosine, sine):
    rows, width = tokens.shape
    here = lambda *shape: pl.BlockSpec(shape, lambda j: (0, 0))
    return pl.pallas_call(
        finish_kernel,
        grid=(1,),
        in_specs=[
            here(rows, width), here(rows, width), here(rows, width), here(rows, width), here(rows, width),
            here(rows, width), here(width, 2 * width), here(1, width), here(rows, LANES), here(rows, LANES),
        ],
        out_specs=[here(rows, width), here(width, 2 * width), here(1, width)],
        out_shape=[
            jax.ShapeDtypeStruct((rows, width), fl),
            jax.ShapeDtypeStruct((width, 2 * width), bf),
            jax.ShapeDtypeStruct((1, width), fl),
        ],
        scratch_shapes=[pltpu.VMEM((rows, width), bf)],
        compiler_params=params(60),
    )(grad_query, kept, back, normed, tokens, grad_middle, full, gain, cosine, sine)


def doubling_gather(part, index, bits, last):
    cur = part
    while bits >= last:
        other = swapped(cur, bits)
        pair = jnp.where(
            (index // bits) % 2 == 0, jnp.stack([cur, other], axis=1), jnp.stack([other, cur], axis=1)
        )
        cur = pair.reshape(2 * cur.shape[0], *cur.shape[1:])
        bits //= 2
    return cur


def halving_sum(part, index, meanwhile):
    n = lax.axis_size("fsdp")
    cur = part.reshape(n, part.shape[0] // n, part.shape[1])
    bits = 1
    while bits < n:
        mine = (index // bits) % 2
        pairs = cur.reshape(cur.shape[0] // 2, 2, cur.shape[1], cur.shape[2])
        keep = lax.dynamic_index_in_dim(pairs, mine, 1, keepdims=False)
        send = lax.dynamic_index_in_dim(pairs, 1 - mine, 1, keepdims=False)
        cur = keep.astype(fl) + swapped(send.astype(bf), bits).astype(fl)
        bits *= 2
        if bits == GROUP:
            cur, meanwhile = lax.optimization_barrier((cur, meanwhile))
    return cur[0], meanwhile


def snake(replicas):
    return [*range(0, replicas, 2), *range(replicas - 1, 0, -2)]


def group_order(pieces, member):
    one, two = member % 2 == 1, member // 2 == 1
    a, b, c, d = pieces
    a, b, c, d = jnp.where(one, b, a), jnp.where(one, a, b), jnp.where(one, d, c), jnp.where(one, c, d)
    return jnp.where(two, c, a), jnp.where(two, d, b), jnp.where(two, a, c), jnp.where(two, b, d)


def per_device(
    tokens, positions, routes, attn_gain, w_query, w_key, w_value, w_out, mlp_gain, w_router,
    w_gate, w_up, w_down, cotangent,
):
    n = lax.axis_size("fsdp")
    index = lax.axis_index("fsdp")
    member = index % GROUP
    rows_dev, model_width = tokens.shape
    own_rows = w_query.shape[0]
    hidden_width = w_gate.shape[2]
    local = EXPERTS // GROUP
    across = [[r * GROUP + g for r in snake(n // GROUP)] for g in range(GROUP)]

    key_value = jnp.concatenate(
        [w_key.reshape(own_rows, 4, LANES), w_value.reshape(own_rows, 4, LANES)], axis=2
    ).reshape(own_rows, model_width)
    gains = jnp.stack([attn_gain, mlp_gain], axis=1)
    packed = jnp.concatenate(
        [
            w_query, key_value, gains, jnp.zeros((own_rows, LANES - 2), bf),
            w_out, w_router, jnp.zeros((own_rows, LANES - EXPERTS), bf),
        ],
        axis=1,
    )
    first_columns = 2 * model_width + LANES
    far = doubling_gather(packed[None], index, n // 2, 2 * GROUP)

    shard = jnp.concatenate([w_gate, w_up, w_down], axis=2).reshape(
        GROUP, local, own_rows, 3 * hidden_width
    )
    pieces = []
    for bits in range(GROUP):
        piece = lax.dynamic_index_in_dim(shard, member ^ bits, 0, keepdims=False)
        pieces.append(swapped(piece, bits) if bits else piece)
    mine = jnp.stack(group_order(pieces, member))
    mine = mine.transpose(0, 2, 1, 3).reshape(GROUP * own_rows, local * 3 * hidden_width)
    mine, far = lax.optimization_barrier((mine, far))
    near, later = far[:, :, :first_columns], far[:, :, first_columns:]
    near, later = lax.optimization_barrier((doubling_gather(near, index, GROUP, GROUP), later))
    near, later = lax.optimization_barrier(
        (doubling_gather(near, index, 2, 2), doubling_gather(later, index, GROUP, GROUP))
    )
    full = doubling_gather(near, index, 1, 1).reshape(n * own_rows, first_columns)
    later = doubling_gather(later, index, 2, 2)
    expert_w = lax.all_gather(mine, "fsdp", axis=0, tiled=True, axis_index_groups=across)

    cot_x = swapped(cotangent, 2)
    cots = (cotangent, cot_x, swapped(cotangent, 1), swapped(cot_x, 1))

    gain_one = full[:, 2 * model_width].astype(fl)[None, :]
    gain_two = full[:, 2 * model_width + 1].astype(fl)[None, :]
    cosine, sine = rope_tables(positions)
    residual = tokens.astype(fl)
    inverse_one = lax.rsqrt(jnp.mean(residual * residual, axis=-1, keepdims=True) + NORM_EPS)
    normed_one = (residual * inverse_one * gain_one).astype(bf)
    own = project(key_value_kernel, normed_one, full, 4, cosine, sine)
    normed_q, own = lax.optimization_barrier((normed_one, own))
    before = shifted(own, "fsdp", 1)
    queries = project(query_kernel, normed_q, full, 0, cosine, sine)
    queries, later = lax.optimization_barrier((queries, later))
    full_out = doubling_gather(later, index, 1, 1).reshape(n * own_rows, model_width + LANES)
    start = (jnp.arange(rows_dev, dtype=jnp.int32) - positions)[:, None]
    context, context_low, log_total = attend(start, queries, before, own)

    context_low, full_out, *cots = lax.optimization_barrier((context_low, full_out, *cots))
    lanes = jnp.arange(LANES, dtype=jnp.int32)
    chosen = jnp.any(routes[:, :, None] == lanes[None, None, :], axis=1).astype(fl)
    middle, block, gates = middle_part(context_low, full_out, tokens, gain_two, chosen)

    block_x = swapped(block, 2)
    blocks = (block, block_x, swapped(block, 1), swapped(block_x, 1))
    first = (member * local).astype(jnp.int32).reshape(1)
    out_keep, gn_keep, out_send, gn_send, expert_grads = experts_part(first, n // GROUP, blocks, cots, expert_w)

    owned_experts = lax.psum_scatter(
        expert_grads, "fsdp", scatter_dimension=0, tiled=True, axis_index_groups=across
    )

    def halfway(kept, sent):
        other = swapped(sent, 1)
        mine = kept[:rows_dev] + other[:rows_dev].astype(fl)
        return mine, (kept[rows_dev:] + other[rows_dev:].astype(fl)).astype(bf)

    gn, gn_away = halfway(gn_keep, gn_send)
    gn = gn + swapped(gn_away, 2).astype(fl)
    grad_middle, grad_context, out_grad, gain_two_grad = middle_back(
        gn, gates, middle, cotangent, context_low, full_out, gain_two
    )
    grad_query, sent, kept = attend_back(
        start, queries, before, own, grad_context, context, log_total, cosine, sine
    )
    back = shifted(sent, "fsdp", -1)
    token_grad, proj_grad, gain_one_grad = finish(
        grad_query, kept, back, normed_one, tokens, grad_middle, full, gain_one, cosine, sine
    )
    gains = jnp.concatenate(
        [gain_one_grad, gain_two_grad, jnp.zeros((LANES - 2, model_width), fl)], axis=0
    ).T.astype(bf)
    out, out_away = halfway(out_keep, out_send)
    owned, (owned_experts, out_away) = halving_sum(
        jnp.concatenate([proj_grad, out_grad, gains], axis=1), index, (owned_experts, out_away)
    )
    activations = (middle + (out + swapped(out_away, 2).astype(fl))).astype(bf)
    owned_kv = owned[:, 1024:2048].reshape(own_rows, 4, 2, LANES)

    pieces = []
    for bits in range(GROUP):
        piece = lax.dynamic_slice_in_dim(owned_experts, (member ^ bits) * own_rows, own_rows, 0)
        pieces.append(swapped(piece, bits) if bits else piece)
    experts = jnp.stack(group_order(pieces, member)).reshape(GROUP, own_rows, local, 3, hidden_width)
    experts = experts.transpose(3, 0, 2, 1, 4).reshape(3, EXPERTS, own_rows, hidden_width).astype(fl)
    return (
        activations,
        token_grad,
        owned[:, 3200],
        owned[:, :1024],
        owned_kv[:, :, 0].reshape(own_rows, 512),
        owned_kv[:, :, 1].reshape(own_rows, 512),
        owned[:, 2048:3072],
        owned[:, 3201],
        owned[:, 3072 : 3072 + EXPERTS],
        experts[0],
        experts[1],
        experts[2],
    )


def solution(mesh):
    rows = P("fsdp", None)
    line = P("fsdp")
    stack = P(None, "fsdp", None)
    return jax.shard_map(
        per_device,
        mesh=mesh,
        in_specs=(rows, line, rows, line, rows, rows, rows, rows, line, rows, stack, stack, stack, rows),
        out_specs=(rows, rows, line, rows, rows, rows, rows, line, rows, stack, stack, stack),
        check_vma=False,
    )
```

```python
import jax
import jax.numpy as jnp
from jax import lax
from jax.experimental import pallas as pl
from jax.experimental.pallas import tpu as pltpu
from jax.sharding import PartitionSpec as P

HEADS = 16
KV_HEADS = 8
HEAD_DIM = 64
TOP = 8
EXPERTS = 16
GROUP = 4
LANES = 128
NORM_EPS = 1e-06
ROPE_THETA = 10000.0
MASKED = -1e30
MIB = 1024 * 1024

bf = jnp.bfloat16
fl = jnp.float32
SLOT = (0, 2, 1, 3)

NN = (((1,), (0,)), ((), ()))
NT = (((1,), (1,)), ((), ()))
TN = (((0,), (0,)), ((), ()))


def mm(a, b, dims=NN):
    return lax.dot_general(a, b, dims, preferred_element_type=fl)


def params(mib):
    return pltpu.CompilerParams(vmem_limit_bytes=mib * MIB)


def shifted(block, axis, distance):
    devices = range(lax.axis_size(axis))
    route = [(i - distance, i) for i in devices if i - distance in devices]
    return lax.ppermute(block, axis, route)


def swapped(block, bits):
    return lax.ppermute(block, "fsdp", [(i, i ^ bits) for i in range(lax.axis_size("fsdp"))])


def lane_index(shape):
    return lax.broadcasted_iota(jnp.int32, shape, len(shape) - 1)


def swap_halves(v):
    first = (lane_index(v.shape) & 32) == 0
    return jnp.where(first, pltpu.roll(v, LANES - 32, 1), pltpu.roll(v, 32, 1))


def rope_tables(positions):
    half_width = HEAD_DIM // 2
    frequency = ROPE_THETA ** (-(jnp.arange(half_width, dtype=fl) * 2.0) / HEAD_DIM)
    angle_rows = positions.astype(fl)[:, None] * frequency[None, :]
    cosine, sine = jnp.cos(angle_rows), jnp.sin(angle_rows)
    return (
        jnp.concatenate([cosine] * 4, axis=1),
        jnp.concatenate([-sine, sine, -sine, sine], axis=1),
    )


def query_kernel(x_ref, w_ref, cos_ref, sin_ref, out_ref):
    lin = mm(x_ref[...], w_ref[...])
    for part in range(2):
        piece = lin[:, part * LANES : (part + 1) * LANES]
        turned = piece * cos_ref[...] + swap_halves(piece) * sin_ref[...]
        out_ref[:, part * LANES : (part + 1) * LANES] = (turned.astype(bf) * HEAD_DIM**-0.5).astype(bf)


def key_value_kernel(x_ref, w_ref, cos_ref, sin_ref, out_ref):
    lin = mm(x_ref[...], w_ref[...])
    piece = lin[:, :LANES]
    out_ref[:, :LANES] = (piece * cos_ref[...] + swap_halves(piece) * sin_ref[...]).astype(bf)
    out_ref[:, LANES:] = lin[:, LANES:].astype(bf)


def project(kernel, normed, weights, first_block, cosine, sine):
    rows, width = normed.shape
    return pl.pallas_call(
        kernel,
        grid=(4,),
        in_specs=[
            pl.BlockSpec((rows, width), lambda j: (0, 0)),
            pl.BlockSpec((width, 256), lambda j: (0, first_block + j)),
            pl.BlockSpec((rows, LANES), lambda j: (0, 0)),
            pl.BlockSpec((rows, LANES), lambda j: (0, 0)),
        ],
        out_specs=pl.BlockSpec((rows, 256), lambda j: (0, j)),
        out_shape=jax.ShapeDtypeStruct((rows, 1024), bf),
        compiler_params=params(32),
    )(normed, weights, cosine, sine)


def fill_bias(start_ref, bias_ref):
    rows = bias_ref.shape[0]
    column = lax.broadcasted_iota(jnp.int32, bias_ref.shape, 1) - rows
    row = lax.broadcasted_iota(jnp.int32, bias_ref.shape, 0)
    seen = (column >= start_ref[...]) & (column <= row)
    bias_ref[...] = jnp.where(seen, 0.0, MASKED)


def attend_kernel(start_ref, q_ref, prev_ref, own_ref, ctx_ref, low_ref, lse_ref, bias_ref, kv_ref):
    rows = q_ref.shape[0]
    half = rows // 2

    @pl.when(pl.program_id(0) == 0)
    def _():
        fill_bias(start_ref, bias_ref)

    kv_ref[:rows, :] = prev_ref[...]
    kv_ref[rows:, :] = own_ref[...]
    for tile in range(2):
        queries = pl.ds(tile * half, half)
        keys = rows + (tile + 1) * half
        bias = bias_ref[queries, :keys]
        for head in range(4):
            lane = 64 * (head // 2)
            scores = mm(
                q_ref[queries, head * 64 : head * 64 + 64], kv_ref[:keys, lane : lane + 64], NT
            )
            scores = scores + bias
            row_max = jnp.max(scores, axis=1, keepdims=True)
            weights = jnp.exp(scores - row_max)
            total = jnp.sum(weights, axis=1, keepdims=True)
            probs = (weights * (1.0 / total)).astype(bf)
            context = mm(probs, kv_ref[:keys, LANES + lane : LANES + lane + 64])
            ctx_ref[queries, head * 64 : head * 64 + 64] = context
            low_ref[queries, head * 64 : head * 64 + 64] = context.astype(bf)
            lse_ref[0, queries, head : head + 1] = row_max + jnp.log(total)


def attend(start, queries, before, own):
    rows = queries.shape[0]
    wide = pl.BlockSpec((rows, 256), lambda j: (0, j))
    return pl.pallas_call(
        attend_kernel,
        grid=(4,),
        in_specs=[pl.BlockSpec((rows, 1), lambda j: (0, 0)), wide, wide, wide],
        out_specs=[wide, wide, pl.BlockSpec((1, rows, LANES), lambda j: (j, 0, 0))],
        out_shape=[
            jax.ShapeDtypeStruct((rows, 1024), fl),
            jax.ShapeDtypeStruct((rows, 1024), bf),
            jax.ShapeDtypeStruct((4, rows, LANES), fl),
        ],
        scratch_shapes=[pltpu.VMEM((rows, 2 * rows), fl), pltpu.VMEM((2 * rows, 256), bf)],
        compiler_params=params(40),
    )(start, queries, before, own)


def attend_back_step(q_ref, kv_ref, gctx_ref, ctx_ref, lse_ref, bias, queries, keys, head):
    lane = 64 * (head // 2)
    here = slice(head * 64, head * 64 + 64)
    query = q_ref[queries, here]
    grad = gctx_ref[queries, here]
    key = kv_ref[:keys, lane : lane + 64]
    value = kv_ref[:keys, LANES + lane : LANES + lane + 64]
    inner = jnp.sum(grad.astype(fl) * ctx_ref[queries, here], axis=1, keepdims=True)
    scores = mm(query, key, NT) + bias
    probs = jnp.exp(scores - lse_ref[0, queries, head : head + 1])
    grad_scores = (probs * (mm(grad, value, NT) - inner)).astype(bf)
    return (
        mm(grad_scores, key) * HEAD_DIM**-0.5,
        mm(grad_scores, query, TN),
        mm(probs.astype(bf), grad, TN),
    )


def attend_back_prev_kernel(start_ref, q_ref, prev_ref, gctx_ref, ctx_ref, lse_ref, gq_ref, sent_ref, bias_ref, gkv_ref):
    rows = q_ref.shape[0]

    @pl.when(pl.program_id(0) == 0)
    def _():
        column = lax.broadcasted_iota(jnp.int32, bias_ref.shape, 1) - rows
        bias_ref[...] = jnp.where(column >= start_ref[...], 0.0, MASKED)

    gkv_ref[...] = jnp.zeros_like(gkv_ref)
    for head in range(4):
        lane = 64 * (head // 2)
        gq, gk, gv = attend_back_step(
            q_ref, prev_ref, gctx_ref, ctx_ref, lse_ref, bias_ref[...], slice(None), rows, head
        )
        gq_ref[:, head * 64 : head * 64 + 64] = gq
        gkv_ref[:, lane : lane + 64] += gk
        gkv_ref[:, LANES + lane : LANES + lane + 64] += gv
    sent_ref[...] = gkv_ref[...].astype(bf)


def attend_back_own_kernel(
    start_ref, q_ref, own_ref, gctx_ref, ctx_ref, lse_ref, part_ref, cos_ref, sin_ref,
    gq_ref, kept_ref, bias_ref, gq_acc_ref,
):
    rows = q_ref.shape[0]
    half = rows // 2

    @pl.when(pl.program_id(0) == 0)
    def _():
        column = lax.broadcasted_iota(jnp.int32, bias_ref.shape, 1)
        row = lax.broadcasted_iota(jnp.int32, bias_ref.shape, 0)
        bias_ref[...] = jnp.where((column >= start_ref[...]) & (column <= row), 0.0, MASKED)

    kept_ref[...] = jnp.zeros_like(kept_ref)
    for tile in range(2):
        queries = pl.ds(tile * half, half)
        keys = (tile + 1) * half
        for head in range(4):
            lane = 64 * (head // 2)
            here = slice(head * 64, head * 64 + 64)
            gq, gk, gv = attend_back_step(
                q_ref, own_ref, gctx_ref, ctx_ref, lse_ref, bias_ref[queries, :keys], queries, keys, head
            )
            gq_acc_ref[queries, here] = gq + part_ref[queries, here]
            kept_ref[:keys, lane : lane + 64] += gk
            kept_ref[:keys, LANES + lane : LANES + lane + 64] += gv
    for part in range(2):
        here = slice(part * LANES, part * LANES + LANES)
        piece = gq_acc_ref[:, here]
        gq_ref[:, here] = (piece * cos_ref[...] - swap_halves(piece) * sin_ref[...]).astype(bf)


def attend_back_prev(start, queries, before, grad_context, context, log_total):
    rows = queries.shape[0]
    wide = pl.BlockSpec((rows, 256), lambda j: (0, j))
    return pl.pallas_call(
        attend_back_prev_kernel,
        grid=(4,),
        in_specs=[
            pl.BlockSpec((rows, 1), lambda j: (0, 0)), wide, wide, wide, wide,
            pl.BlockSpec((1, rows, LANES), lambda j: (j, 0, 0)),
        ],
        out_specs=[wide, wide],
        out_shape=[jax.ShapeDtypeStruct((rows, 1024), fl), jax.ShapeDtypeStruct((rows, 1024), bf)],
        scratch_shapes=[pltpu.VMEM((rows, rows), fl), pltpu.VMEM((rows, 256), fl)],
        compiler_params=params(48),
    )(start, queries, before, grad_context, context, log_total)


def attend_back_own(start, queries, own, grad_context, context, log_total, part, cosine, sine):
    rows = queries.shape[0]
    wide = pl.BlockSpec((rows, 256), lambda j: (0, j))
    table = pl.BlockSpec((rows, LANES), lambda j: (0, 0))
    return pl.pallas_call(
        attend_back_own_kernel,
        grid=(4,),
        in_specs=[
            pl.BlockSpec((rows, 1), lambda j: (0, 0)), wide, wide, wide, wide,
            pl.BlockSpec((1, rows, LANES), lambda j: (j, 0, 0)), wide, table, table,
        ],
        out_specs=[wide, wide],
        out_shape=[jax.ShapeDtypeStruct((rows, 1024), bf), jax.ShapeDtypeStruct((rows, 1024), fl)],
        scratch_shapes=[pltpu.VMEM((rows, rows), fl), pltpu.VMEM((rows, 256), fl)],
        compiler_params=params(48),
    )(start, queries, own, grad_context, context, log_total, part, cosine, sine)


def middle_kernel(ctx_ref, out_w_ref, router_ref, x_ref, gain_ref, chosen_ref, middle_ref, block_ref, gates_ref):
    width = x_ref.shape[1]
    middle = x_ref[...].astype(fl) + mm(ctx_ref[...], out_w_ref[...])
    inverse = lax.rsqrt(jnp.mean(middle * middle, axis=1, keepdims=True) + NORM_EPS)
    normed = (middle * inverse * gain_ref[...]).astype(bf)
    logits = mm(normed, router_ref[...])
    chosen = chosen_ref[...] > 0.0
    logits = jnp.where(chosen, logits, MASKED)
    weights = jnp.exp(logits - jnp.max(logits, axis=1, keepdims=True))
    weights = jnp.where(chosen, weights, 0.0)
    gates = weights / jnp.sum(weights, axis=1, keepdims=True)
    high = gates.astype(bf).astype(fl)
    middle_ref[...] = middle
    gates_ref[...] = gates
    block_ref[:, :width] = normed
    block_ref[:, width:] = (high + pltpu.roll(gates - high, EXPERTS, 1)).astype(bf)


def middle_part(ctx, full, tokens, gain, chosen):
    rows, width = tokens.shape
    return pl.pallas_call(
        middle_kernel,
        grid=(1,),
        in_specs=[
            pl.BlockSpec((rows, width), lambda j: (0, 0)),
            pl.BlockSpec((width, width), lambda j: (0, 2)),
            pl.BlockSpec((width, LANES), lambda j: (0, 24)),
            pl.BlockSpec((rows, width), lambda j: (0, 0)),
            pl.BlockSpec((1, width), lambda j: (0, 0)),
            pl.BlockSpec((rows, LANES), lambda j: (0, 0)),
        ],
        out_specs=[
            pl.BlockSpec((rows, width), lambda j: (0, 0)),
            pl.BlockSpec((rows, width + LANES), lambda j: (0, 0)),
            pl.BlockSpec((rows, LANES), lambda j: (0, 0)),
        ],
        out_shape=[
            jax.ShapeDtypeStruct((rows, width), fl),
            jax.ShapeDtypeStruct((rows, width + LANES), bf),
            jax.ShapeDtypeStruct((rows, LANES), fl),
        ],
        compiler_params=params(48),
    )(ctx, full, full, tokens, gain, chosen)


def experts_kernel(
    first_ref, x0, x1, x2, x3, c0, c1, c2, c3, w_ref, out_hbm, gn_hbm, out_send, gn_send, grad_ref,
    xs, cs, xt, ct, ws, out_acc, gn_acc, hid_s, gate_s, up_s, sems, w_sems,
):
    step = pl.program_id(0)
    steps = pl.num_programs(0)
    rows = c0.shape[0]
    width = c0.shape[1]
    cols = ws.shape[2]
    hidden_width = cols // 3
    expert = first_ref[0] + step
    order = snake(w_sems.shape[1])
    size = width // len(order)
    held = lax.rem(step, 2)

    def weight_copies(which, slot):
        columns = pl.ds(pl.multiple_of(which * cols, cols), cols)
        return [
            pltpu.make_async_copy(
                w_ref.at[pl.ds(place * size, size), columns],
                ws.at[slot, pl.ds(replica * size, size), :],
                w_sems.at[slot, place],
            )
            for place, replica in enumerate(order)
        ]

    @pl.when(step == 0)
    def _():
        copies = []
        for slot, (x, c) in enumerate(((x0, c0), (x1, c1), (x2, c2), (x3, c3))):
            here = pl.ds(slot * rows, rows)
            copies.append(pltpu.make_async_copy(x, xs.at[here], sems.at[2 * slot]))
            copies.append(pltpu.make_async_copy(c, cs.at[here], sems.at[2 * slot + 1]))
        for copy in copies + weight_copies(0, 0) + weight_copies(1, 1):
            copy.start()
        for copy in copies:
            copy.wait()
        out_acc[...] = jnp.zeros_like(out_acc)
        gn_acc[...] = jnp.zeros_like(gn_acc)
        for slot in range(GROUP):
            here = slice(slot * rows, (slot + 1) * rows)
            for source, target in ((xs, xt), (cs, ct)):
                turned = source[here, :width].T
                for place, replica in enumerate(order):
                    target[place * size : (place + 1) * size, here] = turned[
                        replica * size : (replica + 1) * size
                    ]

    for copy in weight_copies(step, held):
        copy.wait()

    def tile_step(tile, carry):
        here = pl.ds(pl.multiple_of(tile * rows, rows), rows)
        x_tile = xs[here, :width]
        gate_w = ws[held, :, :hidden_width]
        up_w = ws[held, :, hidden_width : 2 * hidden_width]
        down_w = ws[held, :, 2 * hidden_width :]
        gate = mm(x_tile, gate_w)
        up = mm(x_tile, up_w)
        raw = mm(cs[here, :], down_w)
        packed = xs[here, width:].astype(fl)
        lane = lane_index(packed.shape)
        mine = (lane == expert) | (lane == expert + EXPERTS)
        gates = jnp.sum(jnp.where(mine, packed, 0.0), axis=1, keepdims=True)
        sigmoid = 1.0 / (1.0 + jnp.exp(-gate))
        silu = gate * sigmoid
        hidden = (silu * up).astype(bf).astype(fl)
        grad_gates = jnp.sum(hidden * raw, axis=1, keepdims=True)
        grad_hidden = raw * gates
        hid = (hidden * gates).astype(bf)
        grad_gate = (grad_hidden * up * sigmoid * (1.0 + gate * (1.0 - sigmoid))).astype(bf)
        grad_up = (grad_hidden * silu).astype(bf)
        hid_s[here, :] = hid
        gate_s[here, :] = grad_gate
        up_s[here, :] = grad_up
        out_acc[here, :] += mm(hid, down_w, NT)
        gn_acc[here, :width] += mm(grad_gate, gate_w, NT) + mm(grad_up, up_w, NT)
        gn_acc[here, width:] += jnp.where(lane == expert, grad_gates, 0.0)
        return carry

    lax.fori_loop(0, GROUP, tile_step, 0)

    @pl.when(step + 2 < steps)
    def _():
        for copy in weight_copies(step + 2, held):
            copy.start()

    half = out_hbm.shape[0]
    results = [
        pltpu.make_async_copy(out_acc.at[:half], out_hbm, sems.at[0]),
        pltpu.make_async_copy(gn_acc.at[:half], gn_hbm, sems.at[1]),
        pltpu.make_async_copy(xs.at[half:, :width], out_send, sems.at[2]),
        pltpu.make_async_copy(xs.at[:half], gn_send, sems.at[3]),
    ]

    @pl.when(step == steps - 1)
    def _():
        gates_part = gn_acc[:, width:]
        high = gates_part.astype(bf).astype(fl)
        low = (gates_part - high).astype(bf).astype(fl)
        gn_acc[:, width:] = high + pltpu.roll(low, EXPERTS, 1)
        xs[:half, :] = gn_acc[half:, :].astype(bf)
        xs[half:, :width] = out_acc[half:, :].astype(bf)
        for copy in results:
            copy.start()

    grad_ref[:, :hidden_width] = mm(xt[...], gate_s[...]).astype(bf)
    grad_ref[:, hidden_width : 2 * hidden_width] = mm(xt[...], up_s[...]).astype(bf)
    grad_ref[:, 2 * hidden_width :] = mm(ct[...], hid_s[...]).astype(bf)

    @pl.when(step == steps - 1)
    def _():
        for copy in results:
            copy.wait()


def experts_part(first, replicas, blocks, cots, weights):
    rows, width = cots[0].shape
    local = EXPERTS // GROUP
    cols = weights.shape[1] // local
    hidden_width = cols // 3
    total = GROUP * rows
    anywhere = pl.BlockSpec(memory_space=pl.ANY)
    return pl.pallas_call(
        experts_kernel,
        grid_spec=pltpu.PrefetchScalarGridSpec(
            num_scalar_prefetch=1,
            grid=(local,),
            in_specs=[anywhere] * 9,
            out_specs=[anywhere] * 4 + [pl.BlockSpec((width, cols), lambda e, s: (0, e))],
            scratch_shapes=[
                pltpu.VMEM((total, width + LANES), bf),
                pltpu.VMEM((total, width), bf),
                pltpu.VMEM((width, total), bf),
                pltpu.VMEM((width, total), bf),
                pltpu.VMEM((2, width, cols), bf),
                pltpu.VMEM((total, width), fl),
                pltpu.VMEM((total, width + LANES), fl),
                pltpu.VMEM((total, hidden_width), bf),
                pltpu.VMEM((total, hidden_width), bf),
                pltpu.VMEM((total, hidden_width), bf),
                pltpu.SemaphoreType.DMA((8,)),
                pltpu.SemaphoreType.DMA((2, replicas)),
            ],
        ),
        out_shape=[
            jax.ShapeDtypeStruct((total // 2, width), fl),
            jax.ShapeDtypeStruct((total // 2, width + LANES), fl),
            jax.ShapeDtypeStruct((total // 2, width), bf),
            jax.ShapeDtypeStruct((total // 2, width + LANES), bf),
            jax.ShapeDtypeStruct((width, local * cols), bf),
        ],
        compiler_params=params(62),
    )(first, *blocks, *cots, weights)


def middle_back_kernel(
    gn_ref, gates_ref, middle_ref, cot_ref, ctx_ref, out_w_ref, router_ref, gain_ref,
    gm_ref, gctx_ref, gw_ref, gain_grad_ref,
):
    width = cot_ref.shape[1]
    packed = gn_ref[:, width:]
    gates = gates_ref[...]
    grad_gates = packed + pltpu.roll(packed, LANES - EXPERTS, 1)
    inner = jnp.sum(gates * grad_gates, axis=1, keepdims=True)
    grad_logits = (gates * (grad_gates - inner)).astype(bf)
    middle = middle_ref[...]
    inverse = lax.rsqrt(jnp.mean(middle * middle, axis=1, keepdims=True) + NORM_EPS)
    gain = gain_ref[...]
    unit = middle * inverse
    normed = (unit * gain).astype(bf)
    grad_normed = gn_ref[:, :width] + mm(grad_logits, router_ref[...], NT)
    gw_ref[:, width:] = mm(normed, grad_logits, TN).astype(bf)
    gain_grad_ref[...] = jnp.sum(grad_normed * unit, axis=0, keepdims=True)
    scaled = grad_normed * gain
    mean = jnp.mean(scaled * middle, axis=1, keepdims=True)
    grad_middle = cot_ref[...].astype(fl) + inverse * scaled - unit * (inverse * inverse * mean)
    gm_ref[...] = grad_middle
    branch = grad_middle.astype(bf)
    gctx_ref[...] = mm(branch, out_w_ref[...], NT).astype(bf)
    gw_ref[:, :width] = mm(ctx_ref[...], branch, TN).astype(bf)


def middle_back(gn, gates, middle, cot, ctx, full, gain):
    rows, width = cot.shape
    here = lambda *shape: pl.BlockSpec(shape, lambda j: (0, 0))
    return pl.pallas_call(
        middle_back_kernel,
        grid=(1,),
        in_specs=[
            here(rows, width + LANES), here(rows, LANES), here(rows, width), here(rows, width), here(rows, width),
            pl.BlockSpec((width, width), lambda j: (0, 2)),
            pl.BlockSpec((width, LANES), lambda j: (0, 24)),
            here(1, width),
        ],
        out_specs=[here(rows, width), here(rows, width), here(width, width + LANES), here(1, width)],
        out_shape=[
            jax.ShapeDtypeStruct((rows, width), fl),
            jax.ShapeDtypeStruct((rows, width), bf),
            jax.ShapeDtypeStruct((width, width + LANES), bf),
            jax.ShapeDtypeStruct((1, width), fl),
        ],
        compiler_params=params(56),
    )(gn, gates, middle, cot, ctx, full, full, gain)


def query_back_kernel(gq_ref, normed_ref, w_ref, gw_ref, part_ref):
    gw_ref[...] = mm(normed_ref[...], gq_ref[...], TN).astype(bf)
    part_ref[...] = mm(gq_ref[...], w_ref[...], NT)


def query_back(grad_query, normed, full):
    rows, width = normed.shape
    here = lambda *shape: pl.BlockSpec(shape, lambda j: (0, 0))
    return pl.pallas_call(
        query_back_kernel,
        grid=(1,),
        in_specs=[here(rows, width), here(rows, width), here(width, width)],
        out_specs=[here(width, width), here(rows, width)],
        out_shape=[jax.ShapeDtypeStruct((width, width), bf), jax.ShapeDtypeStruct((rows, width), fl)],
        compiler_params=params(48),
    )(grad_query, normed, full)


def finish_kernel(
    part_ref, kept_ref, back_ref, normed_ref, x_ref, gm_ref, w_ref, gain_ref, cos_ref, sin_ref,
    token_ref, gw_ref, gain_grad_ref, gkv_ref,
):
    for part in range(4):
        first = part * 256
        both = kept_ref[:, first : first + 256] + back_ref[:, first : first + 256].astype(fl)
        piece = both[:, :LANES]
        gkv_ref[:, first : first + LANES] = (
            piece * cos_ref[...] - swap_halves(piece) * sin_ref[...]
        ).astype(bf)
        gkv_ref[:, first + LANES : first + 256] = both[:, LANES:].astype(bf)
    gw_ref[...] = mm(normed_ref[...], gkv_ref[...], TN).astype(bf)
    grad_normed = part_ref[...] + mm(gkv_ref[...], w_ref[...], NT)
    x = x_ref[...].astype(fl)
    inverse = lax.rsqrt(jnp.mean(x * x, axis=1, keepdims=True) + NORM_EPS)
    unit = x * inverse
    gain_grad_ref[...] = jnp.sum(grad_normed * unit, axis=0, keepdims=True)
    scaled = grad_normed * gain_ref[...]
    mean = jnp.mean(scaled * x, axis=1, keepdims=True)
    token_ref[...] = gm_ref[...] + inverse * scaled - unit * (inverse * inverse * mean)


def finish(part, kept, back, normed, tokens, grad_middle, full, gain, cosine, sine):
    rows, width = tokens.shape
    here = lambda *shape: pl.BlockSpec(shape, lambda j: (0, 0))
    return pl.pallas_call(
        finish_kernel,
        grid=(1,),
        in_specs=[here(rows, width)] * 6
        + [
            pl.BlockSpec((width, width), lambda j: (0, 1)),
            here(1, width), here(rows, LANES), here(rows, LANES),
        ],
        out_specs=[here(rows, width), here(width, width), here(1, width)],
        out_shape=[
            jax.ShapeDtypeStruct((rows, width), fl),
            jax.ShapeDtypeStruct((width, width), bf),
            jax.ShapeDtypeStruct((1, width), fl),
        ],
        scratch_shapes=[pltpu.VMEM((rows, width), bf)],
        compiler_params=params(60),
    )(part, kept, back, normed, tokens, grad_middle, full, gain, cosine, sine)


def doubling_gather(part, index, bits, last):
    cur = part
    while bits >= last:
        other = swapped(cur, bits)
        pair = jnp.where(
            (index // bits) % 2 == 0, jnp.stack([cur, other], axis=1), jnp.stack([other, cur], axis=1)
        )
        cur = pair.reshape(2 * cur.shape[0], *cur.shape[1:])
        bits //= 2
    return cur


def halving_sum(part, index, meanwhile):
    n = lax.axis_size("fsdp")
    cur = part.reshape(n, part.shape[0] // n, part.shape[1])
    bits = 1
    while bits < n:
        mine = (index // bits) % 2
        pairs = cur.reshape(cur.shape[0] // 2, 2, cur.shape[1], cur.shape[2])
        keep = lax.dynamic_index_in_dim(pairs, mine, 1, keepdims=False)
        send = lax.dynamic_index_in_dim(pairs, 1 - mine, 1, keepdims=False)
        cur = keep.astype(fl) + swapped(send.astype(bf), bits).astype(fl)
        bits *= 2
        if bits == GROUP:
            cur, meanwhile = lax.optimization_barrier((cur, meanwhile))
    return cur[0], meanwhile


def snake(replicas):
    return [*range(0, replicas, 2), *range(replicas - 1, 0, -2)]


def group_order(pieces, member):
    one, two = member % 2 == 1, member // 2 == 1
    a, b, c, d = pieces
    a, b, c, d = jnp.where(one, b, a), jnp.where(one, a, b), jnp.where(one, d, c), jnp.where(one, c, d)
    return jnp.where(two, c, a), jnp.where(two, d, b), jnp.where(two, a, c), jnp.where(two, b, d)


def per_device(
    tokens, positions, routes, attn_gain, w_query, w_key, w_value, w_out, mlp_gain, w_router,
    w_gate, w_up, w_down, cotangent,
):
    n = lax.axis_size("fsdp")
    index = lax.axis_index("fsdp")
    member = index % GROUP
    rows_dev, model_width = tokens.shape
    own_rows = w_query.shape[0]
    hidden_width = w_gate.shape[2]
    local = EXPERTS // GROUP
    across = [[r * GROUP + g for r in snake(n // GROUP)] for g in range(GROUP)]

    key_value = jnp.concatenate(
        [w_key.reshape(own_rows, 4, LANES), w_value.reshape(own_rows, 4, LANES)], axis=2
    ).reshape(own_rows, model_width)
    small = jnp.concatenate(
        [w_router, attn_gain[:, None], mlp_gain[:, None], jnp.zeros((own_rows, LANES - EXPERTS - 2), bf)],
        axis=1,
    )
    packed = jnp.concatenate([w_query, key_value, w_out, small], axis=1)
    far = doubling_gather(packed[None], index, n // 2, 2 * GROUP)

    shard = jnp.concatenate([w_gate, w_up, w_down], axis=2).reshape(
        GROUP, local, own_rows, 3 * hidden_width
    )
    pieces = []
    for bits in range(GROUP):
        piece = lax.dynamic_index_in_dim(shard, member ^ bits, 0, keepdims=False)
        pieces.append(swapped(piece, bits) if bits else piece)
    mine = jnp.stack(group_order(pieces, member))
    mine = mine.transpose(0, 2, 1, 3).reshape(GROUP * own_rows, local * 3 * hidden_width)
    mine, far = lax.optimization_barrier((mine, far))
    full = doubling_gather(far, index, GROUP, 1).reshape(n * own_rows, packed.shape[1])
    expert_w = lax.all_gather(mine, "fsdp", axis=0, tiled=True, axis_index_groups=across)

    cot_x = swapped(cotangent, 2)
    cots = (cotangent, cot_x, swapped(cotangent, 1), swapped(cot_x, 1))

    gain_one = full[:, 3088].astype(fl)[None, :]
    gain_two = full[:, 3089].astype(fl)[None, :]
    cosine, sine = rope_tables(positions)
    residual = tokens.astype(fl)
    inverse_one = lax.rsqrt(jnp.mean(residual * residual, axis=-1, keepdims=True) + NORM_EPS)
    normed_one = (residual * inverse_one * gain_one).astype(bf)
    own = project(key_value_kernel, normed_one, full, 4, cosine, sine)
    before = shifted(own, "fsdp", 1)
    queries = project(query_kernel, normed_one, full, 0, cosine, sine)
    start = (jnp.arange(rows_dev, dtype=jnp.int32) - positions)[:, None]
    context, context_low, log_total = attend(start, queries, before, own)

    context_low, *cots = lax.optimization_barrier((context_low, *cots))
    lanes = jnp.arange(LANES, dtype=jnp.int32)
    chosen = jnp.any(routes[:, :, None] == lanes[None, None, :], axis=1).astype(fl)
    middle, block, gates = middle_part(context_low, full, tokens, gain_two, chosen)

    block_x = swapped(block, 2)
    blocks = (block, block_x, swapped(block, 1), swapped(block_x, 1))
    first = (member * local).astype(jnp.int32).reshape(1)
    out_keep, gn_keep, out_send, gn_send, expert_grads = experts_part(first, n // GROUP, blocks, cots, expert_w)

    owned_experts = lax.psum_scatter(
        expert_grads, "fsdp", scatter_dimension=0, tiled=True, axis_index_groups=across
    )

    def returned(kept, sent):
        other = swapped(sent, 1)
        mine = kept[:rows_dev] + other[:rows_dev].astype(fl)
        away = (kept[rows_dev:] + other[rows_dev:].astype(fl)).astype(bf)
        return mine + swapped(away, 2).astype(fl)

    gn = returned(gn_keep, gn_send)
    grad_middle, grad_context, out_grad, gain_two_grad = middle_back(
        gn, gates, middle, cotangent, context_low, full, gain_two
    )
    activations = (middle + returned(out_keep, out_send)).astype(bf)
    part, sent = attend_back_prev(start, queries, before, grad_context, context, log_total)
    back = shifted(sent, "fsdp", -1)
    grad_query, kept = attend_back_own(
        start, queries, own, grad_context, context, log_total, part, cosine, sine
    )
    query_grad, part = query_back(grad_query, normed_one, full)
    token_grad, kv_grad, gain_one_grad = finish(
        part, kept, back, normed_one, tokens, grad_middle, full, gain_one, cosine, sine
    )
    gains = jnp.concatenate(
        [gain_one_grad, gain_two_grad, jnp.zeros((LANES - 2, model_width), fl)], axis=0
    ).T.astype(bf)
    owned, owned_experts = halving_sum(
        jnp.concatenate([query_grad, kv_grad, out_grad, gains], axis=1), index, owned_experts
    )
    owned_kv = owned[:, 1024:2048].reshape(own_rows, 4, 2, LANES)

    pieces = []
    for bits in range(GROUP):
        piece = lax.dynamic_slice_in_dim(owned_experts, (member ^ bits) * own_rows, own_rows, 0)
        pieces.append(swapped(piece, bits) if bits else piece)
    experts = jnp.stack(group_order(pieces, member)).reshape(GROUP, own_rows, local, 3, hidden_width)
    experts = experts.transpose(3, 0, 2, 1, 4).reshape(3, EXPERTS, own_rows, hidden_width).astype(fl)
    return (
        activations,
        token_grad,
        owned[:, 3200],
        owned[:, :1024],
        owned_kv[:, :, 0].reshape(own_rows, 512),
        owned_kv[:, :, 1].reshape(own_rows, 512),
        owned[:, 2048:3072],
        owned[:, 3201],
        owned[:, 3072 : 3072 + EXPERTS],
        experts[0],
        experts[1],
        experts[2],
    )


def solution(mesh):
    rows = P("fsdp", None)
    line = P("fsdp")
    stack = P(None, "fsdp", None)
    return jax.shard_map(
        per_device,
        mesh=mesh,
        in_specs=(rows, line, rows, line, rows, rows, rows, rows, line, rows, stack, stack, stack, rows),
        out_specs=(rows, rows, line, rows, rows, rows, rows, line, rows, stack, stack, stack),
        check_vma=False,
    )
```

```python
import jax
import jax.numpy as jnp
from jax import lax
from jax.experimental import pallas as pl
from jax.experimental.pallas import tpu as pltpu
from jax.sharding import PartitionSpec as P

HEADS = 16
KV_HEADS = 8
HEAD_DIM = 64
TOP = 8
EXPERTS = 16
GROUP = 4
LANES = 128
NORM_EPS = 1e-06
ROPE_THETA = 10000.0
MASKED = -1e30
MIB = 1024 * 1024

bf = jnp.bfloat16
fl = jnp.float32
SLOT = (0, 2, 1, 3)

NN = (((1,), (0,)), ((), ()))
NT = (((1,), (1,)), ((), ()))
TN = (((0,), (0,)), ((), ()))


def mm(a, b, dims=NN):
    return lax.dot_general(a, b, dims, preferred_element_type=fl)


def params(mib):
    return pltpu.CompilerParams(vmem_limit_bytes=mib * MIB)


def shifted(block, axis, distance):
    devices = range(lax.axis_size(axis))
    route = [(i - distance, i) for i in devices if i - distance in devices]
    return lax.ppermute(block, axis, route)


def swapped(block, bits):
    return lax.ppermute(block, "fsdp", [(i, i ^ bits) for i in range(lax.axis_size("fsdp"))])


def lane_index(shape):
    return lax.broadcasted_iota(jnp.int32, shape, len(shape) - 1)


def swap_halves(v):
    first = (lane_index(v.shape) & 32) == 0
    return jnp.where(first, pltpu.roll(v, LANES - 32, 1), pltpu.roll(v, 32, 1))


def rope_tables(positions):
    half_width = HEAD_DIM // 2
    frequency = ROPE_THETA ** (-(jnp.arange(half_width, dtype=fl) * 2.0) / HEAD_DIM)
    angle_rows = positions.astype(fl)[:, None] * frequency[None, :]
    cosine, sine = jnp.cos(angle_rows), jnp.sin(angle_rows)
    return (
        jnp.concatenate([cosine] * 4, axis=1),
        jnp.concatenate([-sine, sine, -sine, sine], axis=1),
    )


def query_kernel(x_ref, w_ref, cos_ref, sin_ref, out_ref):
    lin = mm(x_ref[...], w_ref[...])
    for part in range(2):
        piece = lin[:, part * LANES : (part + 1) * LANES]
        turned = piece * cos_ref[...] + swap_halves(piece) * sin_ref[...]
        out_ref[:, part * LANES : (part + 1) * LANES] = (turned.astype(bf) * HEAD_DIM**-0.5).astype(bf)


def key_value_kernel(x_ref, w_ref, cos_ref, sin_ref, out_ref):
    lin = mm(x_ref[...], w_ref[...])
    piece = lin[:, :LANES]
    out_ref[:, :LANES] = (piece * cos_ref[...] + swap_halves(piece) * sin_ref[...]).astype(bf)
    out_ref[:, LANES:] = lin[:, LANES:].astype(bf)


def project(kernel, normed, weights, first_block, cosine, sine):
    rows, width = normed.shape
    return pl.pallas_call(
        kernel,
        grid=(4,),
        in_specs=[
            pl.BlockSpec((rows, width), lambda j: (0, 0)),
            pl.BlockSpec((width, 256), lambda j: (0, first_block + j)),
            pl.BlockSpec((rows, LANES), lambda j: (0, 0)),
            pl.BlockSpec((rows, LANES), lambda j: (0, 0)),
        ],
        out_specs=pl.BlockSpec((rows, 256), lambda j: (0, j)),
        out_shape=jax.ShapeDtypeStruct((rows, 1024), bf),
        compiler_params=params(32),
    )(normed, weights, cosine, sine)


def fill_bias(start_ref, bias_ref):
    rows = bias_ref.shape[0]
    column = lax.broadcasted_iota(jnp.int32, bias_ref.shape, 1) - rows
    row = lax.broadcasted_iota(jnp.int32, bias_ref.shape, 0)
    seen = (column >= start_ref[...]) & (column <= row)
    bias_ref[...] = jnp.where(seen, 0.0, MASKED)


def attend_kernel(start_ref, q_ref, prev_ref, own_ref, ctx_ref, low_ref, lse_ref, bias_ref, kv_ref):
    rows = q_ref.shape[0]
    half = rows // 2

    @pl.when(pl.program_id(0) == 0)
    def _():
        fill_bias(start_ref, bias_ref)

    kv_ref[:rows, :] = prev_ref[...]
    kv_ref[rows:, :] = own_ref[...]
    for tile in range(2):
        queries = pl.ds(tile * half, half)
        keys = rows + (tile + 1) * half
        bias = bias_ref[queries, :keys]
        for head in range(4):
            lane = 64 * (head // 2)
            scores = mm(
                q_ref[queries, head * 64 : head * 64 + 64], kv_ref[:keys, lane : lane + 64], NT
            )
            scores = scores + bias
            row_max = jnp.max(scores, axis=1, keepdims=True)
            weights = jnp.exp(scores - row_max)
            total = jnp.sum(weights, axis=1, keepdims=True)
            probs = (weights * (1.0 / total)).astype(bf)
            context = mm(probs, kv_ref[:keys, LANES + lane : LANES + lane + 64])
            ctx_ref[queries, head * 64 : head * 64 + 64] = context
            low_ref[queries, head * 64 : head * 64 + 64] = context.astype(bf)
            lse_ref[0, queries, head : head + 1] = row_max + jnp.log(total)


def attend(start, queries, before, own):
    rows = queries.shape[0]
    wide = pl.BlockSpec((rows, 256), lambda j: (0, j))
    return pl.pallas_call(
        attend_kernel,
        grid=(4,),
        in_specs=[pl.BlockSpec((rows, 1), lambda j: (0, 0)), wide, wide, wide],
        out_specs=[wide, wide, pl.BlockSpec((1, rows, LANES), lambda j: (j, 0, 0))],
        out_shape=[
            jax.ShapeDtypeStruct((rows, 1024), fl),
            jax.ShapeDtypeStruct((rows, 1024), bf),
            jax.ShapeDtypeStruct((4, rows, LANES), fl),
        ],
        scratch_shapes=[pltpu.VMEM((rows, 2 * rows), fl), pltpu.VMEM((2 * rows, 256), bf)],
        compiler_params=params(40),
    )(start, queries, before, own)


def attend_back_step(q_ref, kv_ref, gctx_ref, ctx_ref, lse_ref, bias, queries, keys, head):
    lane = 64 * (head // 2)
    here = slice(head * 64, head * 64 + 64)
    query = q_ref[queries, here]
    grad = gctx_ref[queries, here]
    key = kv_ref[:keys, lane : lane + 64]
    value = kv_ref[:keys, LANES + lane : LANES + lane + 64]
    inner = jnp.sum(grad.astype(fl) * ctx_ref[queries, here], axis=1, keepdims=True)
    scores = mm(query, key, NT) + bias
    probs = jnp.exp(scores - lse_ref[0, queries, head : head + 1])
    grad_scores = (probs * (mm(grad, value, NT) - inner)).astype(bf)
    return (
        mm(grad_scores, key) * HEAD_DIM**-0.5,
        mm(grad_scores, query, TN),
        mm(probs.astype(bf), grad, TN),
    )


def attend_back_prev_kernel(start_ref, q_ref, prev_ref, gctx_ref, ctx_ref, lse_ref, gq_ref, sent_ref, bias_ref, gkv_ref):
    rows = q_ref.shape[0]

    @pl.when(pl.program_id(0) == 0)
    def _():
        column = lax.broadcasted_iota(jnp.int32, bias_ref.shape, 1) - rows
        bias_ref[...] = jnp.where(column >= start_ref[...], 0.0, MASKED)

    gkv_ref[...] = jnp.zeros_like(gkv_ref)
    for head in range(4):
        lane = 64 * (head // 2)
        gq, gk, gv = attend_back_step(
            q_ref, prev_ref, gctx_ref, ctx_ref, lse_ref, bias_ref[...], slice(None), rows, head
        )
        gq_ref[:, head * 64 : head * 64 + 64] = gq
        gkv_ref[:, lane : lane + 64] += gk
        gkv_ref[:, LANES + lane : LANES + lane + 64] += gv
    sent_ref[...] = gkv_ref[...].astype(bf)


def attend_back_own_kernel(
    start_ref, q_ref, own_ref, gctx_ref, ctx_ref, lse_ref, part_ref, cos_ref, sin_ref,
    gq_ref, kept_ref, bias_ref, gq_acc_ref,
):
    rows = q_ref.shape[0]
    half = rows // 2

    @pl.when(pl.program_id(0) == 0)
    def _():
        column = lax.broadcasted_iota(jnp.int32, bias_ref.shape, 1)
        row = lax.broadcasted_iota(jnp.int32, bias_ref.shape, 0)
        bias_ref[...] = jnp.where((column >= start_ref[...]) & (column <= row), 0.0, MASKED)

    kept_ref[...] = jnp.zeros_like(kept_ref)
    for tile in range(2):
        queries = pl.ds(tile * half, half)
        keys = (tile + 1) * half
        for head in range(4):
            lane = 64 * (head // 2)
            here = slice(head * 64, head * 64 + 64)
            gq, gk, gv = attend_back_step(
                q_ref, own_ref, gctx_ref, ctx_ref, lse_ref, bias_ref[queries, :keys], queries, keys, head
            )
            gq_acc_ref[queries, here] = gq + part_ref[queries, here]
            kept_ref[:keys, lane : lane + 64] += gk
            kept_ref[:keys, LANES + lane : LANES + lane + 64] += gv
    for part in range(2):
        here = slice(part * LANES, part * LANES + LANES)
        piece = gq_acc_ref[:, here]
        gq_ref[:, here] = (piece * cos_ref[...] - swap_halves(piece) * sin_ref[...]).astype(bf)


def attend_back_prev(start, queries, before, grad_context, context, log_total):
    rows = queries.shape[0]
    wide = pl.BlockSpec((rows, 256), lambda j: (0, j))
    return pl.pallas_call(
        attend_back_prev_kernel,
        grid=(4,),
        in_specs=[
            pl.BlockSpec((rows, 1), lambda j: (0, 0)), wide, wide, wide, wide,
            pl.BlockSpec((1, rows, LANES), lambda j: (j, 0, 0)),
        ],
        out_specs=[wide, wide],
        out_shape=[jax.ShapeDtypeStruct((rows, 1024), fl), jax.ShapeDtypeStruct((rows, 1024), bf)],
        scratch_shapes=[pltpu.VMEM((rows, rows), fl), pltpu.VMEM((rows, 256), fl)],
        compiler_params=params(48),
    )(start, queries, before, grad_context, context, log_total)


def attend_back_own(start, queries, own, grad_context, context, log_total, part, cosine, sine):
    rows = queries.shape[0]
    wide = pl.BlockSpec((rows, 256), lambda j: (0, j))
    table = pl.BlockSpec((rows, LANES), lambda j: (0, 0))
    return pl.pallas_call(
        attend_back_own_kernel,
        grid=(4,),
        in_specs=[
            pl.BlockSpec((rows, 1), lambda j: (0, 0)), wide, wide, wide, wide,
            pl.BlockSpec((1, rows, LANES), lambda j: (j, 0, 0)), wide, table, table,
        ],
        out_specs=[wide, wide],
        out_shape=[jax.ShapeDtypeStruct((rows, 1024), bf), jax.ShapeDtypeStruct((rows, 1024), fl)],
        scratch_shapes=[pltpu.VMEM((rows, rows), fl), pltpu.VMEM((rows, 256), fl)],
        compiler_params=params(48),
    )(start, queries, own, grad_context, context, log_total, part, cosine, sine)


def middle_kernel(ctx_ref, out_w_ref, router_ref, x_ref, gain_ref, chosen_ref, middle_ref, block_ref, gates_ref):
    width = x_ref.shape[1]
    middle = x_ref[...].astype(fl) + mm(ctx_ref[...], out_w_ref[...])
    inverse = lax.rsqrt(jnp.mean(middle * middle, axis=1, keepdims=True) + NORM_EPS)
    normed = (middle * inverse * gain_ref[...]).astype(bf)
    logits = mm(normed, router_ref[...])
    chosen = chosen_ref[...] > 0.0
    logits = jnp.where(chosen, logits, MASKED)
    weights = jnp.exp(logits - jnp.max(logits, axis=1, keepdims=True))
    weights = jnp.where(chosen, weights, 0.0)
    gates = weights / jnp.sum(weights, axis=1, keepdims=True)
    high = gates.astype(bf).astype(fl)
    middle_ref[...] = middle
    gates_ref[...] = gates
    block_ref[:, :width] = normed
    block_ref[:, width:] = (high + pltpu.roll(gates - high, EXPERTS, 1)).astype(bf)


def middle_part(ctx, full, tokens, gain, chosen):
    rows, width = tokens.shape
    return pl.pallas_call(
        middle_kernel,
        grid=(1,),
        in_specs=[
            pl.BlockSpec((rows, width), lambda j: (0, 0)),
            pl.BlockSpec((width, width), lambda j: (0, 2)),
            pl.BlockSpec((width, LANES), lambda j: (0, 24)),
            pl.BlockSpec((rows, width), lambda j: (0, 0)),
            pl.BlockSpec((1, width), lambda j: (0, 0)),
            pl.BlockSpec((rows, LANES), lambda j: (0, 0)),
        ],
        out_specs=[
            pl.BlockSpec((rows, width), lambda j: (0, 0)),
            pl.BlockSpec((rows, width + LANES), lambda j: (0, 0)),
            pl.BlockSpec((rows, LANES), lambda j: (0, 0)),
        ],
        out_shape=[
            jax.ShapeDtypeStruct((rows, width), fl),
            jax.ShapeDtypeStruct((rows, width + LANES), bf),
            jax.ShapeDtypeStruct((rows, LANES), fl),
        ],
        compiler_params=params(48),
    )(ctx, full, full, tokens, gain, chosen)


def experts_kernel(
    first_ref, x0, x1, x2, x3, c0, c1, c2, c3, w_ref, out_hbm, gn_hbm, out_send, gn_send, grad_ref,
    xs, cs, xt, ct, ws, out_acc, gn_acc, hid_s, gate_s, up_s, sems, w_sems,
):
    step = pl.program_id(0)
    steps = pl.num_programs(0)
    rows = c0.shape[0]
    width = c0.shape[1]
    cols = ws.shape[2]
    hidden_width = cols // 3
    expert = first_ref[0] + step
    order = snake(w_sems.shape[1])
    size = width // len(order)
    held = lax.rem(step, 2)

    def weight_copies(which, slot):
        columns = pl.ds(pl.multiple_of(which * cols, cols), cols)
        return [
            pltpu.make_async_copy(
                w_ref.at[pl.ds(place * size, size), columns],
                ws.at[slot, pl.ds(replica * size, size), :],
                w_sems.at[slot, place],
            )
            for place, replica in enumerate(order)
        ]

    @pl.when(step == 0)
    def _():
        copies = []
        for slot, (x, c) in enumerate(((x0, c0), (x1, c1), (x2, c2), (x3, c3))):
            here = pl.ds(slot * rows, rows)
            copies.append(pltpu.make_async_copy(x, xs.at[here], sems.at[2 * slot]))
            copies.append(pltpu.make_async_copy(c, cs.at[here], sems.at[2 * slot + 1]))
        for copy in copies + weight_copies(0, 0) + weight_copies(1, 1):
            copy.start()
        for copy in copies:
            copy.wait()
        out_acc[...] = jnp.zeros_like(out_acc)
        gn_acc[...] = jnp.zeros_like(gn_acc)
        for slot in range(GROUP):
            here = slice(slot * rows, (slot + 1) * rows)
            for source, target in ((xs, xt), (cs, ct)):
                turned = source[here, :width].T
                for place, replica in enumerate(order):
                    target[place * size : (place + 1) * size, here] = turned[
                        replica * size : (replica + 1) * size
                    ]

    for copy in weight_copies(step, held):
        copy.wait()

    def tile_step(tile, carry):
        here = pl.ds(pl.multiple_of(tile * rows, rows), rows)
        x_tile = xs[here, :width]
        gate_w = ws[held, :, :hidden_width]
        up_w = ws[held, :, hidden_width : 2 * hidden_width]
        down_w = ws[held, :, 2 * hidden_width :]
        gate = mm(x_tile, gate_w)
        up = mm(x_tile, up_w)
        raw = mm(cs[here, :], down_w)
        packed = xs[here, width:].astype(fl)
        lane = lane_index(packed.shape)
        mine = (lane == expert) | (lane == expert + EXPERTS)
        gates = jnp.sum(jnp.where(mine, packed, 0.0), axis=1, keepdims=True)
        sigmoid = 1.0 / (1.0 + jnp.exp(-gate))
        silu = gate * sigmoid
        hidden = (silu * up).astype(bf).astype(fl)
        grad_gates = jnp.sum(hidden * raw, axis=1, keepdims=True)
        grad_hidden = raw * gates
        hid = (hidden * gates).astype(bf)
        grad_gate = (grad_hidden * up * sigmoid * (1.0 + gate * (1.0 - sigmoid))).astype(bf)
        grad_up = (grad_hidden * silu).astype(bf)
        hid_s[here, :] = hid
        gate_s[here, :] = grad_gate
        up_s[here, :] = grad_up
        out_acc[here, :] += mm(hid, down_w, NT)
        gn_acc[here, :width] += mm(grad_gate, gate_w, NT) + mm(grad_up, up_w, NT)
        gn_acc[here, width:] += jnp.where(lane == expert, grad_gates, 0.0)
        return carry

    lax.fori_loop(0, GROUP, tile_step, 0)

    @pl.when(step + 2 < steps)
    def _():
        for copy in weight_copies(step + 2, held):
            copy.start()

    half = out_hbm.shape[0]
    results = [
        pltpu.make_async_copy(out_acc.at[:half], out_hbm, sems.at[0]),
        pltpu.make_async_copy(gn_acc.at[:half], gn_hbm, sems.at[1]),
        pltpu.make_async_copy(xs.at[half:, :width], out_send, sems.at[2]),
        pltpu.make_async_copy(xs.at[:half], gn_send, sems.at[3]),
    ]

    @pl.when(step == steps - 1)
    def _():
        gates_part = gn_acc[:, width:]
        high = gates_part.astype(bf).astype(fl)
        low = (gates_part - high).astype(bf).astype(fl)
        gn_acc[:, width:] = high + pltpu.roll(low, EXPERTS, 1)
        xs[:half, :] = gn_acc[half:, :].astype(bf)
        xs[half:, :width] = out_acc[half:, :].astype(bf)
        for copy in results:
            copy.start()

    grad_ref[:, :hidden_width] = mm(xt[...], gate_s[...]).astype(bf)
    grad_ref[:, hidden_width : 2 * hidden_width] = mm(xt[...], up_s[...]).astype(bf)
    grad_ref[:, 2 * hidden_width :] = mm(ct[...], hid_s[...]).astype(bf)

    @pl.when(step == steps - 1)
    def _():
        for copy in results:
            copy.wait()


def experts_part(first, replicas, blocks, cots, weights):
    rows, width = cots[0].shape
    local = EXPERTS // GROUP
    cols = weights.shape[1] // local
    hidden_width = cols // 3
    total = GROUP * rows
    anywhere = pl.BlockSpec(memory_space=pl.ANY)
    return pl.pallas_call(
        experts_kernel,
        grid_spec=pltpu.PrefetchScalarGridSpec(
            num_scalar_prefetch=1,
            grid=(local,),
            in_specs=[anywhere] * 9,
            out_specs=[anywhere] * 4 + [pl.BlockSpec((width, cols), lambda e, s: (0, e))],
            scratch_shapes=[
                pltpu.VMEM((total, width + LANES), bf),
                pltpu.VMEM((total, width), bf),
                pltpu.VMEM((width, total), bf),
                pltpu.VMEM((width, total), bf),
                pltpu.VMEM((2, width, cols), bf),
                pltpu.VMEM((total, width), fl),
                pltpu.VMEM((total, width + LANES), fl),
                pltpu.VMEM((total, hidden_width), bf),
                pltpu.VMEM((total, hidden_width), bf),
                pltpu.VMEM((total, hidden_width), bf),
                pltpu.SemaphoreType.DMA((8,)),
                pltpu.SemaphoreType.DMA((2, replicas)),
            ],
        ),
        out_shape=[
            jax.ShapeDtypeStruct((total // 2, width), fl),
            jax.ShapeDtypeStruct((total // 2, width + LANES), fl),
            jax.ShapeDtypeStruct((total // 2, width), bf),
            jax.ShapeDtypeStruct((total // 2, width + LANES), bf),
            jax.ShapeDtypeStruct((width, local * cols), bf),
        ],
        compiler_params=params(62),
    )(first, *blocks, *cots, weights)


def middle_back_kernel(
    gn_ref, gates_ref, middle_ref, cot_ref, ctx_ref, out_w_ref, router_ref, gain_ref,
    gm_ref, gctx_ref, gw_ref, gain_grad_ref,
):
    width = cot_ref.shape[1]
    packed = gn_ref[:, width:]
    gates = gates_ref[...]
    grad_gates = packed + pltpu.roll(packed, LANES - EXPERTS, 1)
    inner = jnp.sum(gates * grad_gates, axis=1, keepdims=True)
    grad_logits = (gates * (grad_gates - inner)).astype(bf)
    middle = middle_ref[...]
    inverse = lax.rsqrt(jnp.mean(middle * middle, axis=1, keepdims=True) + NORM_EPS)
    gain = gain_ref[...]
    unit = middle * inverse
    normed = (unit * gain).astype(bf)
    grad_normed = gn_ref[:, :width] + mm(grad_logits, router_ref[...], NT)
    gw_ref[:, width:] = mm(normed, grad_logits, TN).astype(bf)
    gain_grad_ref[...] = jnp.sum(grad_normed * unit, axis=0, keepdims=True)
    scaled = grad_normed * gain
    mean = jnp.mean(scaled * middle, axis=1, keepdims=True)
    grad_middle = cot_ref[...].astype(fl) + inverse * scaled - unit * (inverse * inverse * mean)
    gm_ref[...] = grad_middle
    branch = grad_middle.astype(bf)
    gctx_ref[...] = mm(branch, out_w_ref[...], NT).astype(bf)
    gw_ref[:, :width] = mm(ctx_ref[...], branch, TN).astype(bf)


def middle_back(gn, gates, middle, cot, ctx, full, gain):
    rows, width = cot.shape
    here = lambda *shape: pl.BlockSpec(shape, lambda j: (0, 0))
    return pl.pallas_call(
        middle_back_kernel,
        grid=(1,),
        in_specs=[
            here(rows, width + LANES), here(rows, LANES), here(rows, width), here(rows, width), here(rows, width),
            pl.BlockSpec((width, width), lambda j: (0, 2)),
            pl.BlockSpec((width, LANES), lambda j: (0, 24)),
            here(1, width),
        ],
        out_specs=[here(rows, width), here(rows, width), here(width, width + LANES), here(1, width)],
        out_shape=[
            jax.ShapeDtypeStruct((rows, width), fl),
            jax.ShapeDtypeStruct((rows, width), bf),
            jax.ShapeDtypeStruct((width, width + LANES), bf),
            jax.ShapeDtypeStruct((1, width), fl),
        ],
        compiler_params=params(56),
    )(gn, gates, middle, cot, ctx, full, full, gain)


def query_back_kernel(gq_ref, normed_ref, w_ref, gw_ref, part_ref):
    gw_ref[...] = mm(normed_ref[...], gq_ref[...], TN).astype(bf)
    part_ref[...] = mm(gq_ref[...], w_ref[...], NT)


def query_back(grad_query, normed, full):
    rows, width = normed.shape
    here = lambda *shape: pl.BlockSpec(shape, lambda j: (0, 0))
    return pl.pallas_call(
        query_back_kernel,
        grid=(1,),
        in_specs=[here(rows, width), here(rows, width), here(width, width)],
        out_specs=[here(width, width), here(rows, width)],
        out_shape=[jax.ShapeDtypeStruct((width, width), bf), jax.ShapeDtypeStruct((rows, width), fl)],
        compiler_params=params(48),
    )(grad_query, normed, full)


def finish_kernel(
    part_ref, kept_ref, back_ref, normed_ref, x_ref, gm_ref, w_ref, gain_ref, cos_ref, sin_ref,
    token_ref, gw_ref, gain_grad_ref, gkv_ref,
):
    for part in range(4):
        first = part * 256
        both = kept_ref[:, first : first + 256] + back_ref[:, first : first + 256].astype(fl)
        piece = both[:, :LANES]
        gkv_ref[:, first : first + LANES] = (
            piece * cos_ref[...] - swap_halves(piece) * sin_ref[...]
        ).astype(bf)
        gkv_ref[:, first + LANES : first + 256] = both[:, LANES:].astype(bf)
    gw_ref[...] = mm(normed_ref[...], gkv_ref[...], TN).astype(bf)
    grad_normed = part_ref[...] + mm(gkv_ref[...], w_ref[...], NT)
    x = x_ref[...].astype(fl)
    inverse = lax.rsqrt(jnp.mean(x * x, axis=1, keepdims=True) + NORM_EPS)
    unit = x * inverse
    gain_grad_ref[...] = jnp.sum(grad_normed * unit, axis=0, keepdims=True)
    scaled = grad_normed * gain_ref[...]
    mean = jnp.mean(scaled * x, axis=1, keepdims=True)
    token_ref[...] = gm_ref[...] + inverse * scaled - unit * (inverse * inverse * mean)


def finish(part, kept, back, normed, tokens, grad_middle, full, gain, cosine, sine):
    rows, width = tokens.shape
    here = lambda *shape: pl.BlockSpec(shape, lambda j: (0, 0))
    return pl.pallas_call(
        finish_kernel,
        grid=(1,),
        in_specs=[here(rows, width)] * 6
        + [
            pl.BlockSpec((width, width), lambda j: (0, 1)),
            here(1, width), here(rows, LANES), here(rows, LANES),
        ],
        out_specs=[here(rows, width), here(width, width), here(1, width)],
        out_shape=[
            jax.ShapeDtypeStruct((rows, width), fl),
            jax.ShapeDtypeStruct((width, width), bf),
            jax.ShapeDtypeStruct((1, width), fl),
        ],
        scratch_shapes=[pltpu.VMEM((rows, width), bf)],
        compiler_params=params(60),
    )(part, kept, back, normed, tokens, grad_middle, full, gain, cosine, sine)


def doubling_gather(part, index, bits, last):
    cur = part
    while bits >= last:
        other = swapped(cur, bits)
        pair = jnp.where(
            (index // bits) % 2 == 0, jnp.stack([cur, other], axis=1), jnp.stack([other, cur], axis=1)
        )
        cur = pair.reshape(2 * cur.shape[0], *cur.shape[1:])
        bits //= 2
    return cur


def halving_step(cur, index, left, bits):
    place = left.index(bits)
    mine = (index // bits) % 2
    pairs = cur.reshape(2**place, 2, 2 ** (len(left) - place - 1), *cur.shape[1:])
    keep = lax.dynamic_index_in_dim(pairs, mine, 1, keepdims=False)
    send = lax.dynamic_index_in_dim(pairs, 1 - mine, 1, keepdims=False)
    kept = keep.astype(fl) + swapped(send.astype(bf), bits).astype(fl)
    return kept.reshape(cur.shape[0] // 2, *cur.shape[1:]), [b for b in left if b != bits]


def halving_sum(part, index, meanwhile):
    n = lax.axis_size("fsdp")
    steps = [2**place for place in range(n.bit_length() - 1)]
    cur = part.reshape(n, part.shape[0] // n, part.shape[1])
    cur, left = halving_step(cur, index, steps[::-1], steps[0])
    middle = cur.shape[2] // 2
    orders = (steps[1:], [steps[2], steps[1], *steps[3:]])
    halves = [(cur[:, :, :middle], left), (cur[:, :, middle:], left)]
    for turn in range(len(steps) - 1):
        halves = [halving_step(half[0], index, half[1], order[turn]) for half, order in zip(halves, orders)]
        one, two, *extra = lax.optimization_barrier(
            (halves[0][0], halves[1][0], *((meanwhile,) if turn == 0 else ()))
        )
        meanwhile = extra[0] if extra else meanwhile
        halves = [(one, halves[0][1]), (two, halves[1][1])]
    return jnp.concatenate([half[0][0] for half in halves], axis=1), meanwhile


def snake(replicas):
    return [*range(0, replicas, 2), *range(replicas - 1, 0, -2)]


def group_order(pieces, member):
    one, two = member % 2 == 1, member // 2 == 1
    a, b, c, d = pieces
    a, b, c, d = jnp.where(one, b, a), jnp.where(one, a, b), jnp.where(one, d, c), jnp.where(one, c, d)
    return jnp.where(two, c, a), jnp.where(two, d, b), jnp.where(two, a, c), jnp.where(two, b, d)


def per_device(
    tokens, positions, routes, attn_gain, w_query, w_key, w_value, w_out, mlp_gain, w_router,
    w_gate, w_up, w_down, cotangent,
):
    n = lax.axis_size("fsdp")
    index = lax.axis_index("fsdp")
    member = index % GROUP
    rows_dev, model_width = tokens.shape
    own_rows = w_query.shape[0]
    hidden_width = w_gate.shape[2]
    local = EXPERTS // GROUP
    across = [[r * GROUP + g for r in snake(n // GROUP)] for g in range(GROUP)]

    key_value = jnp.concatenate(
        [w_key.reshape(own_rows, 4, LANES), w_value.reshape(own_rows, 4, LANES)], axis=2
    ).reshape(own_rows, model_width)
    small = jnp.concatenate(
        [w_router, attn_gain[:, None], mlp_gain[:, None], jnp.zeros((own_rows, LANES - EXPERTS - 2), bf)],
        axis=1,
    )
    packed = jnp.concatenate([w_query, key_value, w_out, small], axis=1)
    far = doubling_gather(packed[None], index, n // 2, GROUP)

    shard = jnp.concatenate([w_gate, w_up, w_down], axis=2).reshape(
        GROUP, local, own_rows, 3 * hidden_width
    )
    pieces = []
    for bits in range(GROUP):
        piece = lax.dynamic_index_in_dim(shard, member ^ bits, 0, keepdims=False)
        pieces.append(swapped(piece, bits) if bits else piece)
    mine = jnp.stack(group_order(pieces, member))
    mine = mine.transpose(0, 2, 1, 3).reshape(GROUP * own_rows, local * 3 * hidden_width)
    mine, far = lax.optimization_barrier((mine, far))
    full = doubling_gather(far, index, GROUP // 2, 1).reshape(n * own_rows, packed.shape[1])
    expert_w = lax.all_gather(mine, "fsdp", axis=0, tiled=True, axis_index_groups=across)

    cot_x = swapped(cotangent, 2)
    cots = (cotangent, cot_x, swapped(cotangent, 1), swapped(cot_x, 1))

    gain_one = full[:, 3088].astype(fl)[None, :]
    gain_two = full[:, 3089].astype(fl)[None, :]
    cosine, sine = rope_tables(positions)
    residual = tokens.astype(fl)
    inverse_one = lax.rsqrt(jnp.mean(residual * residual, axis=-1, keepdims=True) + NORM_EPS)
    normed_one = (residual * inverse_one * gain_one).astype(bf)
    own = project(key_value_kernel, normed_one, full, 4, cosine, sine)
    before = shifted(own, "fsdp", 1)
    queries = project(query_kernel, normed_one, full, 0, cosine, sine)
    start = (jnp.arange(rows_dev, dtype=jnp.int32) - positions)[:, None]
    context, context_low, log_total = attend(start, queries, before, own)

    context_low, *cots = lax.optimization_barrier((context_low, *cots))
    lanes = jnp.arange(LANES, dtype=jnp.int32)
    chosen = jnp.any(routes[:, :, None] == lanes[None, None, :], axis=1).astype(fl)
    middle, block, gates = middle_part(context_low, full, tokens, gain_two, chosen)

    block_x = swapped(block, 2)
    blocks = (block, block_x, swapped(block, 1), swapped(block_x, 1))
    first = (member * local).astype(jnp.int32).reshape(1)
    out_keep, gn_keep, out_send, gn_send, expert_grads = experts_part(first, n // GROUP, blocks, cots, expert_w)

    owned_experts = lax.psum_scatter(
        expert_grads, "fsdp", scatter_dimension=0, tiled=True, axis_index_groups=across
    )

    def returned(kept, sent):
        other = swapped(sent, 1)
        mine = kept[:rows_dev] + other[:rows_dev].astype(fl)
        away = (kept[rows_dev:] + other[rows_dev:].astype(fl)).astype(bf)
        return mine + swapped(away, 2).astype(fl)

    gn = returned(gn_keep, gn_send)
    grad_middle, grad_context, out_grad, gain_two_grad = middle_back(
        gn, gates, middle, cotangent, context_low, full, gain_two
    )
    activations = (middle + returned(out_keep, out_send)).astype(bf)
    part, sent = attend_back_prev(start, queries, before, grad_context, context, log_total)
    back = shifted(sent, "fsdp", -1)
    grad_query, kept = attend_back_own(
        start, queries, own, grad_context, context, log_total, part, cosine, sine
    )
    query_grad, part = query_back(grad_query, normed_one, full)
    token_grad, kv_grad, gain_one_grad = finish(
        part, kept, back, normed_one, tokens, grad_middle, full, gain_one, cosine, sine
    )
    gains = jnp.concatenate(
        [gain_one_grad, gain_two_grad, jnp.zeros((LANES - 2, model_width), fl)], axis=0
    ).T.astype(bf)
    owned, owned_experts = halving_sum(
        jnp.concatenate([query_grad, kv_grad, out_grad, gains], axis=1), index, owned_experts
    )
    owned_kv = owned[:, 1024:2048].reshape(own_rows, 4, 2, LANES)

    pieces = []
    for bits in range(GROUP):
        piece = lax.dynamic_slice_in_dim(owned_experts, (member ^ bits) * own_rows, own_rows, 0)
        pieces.append(swapped(piece, bits) if bits else piece)
    experts = jnp.stack(group_order(pieces, member)).reshape(GROUP, own_rows, local, 3, hidden_width)
    experts = experts.transpose(3, 0, 2, 1, 4).reshape(3, EXPERTS, own_rows, hidden_width).astype(fl)
    return (
        activations,
        token_grad,
        owned[:, 3200],
        owned[:, :1024],
        owned_kv[:, :, 0].reshape(own_rows, 512),
        owned_kv[:, :, 1].reshape(own_rows, 512),
        owned[:, 2048:3072],
        owned[:, 3201],
        owned[:, 3072 : 3072 + EXPERTS],
        experts[0],
        experts[1],
        experts[2],
    )


def solution(mesh):
    rows = P("fsdp", None)
    line = P("fsdp")
    stack = P(None, "fsdp", None)
    return jax.shard_map(
        per_device,
        mesh=mesh,
        in_specs=(rows, line, rows, line, rows, rows, rows, rows, line, rows, stack, stack, stack, rows),
        out_specs=(rows, rows, line, rows, rows, rows, rows, line, rows, stack, stack, stack),
        check_vma=False,
    )
```
